512 devices in a mesh: section: 4 (over x), ha: 16 (over y, core), wa: 8 (over z).
Axes of the slice: x: 4, y: 8, z: 8, core: 2. Of those that a mesh axis runs over, the one named last changes fastest.
Arguments:
- coarse_inputs: bfloat16 [4, 4, 192, 32, 128], P('section', None, None, 'ha', 'wa'), may hold values from -6 to 6
- init_level3: bfloat16 [192, 32, 128], P(None, 'ha', 'wa'), may hold values from -6 to 6
- init_level4: bfloat16 [96, 64, 256], P(None, 'ha', 'wa'), may hold values from -6 to 6
- weight_level3: bfloat16 [576, 9, 384], P('ha'), may hold values from -0.109375 to 0.109375
- weight_level4: bfloat16 [288, 9, 192], P('ha'), may hold values from -0.15625 to 0.15625
- lift_map: bfloat16 [96, 192], replicated, may hold values from -0.4375 to 0.4375
- readout: bfloat16 [16, 96], replicated, may hold values from -0.625 to 0.625
Outputs:
- precip: float32 [4, 4, 16, 64, 256], P('section', None, None, 'ha', 'wa')
The draws below stay inside these ranges and needn't reach their ends.
All inputs are finite; a program needn't handle non-finite values.
Results may differ from the reference program's by a relative error of at most 0.008.
Values may be sent and summed in bfloat16 or wider, within the bound.
A program may use at most 128 MiB of HBM per device.

```python
import jax
import jax.numpy as jnp
from jax import lax

C3 = 192
C4 = 96
SUB = 16
MEMBERS = 4
LEADS = 4
H4 = 64
W4 = 256
H3 = 32
W3 = 128


def block_scale(own_key, extent, shards, low, high):
    def one(dim, shards_of):
        steps = jax.random.uniform(jax.random.fold_in(jax.random.fold_in(own_key, 6), dim), (shards_of,), jnp.float32, low / len(shards), high / len(shards))
        return jnp.repeat(jnp.exp(steps), extent[dim] // shards_of).reshape((-1,) + (1,) * (len(extent) - dim - 1))

    loudness = one(*shards[0])
    for cut in shards[1:]:
        loudness = loudness * one(*cut)
    return loudness


def normal_values(rng, shape, spread, bound, cuts=(), kind=jnp.bfloat16):
    drawn = jax.random.normal(rng, shape, jnp.float32) * spread
    if len(cuts) > 0:
        drawn = block_scale(rng, shape, cuts, -0.22, 0.18) * drawn
    return jnp.clip(drawn, min=-bound, max=bound).astype(kind)


def setup_inputs(seed: int = 0) -> dict:
    arg_keys = jax.random.split(jax.random.key(seed), 8)
    coarse_inputs = normal_values(arg_keys[0], (LEADS, MEMBERS, C3, H3, W3), 1.0, 6.0, ((0, 4), (3, 16), (4, 8)))
    init_level3 = normal_values(arg_keys[1], (C3, H3, W3), 1.0, 6.0, ((1, 16), (2, 8)))
    init_level4 = normal_values(arg_keys[2], (C4, H4, W4), 1.0, 6.0, ((1, 16), (2, 8)))
    weight_level3 = normal_values(arg_keys[3], (3 * C3, 9, 2 * C3), (18 * C3) ** -0.5, 0.109375, ((0, 16),))
    weight_level4 = normal_values(arg_keys[4], (3 * C4, 9, 2 * C4), (18 * C4) ** -0.5, 0.15625, ((0, 16),))
    lift_map = normal_values(arg_keys[5], (C4, C3), C3 ** -0.5, 0.4375)
    readout = normal_values(arg_keys[6], (SUB, C4), C4 ** -0.5, 0.625)
    return dict(coarse_inputs=coarse_inputs, init_level3=init_level3, init_level4=init_level4, weight_level3=weight_level3, weight_level4=weight_level4, lift_map=lift_map, readout=readout)


def convolve(field, kernel):
    return lax.conv_general_dilated(field[None].astype(jnp.float32), kernel.astype(jnp.float32), (1, 1), "SAME", precision=lax.Precision.HIGHEST)[0]


def recur_field(inputs, previous, weight):
    channels = previous.shape[0]
    kernel = weight.reshape(3 * channels, 3, 3, 2 * channels).transpose(0, 3, 1, 2)
    gate_sums = convolve(jnp.concatenate([inputs, previous], 0), kernel[:2 * channels])
    reset_gate = jax.nn.sigmoid(gate_sums[:channels])
    update = jax.nn.sigmoid(gate_sums[channels:])
    prior_state = previous.astype(jnp.float32)
    gated_state = (reset_gate * prior_state).astype(jnp.bfloat16)
    candidate = jax.nn.relu(convolve(jnp.concatenate([inputs, gated_state], 0), kernel[2 * channels:]))
    return (update * prior_state + (1.0 - update) * candidate).astype(jnp.bfloat16)


def reference(coarse_inputs, init_level3, init_level4, weight_level3, weight_level4, lift_map, readout):
    outputs = []
    for member in range(MEMBERS):
        level3_state = init_level3
        level4_state = init_level4
        by_lead = []
        for lead_time in range(LEADS):
            level3_state = recur_field(coarse_inputs[lead_time, member], level3_state, weight_level3)
            coarse_lift = jnp.dot(lift_map, level3_state.reshape(C3, H3 * W3), preferred_element_type=jnp.float32)
            coarse_lift = coarse_lift.astype(jnp.bfloat16).reshape(C4, H3, W3)
            lifted = jnp.repeat(jnp.repeat(coarse_lift, 2, axis=1), 2, axis=2)
            level4_state = recur_field(lifted, level4_state, weight_level4)
            field = jnp.dot(readout, level4_state.reshape(C4, H4 * W4), preferred_element_type=jnp.float32)
            by_lead.append(field.reshape(SUB, H4, W4))
        outputs.append(jnp.stack(by_lead, 0))
    return jnp.stack(outputs, 1)
```

```python
import jax
import jax.numpy as jnp
from jax import lax
from jax.experimental import pallas as pl
from jax.experimental.pallas import tpu as pltpu
from jax.sharding import PartitionSpec as P

MESH = pl.DeviceIdType.MESH
BF16 = jnp.bfloat16
F32 = jnp.float32

NS, NH, NW = 4, 16, 8
LEADS = 4

Z3, Z4, X3, X4 = 1, 1, 5, 3
H3R, H4R = 288, 144
WIN3, WIN4 = 48, 32
ZR = Z3 * H3R + Z4 * H4R
XR = X3 * H3R + X4 * H4R
ZWIN = Z3 * WIN3 + Z4 * WIN4
XWIN = X3 * WIN3 + X4 * WIN4
XBASE = NW * ZR
WROWS = NW * ZR + NS * XR
SROWS = NW * ZWIN + NS * XWIN

NEIGHBOURS = [(dy, dx) for dy in (-1, 0, 1) for dx in (-1, 0, 1) if (dy, dx) != (0, 0)]


def off3(kb):
    if kb < NW * Z3:
        return (kb // Z3) * ZR + (kb % Z3) * H3R
    kb -= NW * Z3
    return XBASE + (kb // X3) * XR + (kb % X3) * H3R


def off4(kb):
    if kb < NW * Z4:
        return (kb // Z4) * ZR + Z3 * H3R + (kb % Z4) * H4R
    kb -= NW * Z4
    return XBASE + (kb // X4) * XR + X3 * H3R + (kb % X4) * H4R


def nt(a, b):
    return lax.dot_general(a, b, (((1,), (1,)), ((), ())), preferred_element_type=F32)


def kernel(
    ws_ref, x_ref, i3_ref, i4_ref, lm_ref, ro_ref, up_ref, o_ref,
    s1, wb, xb, s3, s4, j3, j4, pt, po,
    ss1, rs1, ssz, rsz, ssx, rsx, fsz, frz, fsx, frx,
    sxa, rxa, sxb, rxb, si3, ri3, si4, ri4, st3, rt3, st4, rt4, so, ro_sem,
):
    s = lax.axis_index("section")
    h = lax.axis_index("ha")
    w = lax.axis_index("wa")
    core = lax.rem(h, 2)
    half = h // 8
    slot = lax.rem(h, 8)
    sister = h + 1 - 2 * core

    xb[...] = jnp.zeros_like(xb)
    s3[...] = jnp.zeros_like(s3)
    s4[...] = jnp.zeros_like(s4)
    s3[0, 2:4, 16:32, :] = i3_ref[...]
    s4[0, 2:6, 16:48, :] = i4_ref[...]
    xb[pl.ds(s, 1), 2:4, 16:32, :] = x_ref[pl.ds(s, 1)]

    barrier = pltpu.get_barrier_semaphore()
    count = 0
    for d in range(1, NH):
        pl.semaphore_signal(barrier, inc=1, device_id={"ha": lax.rem(h + d, NH)}, device_id_type=MESH)
        count += 1
    for d in range(1, NW):
        pl.semaphore_signal(barrier, inc=1, device_id={"wa": lax.rem(w + d, NW)}, device_id_type=MESH)
        count += 1
    for d in range(1, NS):
        pl.semaphore_signal(barrier, inc=1, device_id={"section": lax.rem(s + d, NS)}, device_id_type=MESH)
        count += 1
    for dy in (1, NH - 1):
        for dx in (1, NW - 1):
            pl.semaphore_signal(
                barrier, inc=1,
                device_id={"ha": lax.rem(h + dy, NH), "wa": lax.rem(w + dx, NW)},
                device_id_type=MESH,
            )
            count += 1
    pl.semaphore_wait(barrier, count)

    def remote(src, dst, send, recv, **where):
        return pltpu.make_async_remote_copy(
            src_ref=src, dst_ref=dst, send_sem=send, recv_sem=recv, device_id=where, device_id_type=MESH
        )

    def exists(dy, dx):
        hh, ww = h + dy, w + dx
        ok = None
        for cond in ([hh >= 0] if dy < 0 else [hh < NH] if dy > 0 else []) + (
            [ww >= 0] if dx < 0 else [ww < NW] if dx > 0 else []
        ):
            ok = cond if ok is None else jnp.logical_and(ok, cond)
        return ok

    def each_neighbour(make, action):
        for n, (dy, dx) in enumerate(NEIGHBOURS):
            @pl.when(exists(dy, dx))
            def _(n=n, dy=dy, dx=dx):
                getattr(make(n, dy, dx), action)()

    def copy_x(n, dy, dx):
        return remote(
            xb.at[:, 2:4, 16:32, :],
            xb.at[:, 2 - 2 * dy : 4 - 2 * dy, 16 - 16 * dx : 32 - 16 * dx, :],
            sxb.at[n], rxb.at[n], ha=h + dy, wa=w + dx,
        )

    def copy_3(src, t, ss, rs):
        def make(n, dy, dx):
            return remote(
                src, s3.at[t, 2 - 2 * dy : 4 - 2 * dy, 16 - 16 * dx : 32 - 16 * dx, :],
                ss.at[n], rs.at[n], ha=h + dy, wa=w + dx,
            )
        return make

    def copy_4(src, row0, col0, t, ss, rs):
        def make(n, dy, dx):
            r0, r1 = {-1: (0, 2), 0: (0, 4), 1: (2, 4)}[dy]
            c0, c1 = {-1: (0, 16), 0: (0, 32), 1: (16, 32)}[dx]
            q0, q1 = {-1: (6, 8), 0: (2, 6), 1: (0, 2)}[dy]
            d0, d1 = {-1: (48, 64), 0: (16, 48), 1: (0, 16)}[dx]
            return remote(
                src.at[row0 + r0 : row0 + r1, col0 + c0 : col0 + c1, :],
                s4.at[t, q0:q1, d0:d1, :], ss.at[n], rs.at[n], ha=h + dy, wa=w + dx,
            )
        return make

    def arrive(make):
        def incoming(n, dy, dx):
            return make(NEIGHBOURS.index((-dy, -dx)), -dy, -dx)
        for n, (dy, dx) in enumerate(NEIGHBOURS):
            @pl.when(exists(dy, dx))
            def _(n=n, dy=dy, dx=dx):
                incoming(n, dy, dx).wait_recv()

    def to_column(y, part):
        lo, n, dst = ((w * ZWIN, ZWIN, 0), (NW * ZWIN + s * XWIN, XWIN, ZWIN))[part]
        return remote(
            ws_ref.at[pl.ds(pl.multiple_of(lo, 16), n), :],
            s1.at[slot, dst : dst + n, :],
            ss1.at[part, y], rs1.at[part, slot], ha=2 * y + half,
        )

    def from_column(i, part):
        n, dst = ((ZWIN, 0), (XWIN, ZWIN))[part]
        return remote(
            ws_ref.at[pl.ds(0, n), :], s1.at[i, dst : dst + n, :],
            ss1.at[part, i], rs1.at[part, i], ha=sister,
        )

    def column(action, part):
        for y in range(8):
            @pl.when(2 * y + half != h)
            def _(y=y):
                getattr(to_column(y, part), action)()

    @pl.when(half == core)
    def _():
        s1[pl.ds(slot, 1), 0:ZWIN, :] = ws_ref[pl.ds(pl.multiple_of(w * ZWIN, 16), ZWIN), :][None]
        s1[pl.ds(slot, 1), ZWIN : ZWIN + XWIN, :] = ws_ref[
            pl.ds(pl.multiple_of(NW * ZWIN + s * XWIN, 16), XWIN), :
        ][None]

    def to_member(d):
        m = lax.rem(s + d, NS)
        return remote(x_ref.at[m], xb.at[s, 2:4, 16:32, :], sxa.at[d], rxa.at[d], section=m)

    def from_lead(d):
        src = lax.rem(s + NS - d, NS)
        return remote(x_ref.at[0], xb.at[src, 2:4, 16:32, :], sxa.at[d], rxa.at[d], section=src)

    for d in range(1, NS):
        to_member(d).start()
    column("start", 1)
    column("start", 0)
    init3 = copy_3(i3_ref, 0, si3, ri3)
    init4 = copy_4(i4_ref, 0, 0, 0, si4, ri4)
    each_neighbour(init3, "start")
    each_neighbour(init4, "start")
    for d in range(1, NS):
        from_lead(d).wait_recv()
    each_neighbour(copy_x, "start")

    def wait_column(part):
        for i in range(8):
            @pl.when(8 * core + i != h)
            def _(i=i):
                from_column(i, part).wait_recv()

    def merged3(at):
        tiles = []
        for group in range(2):
            part = lambda i, j: s1[4 * group + i, at + 16 * j : at + 16 * j + 16, :]
            tiles += [
                part(0, 0), part(0, 1), part(0, 2) + part(1, 0), part(1, 1), part(1, 2) + part(2, 0),
                part(2, 1), part(2, 2) + part(3, 0), part(3, 1), part(3, 2),
            ]
        return jnp.concatenate(tiles, 0)

    def merged4(at):
        part = lambda i, j: s1[i, at + 16 * j : at + 16 * j + 16, :]
        tiles = [part(0, 0)] + [part(i, 1) + part(i + 1, 0) for i in range(7)] + [part(7, 1)]
        return jnp.concatenate(tiles, 0)

    def place(base, rows, value):
        wb[pl.ds(core, 1), pl.ds(pl.multiple_of(base, 16), rows), :] = value[None]

    def z_piece(c, z):
        return wb.at[c, pl.ds(pl.multiple_of(z * ZR, 16), ZR), :]

    def x_piece(c, x):
        return wb.at[c, pl.ds(pl.multiple_of(XBASE + x * XR, 16), XR), :]

    def z_copy(d):
        return remote(z_piece(core, w), z_piece(core, w), ssz.at[d], rsz.at[d], wa=lax.rem(w + d, NW))

    def z_from(d):
        z = lax.rem(w + NW - d, NW)
        return remote(z_piece(core, z), z_piece(core, z), ssz.at[d], rsz.at[d], wa=z)

    def x_copy(d):
        return remote(x_piece(core, s), x_piece(core, s), ssx.at[d], rsx.at[d], section=lax.rem(s + d, NS))

    def x_from(d):
        x = lax.rem(s + NS - d, NS)
        return remote(x_piece(core, x), x_piece(core, x), ssx.at[d], rsx.at[d], section=x)

    def z_share(d, c):
        z = lax.rem(w + NW - d, NW)
        return remote(z_piece(c, z), z_piece(c, z), fsz.at[d], frz.at[d], ha=sister)

    def x_share(d, c):
        x = lax.rem(s + NS - d, NS)
        return remote(x_piece(c, x), x_piece(c, x), fsx.at[d], frx.at[d], ha=sister)

    x_order = (1, 3, 2)
    z_order = (1, 7, 2, 6, 3, 5, 4)
    wait_column(1)
    for j in range(X3):
        place(XBASE + s * XR + j * H3R, H3R, merged3(ZWIN + j * WIN3))
    for j in range(X4):
        place(XBASE + s * XR + X3 * H3R + j * H4R, H4R, merged4(ZWIN + X3 * WIN3 + j * WIN4))
    for d in x_order:
        x_copy(d).start()
    x_share(0, core).start()
    wait_column(0)
    for j in range(Z3):
        place(w * ZR + j * H3R, H3R, merged3(j * WIN3))
    for j in range(Z4):
        place(w * ZR + Z3 * H3R + j * H4R, H4R, merged4(Z3 * WIN3 + j * WIN4))
    for d in z_order:
        z_copy(d).start()
    z_share(0, core).start()
    for d in x_order[:2]:
        x_from(d).wait_recv()
        x_share(d, core).start()
    for d in z_order:
        z_from(d).wait_recv()
        z_share(d, core).start()
    for d in x_order[2:]:
        x_from(d).wait_recv()
        x_share(d, core).start()
    arrive(init3)
    arrive(init4)
    arrive(copy_x)
    for d in range(NW):
        z_share(d, 1 - core).wait_recv()
    for d in range(NS):
        x_share(d, 1 - core).wait_recv()

    def rows3(kb, c, lo, hi):
        return wb[c, off3(kb) + lo : off3(kb) + hi, :]

    def rows4(kb, c, lo, hi):
        return wb[c, off4(kb) + lo : off4(kb) + hi, :]

    def gates3(a):
        blocks = []
        for kb in range(9 * a, 9 * a + 9):
            blocks.append(jnp.concatenate([
                rows3(kb, 0, 0, 192), rows3(kb, 0, 128, 192),
                rows3(kb, 0, 192, 288), rows3(kb, 1, 0, 32), rows3(kb, 1, 32, 96), rows3(kb, 1, 32, 96),
            ], 0))
        return jnp.concatenate(blocks, 1)

    def cand3(a):
        zero = jnp.zeros((64, 128), BF16)
        blocks = [
            jnp.concatenate([rows3(kb, 1, 96, 224), zero, rows3(kb, 1, 224, 288)], 0)
            for kb in range(9 * a, 9 * a + 9)
        ]
        return jnp.concatenate(blocks, 1)

    def gates4(a):
        blocks = []
        for kb in range(6 * a, 6 * a + 6):
            blocks.append(jnp.concatenate([
                rows4(kb, 0, 0, 96), rows4(kb, 0, 0, 32),
                rows4(kb, 0, 96, 144), rows4(kb, 1, 0, 48), rows4(kb, 0, 0, 32),
            ], 0))
        return jnp.concatenate(blocks, 1)

    def cand4(a):
        zero = jnp.zeros((32, 128), BF16)
        blocks = [jnp.concatenate([rows4(kb, 1, 48, 144), zero], 0) for kb in range(6 * a, 6 * a + 6)]
        return jnp.concatenate(blocks, 1)

    def taps(ref, r0, r1, c0, c1):
        return jnp.concatenate([ref[r0:r1, c0 + b - 1 : c1 + b - 1, :].astype(BF16) for b in range(3)], 2)

    def level3(t):
        x = xb[t].astype(F32)
        p = s3[t].astype(F32)
        j3[:, :, 0:128] = x[:, :, :128]
        j3[:, :, 128:256] = p[:, :, :128]
        j3[:, :, 256:384] = x[:, :, 128:] + p[:, :, 128:]
        u = taps(j3, 0, 6, 8, 40)
        sums = sum(nt(u[a : a + 4].reshape(128, 1152), gates3(a)) for a in range(3))
        reset = jax.nn.sigmoid(sums[:, :256]).reshape(4, 32, 256)
        update = jax.nn.sigmoid(sums[:, 256:]).reshape(4, 32, 256)[1:3, 8:24, :]
        gated = reset * p[1:5, 8:40, :]
        j3[1:5, 8:40, 128:256] = gated[:, :, :128]
        j3[1:5, 8:40, 256:384] = x[1:5, 8:40, 128:] + gated[:, :, 128:]
        v = taps(j3, 1, 5, 16, 32)
        fresh = sum(nt(v[a : a + 2].reshape(32, 1152), cand3(a)) for a in range(3))
        fresh = jnp.maximum(fresh, 0.0).reshape(2, 16, 256)
        prior = p[2:4, 16:32, :]
        s3[t + 1, 2:4, 16:32, :] = (update * prior + (1.0 - update) * fresh).astype(BF16)

    def level4(t):
        coarse = s3[t + 1, 1:5].astype(F32)[:, 8:40, :].astype(BF16).reshape(128, 256)
        lift = nt(coarse, lm_ref[...]).astype(BF16)
        lifted = jnp.dot(up_ref[...], lift, preferred_element_type=F32).reshape(4, 64, 128)
        p = s4[t].astype(F32)
        for i in range(8):
            j4[i, :, 0:128] = lifted[i // 2]
        j4[:, :, 128:256] = p
        u = taps(j4, 0, 8, 8, 56)
        sums = sum(nt(u[a : a + 6].reshape(288, 768), gates4(a)) for a in range(3))
        reset = jax.nn.sigmoid(sums[:, :128]).reshape(6, 48, 128)
        update = jax.nn.sigmoid(sums[:, 128:]).reshape(6, 48, 128)[1:5, 8:40, :]
        j4[1:7, 8:56, 128:256] = reset * p[1:7, 8:56, :]
        v = taps(j4, 1, 7, 16, 48)
        fresh = sum(nt(v[a : a + 4].reshape(128, 768), cand4(a)) for a in range(3))
        fresh = jnp.maximum(fresh, 0.0).reshape(4, 32, 128)
        prior = p[2:6, 16:48, :]
        state = (update * prior + (1.0 - update) * fresh).astype(BF16)
        if t < LEADS - 1:
            s4[t + 1, 2:6, 16:48, :] = state
        pt[t] = nt(ro_ref[...], state.reshape(128, 128))

        @pl.when(s == t)
        def _():
            po[t] = pt[t]

        @pl.when(s != t)
        def _():
            to_lead(t).start()

    def to_lead(t):
        return remote(pt.at[t], po.at[s], so.at[t], ro_sem.at[s], section=t)

    def from_member(m):
        return remote(pt.at[0], po.at[m], so.at[0], ro_sem.at[m], section=m)

    def exchange3(t):
        return copy_3(s3.at[t + 1, 2:4, 16:32, :], t + 1, st3.at[t], rt3.at[t])

    def exchange4(t):
        return copy_4(s4.at[t + 1], 2, 16, t + 1, st4.at[t], rt4.at[t])

    level3(0)
    each_neighbour(exchange3(0), "start")
    for t in range(LEADS):
        arrive(exchange3(t))
        if t + 1 < LEADS:
            level3(t + 1)
            each_neighbour(exchange3(t + 1), "start")
        if t > 0:
            arrive(exchange4(t - 1))
        level4(t)
        if t + 1 < LEADS:
            each_neighbour(exchange4(t), "start")

    for m in range(NS):
        @pl.when(s != m)
        def _(m=m):
            from_member(m).wait_recv()
    o_ref[...] = po[...]

    for d in range(1, NS):
        to_member(d).wait_send()
        x_copy(d).wait_send()
    for d in range(1, NW):
        z_copy(d).wait_send()
    for d in range(NW):
        z_share(d, core).wait_send()
    for d in range(NS):
        x_share(d, core).wait_send()
    column("wait_send", 0)
    column("wait_send", 1)
    each_neighbour(init3, "wait_send")
    each_neighbour(init4, "wait_send")
    each_neighbour(copy_x, "wait_send")
    for t in range(LEADS):
        each_neighbour(exchange3(t), "wait_send")
        if t + 1 < LEADS:
            each_neighbour(exchange4(t), "wait_send")
    for t in range(LEADS):
        @pl.when(s != t)
        def _(t=t):
            to_lead(t).wait_send()


def shard_windows(weight_level3, weight_level4):
    h = lax.axis_index("ha")
    w3 = weight_level3
    joint = jnp.stack(
        [w3[:, :, :128], w3[:, :, 192:320], jnp.concatenate([w3[:, :, 128:192], w3[:, :, 320:]], 2)], 2
    )
    blocks3 = joint.transpose(1, 2, 0, 3).reshape(27, 36, 128)
    wide3 = lax.dynamic_update_slice(
        jnp.zeros((NW * Z3 + NS * X3, WIN3, 128), BF16), blocks3, (0, 4 * lax.rem(h, 4), 0)
    )
    w4 = jnp.pad(weight_level4.reshape(18, 9, 2, 96), ((0, 0), (0, 0), (0, 0), (0, 32)))
    blocks4 = w4.transpose(1, 2, 0, 3).reshape(18, 18, 128)
    wide4 = lax.dynamic_update_slice(
        jnp.zeros((NW * Z4 + NS * X4, WIN4, 128), BF16), blocks4, (0, 2 * lax.rem(h, 8), 0)
    )
    def pieces(start3, n3, start4, n4, count):
        a = wide3[start3 : start3 + n3 * count].reshape(count, n3 * WIN3, 128)
        b = wide4[start4 : start4 + n4 * count].reshape(count, n4 * WIN4, 128)
        return jnp.concatenate([a, b], 1).reshape(-1, 128)
    return jnp.concatenate(
        [pieces(0, Z3, 0, Z4, NW), pieces(NW * Z3, X3, NW * Z4, X4, NS)], 0
    )


def state_lanes(v):
    gap = jnp.zeros(v.shape[:-1] + (64,), v.dtype)
    return jnp.concatenate([v[..., :128], gap, v[..., 128:]], -1)


def local(coarse_inputs, init_level3, init_level4, weight_level3, weight_level4, lift_map, readout):
    ws = shard_windows(weight_level3, weight_level4)
    x = jnp.pad(coarse_inputs[0].transpose(0, 2, 3, 1), ((0, 0), (0, 0), (0, 0), (0, 64)))
    i3 = state_lanes(init_level3.transpose(1, 2, 0))
    i4 = jnp.pad(init_level4.transpose(1, 2, 0), ((0, 0), (0, 0), (0, 32)))
    lm = jnp.pad(state_lanes(lift_map), ((0, 32), (0, 0)))
    ro = jnp.pad(readout, ((0, 0), (0, 32)))
    fine = jnp.arange(256)
    up = ((fine // 64) * 32 + (fine % 64) // 2)[:, None] == jnp.arange(128)[None, :]
    vmem = pl.BlockSpec(memory_space=pltpu.VMEM)
    dma = pltpu.SemaphoreType.DMA
    fields = pl.pallas_call(
        kernel,
        out_shape=jax.ShapeDtypeStruct((4, 16, 128), F32),
        in_specs=[vmem] * 7,
        out_specs=vmem,
        scratch_shapes=[
            pltpu.VMEM((8, ZWIN + XWIN, 128), BF16),
            pltpu.VMEM((2, WROWS, 128), BF16),
            pltpu.VMEM((4, 6, 48, 256), BF16),
            pltpu.VMEM((5, 6, 48, 256), BF16),
            pltpu.VMEM((4, 8, 64, 128), BF16),
            pltpu.VMEM((6, 48, 384), F32),
            pltpu.VMEM((8, 64, 256), F32),
            pltpu.VMEM((4, 16, 128), F32),
            pltpu.VMEM((4, 16, 128), F32),
            dma((2, 8)), dma((2, 8)),
            dma((NW,)), dma((NW,)), dma((NS,)), dma((NS,)),
            dma((NW,)), dma((NW,)), dma((NS,)), dma((NS,)),
            dma((NS,)), dma((NS,)), dma((8,)), dma((8,)),
            dma((8,)), dma((8,)), dma((8,)), dma((8,)),
            dma((4, 8)), dma((4, 8)), dma((4, 8)), dma((4, 8)),
            dma((4,)), dma((4,)),
        ],
        compiler_params=pltpu.CompilerParams(
            collective_id=0, has_side_effects=True, vmem_limit_bytes=40 << 20
        ),
        name="nowcast",
    )(ws, x, i3, i4, lm, ro, up.astype(BF16))
    return fields.reshape(1, 4, 16, 4, 32)


def solution(mesh):
    return jax.shard_map(
        local,
        mesh=mesh,
        in_specs=(
            P("section", None, None, "ha", "wa"),
            P(None, "ha", "wa"),
            P(None, "ha", "wa"),
            P("ha", None, None),
            P("ha", None, None),
            P(),
            P(),
        ),
        out_specs=P("section", None, None, "ha", "wa"),
        check_vma=False,
    )
```

```python
import jax
import jax.numpy as jnp
from jax import lax
from jax.experimental import pallas as pl
from jax.experimental.pallas import tpu as pltpu
from jax.sharding import PartitionSpec as P

MESH = pl.DeviceIdType.MESH
BF16 = jnp.bfloat16
F32 = jnp.float32

NS, NH, NW = 4, 16, 8
LEADS = 4

X3, X4 = 5, 3
K3, K4 = 8 + NS * X3, 8 + NS * X4
H3R, H4R = 288, 144
WIN3, WIN4 = 80, 48

CHUNKS = [(3, 1, 1), (3, 2, 1), (3, 0, 1), (3, 3, 2), (3, 5, 1), (4, 1, 3), (4, 0, 1)]
CH3, CH4 = range(5), range(5, 7)

NEIGHBOURS = [(dy, dx) for dy in (-1, 0, 1) for dx in (-1, 0, 1) if (dy, dx) != (0, 0)]
X_ORDER = (1, 3, 2)
Z_ORDER = (1, 7, 2, 6, 3, 5, 4)


def nt(a, b):
    return lax.dot_general(a, b, (((1,), (1,)), ((), ())), preferred_element_type=F32)


def kernel(
    x_ref, i3_ref, i4_ref, w3_ref, w4_ref, lm_ref, ro_ref, o_ref,
    i3v, i4v, lmv, rov, own3, own4, sis3, sis4, cw3, cw4, s13, s14, wb3, wb4,
    xb, s3, s4, j3, j4, tmp, lm, ro, up, pt, po,
    load_sem, raw_s, raw_r, col_s, col_r, x_s, x_r, z_s, z_r, f_s, f_r,
    xa_s, xa_r, xn_s, xn_r, n3_s, n3_r, n4_s, n4_r, out_s, out_r,
):
    s = lax.axis_index("section")
    h = lax.axis_index("ha")
    w = lax.axis_index("wa")
    core = lax.rem(h, 2)
    y = h // 2
    sister = h + 1 - 2 * core
    half = y // 4

    def remote(src, dst, send, recv, **where):
        return pltpu.make_async_remote_copy(
            src_ref=src, dst_ref=dst, send_sem=send, recv_sem=recv, device_id=where, device_id_type=MESH
        )

    def wait_bytes(view, sem):
        pltpu.make_async_copy(view, view, sem).wait()

    xb[0] = jnp.zeros(xb.shape[1:], BF16)
    s3[0:5] = jnp.zeros((5,) + s3.shape[1:], BF16)
    s4[0:4] = jnp.zeros((4,) + s4.shape[1:], BF16)
    loads = [
        pltpu.make_async_copy(src, dst, load_sem.at[k])
        for k, (src, dst) in enumerate([
            (w3_ref, own3), (w4_ref, own4), (x_ref.at[s], xb.at[0, s, 2:4, 16:32, :]),
            (i3_ref, i3v), (i4_ref, i4v), (lm_ref, lmv), (ro_ref, rov),
        ])
    ]
    for load in loads:
        load.start()

    barrier = pltpu.get_barrier_semaphore()
    alone = (half == core) & (lax.rem(y, 2) == core)
    count = 0
    greet = [{"ha": sister}, {"ha": lax.rem(h + 2 * core + NH - 1, NH)}]
    greet += [{"wa": lax.rem(w + d, NW)} for d in range(1, NW)]
    greet += [{"section": lax.rem(s + d, NS)} for d in range(1, NS)]
    greet += [
        {"ha": lax.rem(h + dy, NH), "wa": lax.rem(w + dx, NW)} for dy in (1, NH - 1) for dx in (1, NW - 1)
    ]
    for where in greet:
        pl.semaphore_signal(barrier, inc=1, device_id=where, device_id_type=MESH)
    for i in range(4):
        source = 2 * (4 * core + i) + lax.rem(y, 2)
        @pl.when(source != h)
        def _(source=source):
            pl.semaphore_signal(barrier, inc=1, device_id={"ha": source}, device_id_type=MESH)
    pl.semaphore_wait(barrier, len(greet) + 4 - alone.astype(jnp.int32))

    raw3 = remote(w3_ref, sis3, raw_s.at[0], raw_r.at[0], ha=sister)
    raw4 = remote(w4_ref, sis4, raw_s.at[1], raw_r.at[1], ha=sister)
    raw3.start()
    raw4.start()
    for d in range(1, NS):
        m = lax.rem(s + d, NS)
        remote(x_ref.at[m], xb.at[0, s, 2:4, 16:32, :], xa_s, xa_r, section=m).start()

    def placed(rows, count, offset):
        r = lax.broadcasted_iota(jnp.int32, (rows, count), 0)
        c = lax.broadcasted_iota(jnp.int32, (rows, count), 1)
        return jnp.where(r == c + offset, 1.0, 0.0).astype(BF16)

    lane = lax.broadcasted_iota(jnp.int32, (1, 128), 1)
    low = lane < 64
    base3 = 8 * lax.rem(y, 2)
    base4 = 4 * lax.rem(y, 4)
    mine3, other3 = placed(WIN3, 36, base3 + 36 * core), placed(WIN3, 36, base3 + 36 * (1 - core))
    mine4, other4 = placed(WIN4, 18, base4 + 18 * core), placed(WIN4, 18, base4 + 18 * (1 - core))
    loads[0].wait()
    loads[1].wait()
    raw3.wait_recv()
    for tap in range(9):
        rows = jnp.dot(mine3, own3[tap], preferred_element_type=F32) + jnp.dot(
            other3, sis3[tap], preferred_element_type=F32
        )
        v1, v2 = rows[:, 128:256], rows[:, 256:384]
        cw3[3 * tap] = rows[:, :128].astype(BF16)
        cw3[3 * tap + 1] = jnp.where(low, v2, v1).astype(BF16)
        cw3[3 * tap + 2] = jnp.where(low, v1, v2).astype(BF16)
    cw3[27] = jnp.zeros((WIN3, 128), BF16)

    def column_parts(chunk):
        level, slot, n = CHUNKS[chunk]
        cw, s1, per = (cw3, s13, X3) if level == 3 else (cw4, s14, X4)
        first = w if slot == 0 else 8 + s * per + slot - 1
        return cw.at[pl.ds(first, n)], s1.at[lax.rem(y, 4), slot : slot + n], s1.at[:, slot : slot + n]

    def column_start(chunk):
        src, dst, _ = column_parts(chunk)
        for i in range(4):
            target = 2 * (2 * i + core) + half
            @pl.when(target != h)
            def _(target=target):
                remote(src, dst, col_s.at[chunk], col_r.at[chunk], ha=target).start()
        @pl.when(alone)
        def _():
            pltpu.make_async_copy(src, dst, col_r.at[chunk]).start()

    def column_wait(chunk):
        wait_bytes(column_parts(chunk)[2], col_r.at[chunk])

    for chunk in CH3:
        column_start(chunk)
    raw4.wait_recv()
    for tap in range(9):
        rows = jnp.dot(mine4, own4[tap], preferred_element_type=F32) + jnp.dot(
            other4, sis4[tap], preferred_element_type=F32
        )
        cw4[2 * tap] = rows[:, :128].astype(BF16)
        tmp[0:WIN4, 0:64] = rows[:, 128:192]
        tmp[0:WIN4, 64:128] = jnp.zeros((WIN4, 64), F32)
        cw4[2 * tap + 1] = tmp[0:WIN4, 0:128].astype(BF16)
    cw4[18:20] = jnp.zeros((2, WIN4, 128), BF16)
    for chunk in CH4:
        column_start(chunk)

    for load in loads[2:]:
        load.wait()
    tmp[...] = jnp.zeros_like(tmp)
    tmp[0:32, 0:192] = i3v[...].reshape(32, 192).astype(F32)
    tmp[32:128, 0:192] = lmv[...].astype(F32)
    tmp[128:256, 0:96] = i4v[...].reshape(128, 96).astype(F32)
    tmp[256:272, 0:96] = rov[...].astype(F32)
    first = pltpu.roll(tmp[0:128, 0:128], 64, 1).astype(BF16)
    second = pltpu.roll(tmp[0:128, 128:256], 64, 1).astype(BF16)
    s3[0, 2:4, 16:32, 0:128] = first[0:32].reshape(2, 16, 128)
    s3[0, 2:4, 16:32, 128:256] = second[0:32].reshape(2, 16, 128)
    lm[0:96, 0:128] = first[32:128]
    lm[0:96, 128:256] = second[32:128]
    lm[96:128, :] = jnp.zeros((32, 256), BF16)
    third = pltpu.roll(tmp[128:272, 0:128], 96, 1).astype(BF16)
    s4[0, 2:6, 16:48, :] = third[0:128].reshape(4, 32, 128)
    ro[...] = third[128:144]
    fine = lax.broadcasted_iota(jnp.int32, (256, 128), 0)
    cell = lax.broadcasted_iota(jnp.int32, (256, 128), 1)
    up[...] = jnp.where((fine // 64) * 32 + lax.rem(fine, 64) // 2 == cell, 1.0, 0.0).astype(BF16)
    j4[:, :, 192:256] = jnp.zeros((8, 64, 64), F32)

    def away(dy, dx):
        oy = 1 - (h + NH - 1) // NH if dy < 0 else (h + 1) // NH if dy > 0 else 0
        ox = 1 - (w + NW - 1) // NW if dx < 0 else (w + 1) // NW if dx > 0 else 0
        return oy + ox - oy * ox

    def neighbour(dy, dx):
        where = {}
        if dy:
            where["ha"] = lax.rem(h + dy + NH, NH)
        if dx:
            where["wa"] = lax.rem(w + dx + NW, NW)
        return where

    def send_3(t):
        for dy, dx in NEIGHBOURS:
            remote(
                s3.at[t, 2:4, 16:32, :],
                s3.at[t + 5 * away(dy, dx), 2 - 2 * dy : 4 - 2 * dy, 16 - 16 * dx : 32 - 16 * dx, :],
                n3_s.at[t], n3_r.at[t], **neighbour(dy, dx),
            ).start()

    def send_4(t):
        for dy, dx in NEIGHBOURS:
            r0, r1 = {-1: (2, 4), 0: (2, 6), 1: (4, 6)}[dy]
            c0, c1 = {-1: (16, 32), 0: (16, 48), 1: (32, 48)}[dx]
            q0, q1 = {-1: (6, 8), 0: (2, 6), 1: (0, 2)}[dy]
            d0, d1 = {-1: (48, 64), 0: (16, 48), 1: (0, 16)}[dx]
            remote(
                s4.at[t, r0:r1, c0:c1, :], s4.at[t + 4 * away(dy, dx), q0:q1, d0:d1, :],
                n4_s.at[t], n4_r.at[t], **neighbour(dy, dx),
            ).start()

    view_3 = s3.at[0:4, 0:2, 0:32, :]
    view_4 = s4.at[0:3, 2:6, 16:48, :]
    view_x = xb.at[0:2, 0:4, 0:4, 0:32, :]
    view_a = xb.at[0, 0:3, 2:4, 16:32, :]

    send_3(0)
    wait_bytes(view_a, xa_r)
    for dy, dx in NEIGHBOURS:
        remote(
            xb.at[0, :, 2:4, 16:32, :],
            xb.at[away(dy, dx), :, 2 - 2 * dy : 4 - 2 * dy, 16 - 16 * dx : 32 - 16 * dx, :],
            xn_s, xn_r, **neighbour(dy, dx),
        ).start()
    send_4(0)

    def merged3(slot):
        out = []
        for g in (0, 2):
            a, b = s13[g, slot], s13[g + 1, slot]
            out += [a[0:64], a[64:80] + b[0:16], b[16:80]]
        return jnp.concatenate(out, 0)

    def merged4(slot):
        a, b, c, d = (s14[i, slot] for i in range(4))
        return jnp.concatenate(
            [a[0:32], a[32:48] + b[0:16], b[16:32], b[32:48] + c[0:16], c[16:32], c[32:48] + d[0:16], d[16:48]], 0
        )

    def piece(chunk, c, owner):
        level, slot, n = CHUNKS[chunk]
        wb, per = (wb3, X3) if level == 3 else (wb4, X4)
        first = owner if slot == 0 else 8 + owner * per + slot - 1
        return wb.at[c, pl.ds(first, n)]

    def along_wa(chunk):
        return CHUNKS[chunk][1] == 0

    def plane_copy(chunk, d, owner):
        part = piece(chunk, core, owner)
        if along_wa(chunk):
            return remote(part, part, z_s.at[chunk, d], z_r.at[chunk, d], wa=lax.rem(w + d, NW))
        return remote(part, part, x_s.at[chunk, d], x_r.at[chunk, d], section=lax.rem(s + d, NS))

    def owner_of(chunk, d):
        return lax.rem(w + NW - d, NW) if along_wa(chunk) else lax.rem(s + NS - d, NS)

    def order(chunk):
        return Z_ORDER if along_wa(chunk) else X_ORDER

    def share(chunk, d):
        part = piece(chunk, core, owner_of(chunk, d))
        remote(part, part, f_s.at[chunk], f_r.at[chunk], ha=sister).start()

    def shared_view(chunk):
        level, slot, n = CHUNKS[chunk]
        return (wb3 if level == 3 else wb4).at[0, 0 : 8 if slot == 0 else NS * n]

    def plane_start(chunk):
        level, slot, n = CHUNKS[chunk]
        column_wait(chunk)
        wb, merged, per = (wb3, merged3, X3) if level == 3 else (wb4, merged4, X4)
        for k in range(n):
            kb = w if slot == 0 else 8 + s * per + slot - 1 + k
            wb[pl.ds(core, 1), pl.ds(kb, 1)] = merged(slot + k)[None, None]
        for d in order(chunk):
            plane_copy(chunk, d, owner_of(chunk, 0)).start()
        share(chunk, 0)

    def plane_pass(chunk, ds):
        for d in ds:
            plane_copy(chunk, d, owner_of(chunk, d)).wait_recv()
            share(chunk, d)

    for chunk in (0, 1, 2):
        plane_start(chunk)
    plane_pass(0, X_ORDER)
    plane_start(3)
    plane_pass(1, X_ORDER)
    plane_start(4)
    plane_pass(2, Z_ORDER[:4])
    plane_pass(3, X_ORDER)
    for chunk in CH4:
        plane_start(chunk)
    plane_pass(2, Z_ORDER[4:])
    plane_pass(4, X_ORDER)
    wait_bytes(view_3, n3_r.at[0])
    wait_bytes(view_x, xn_r)
    wait_bytes(view_4, n4_r.at[0])
    for chunk in CH3:
        wait_bytes(shared_view(chunk), f_r.at[chunk])

    def gates3(a):
        blocks = []
        for kb in range(9 * a, 9 * a + 9):
            lo, hi = wb3.at[0, kb], wb3.at[1, kb]
            blocks.append(jnp.concatenate([
                lo[64:128, :], lo[0:64, :], lo[128:192, :], lo[128:192, :],
                lo[256:288, :], hi[0:32, :], lo[192:256, :], hi[32:96, :], hi[32:96, :],
            ], 0))
        return jnp.concatenate(blocks, 1)

    def cand3(a):
        zero = jnp.zeros((64, 128), BF16)
        blocks = []
        for kb in range(9 * a, 9 * a + 9):
            hi = wb3.at[1, kb]
            blocks.append(jnp.concatenate([hi[160:224, :], hi[96:160, :], zero, hi[224:288, :]], 0))
        return jnp.concatenate(blocks, 1)

    def gates4(a):
        blocks = []
        for kb in range(6 * a, 6 * a + 6):
            lo, hi = wb4.at[0, kb], wb4.at[1, kb]
            blocks.append(jnp.concatenate([
                lo[32:96, :], lo[0:32, :], lo[0:32, :],
                lo[128:144, :], hi[0:48, :], lo[96:128, :], lo[96:128, :],
            ], 0))
        return jnp.concatenate(blocks, 1)

    def cand4(a):
        zero = jnp.zeros((32, 128), BF16)
        blocks = []
        for kb in range(6 * a, 6 * a + 6):
            hi = wb4.at[1, kb]
            blocks.append(jnp.concatenate([hi[80:144, :], zero, hi[48:80, :]], 0))
        return jnp.concatenate(blocks, 1)

    def taps(ref, r0, r1, c0, c1):
        return jnp.concatenate([ref[r0:r1, c0 + b - 1 : c1 + b - 1, :].astype(BF16) for b in range(3)], 2)

    def level3(t):
        x = xb[0, t].astype(F32)
        p = s3[t].astype(F32)
        j3[:, :, 0:128] = x[:, :, 0:128]
        j3[:, :, 128:256] = p[:, :, 0:128]
        j3[:, :, 256:320] = x[:, :, 128:192]
        j3[:, :, 320:384] = p[:, :, 192:256]
        u = taps(j3, 0, 6, 8, 40)
        sums = sum(nt(u[a : a + 4].reshape(128, 1152), gates3(a)) for a in range(3))
        reset = jax.nn.sigmoid(sums[:, :256]).reshape(4, 32, 256)
        update = jax.nn.sigmoid(sums[:, 256:]).reshape(4, 32, 256)[1:3, 8:24, :]
        gated = reset * p[1:5, 8:40, :]
        j3[1:5, 8:40, 128:256] = gated[:, :, 0:128]
        j3[1:5, 8:40, 320:384] = gated[:, :, 192:256]
        v = taps(j3, 1, 5, 16, 32)
        fresh = sum(nt(v[a : a + 2].reshape(32, 1152), cand3(a)) for a in range(3))
        fresh = jnp.maximum(fresh, 0.0).reshape(2, 16, 256)
        prior = p[2:4, 16:32, :]
        s3[t + 1, 2:4, 16:32, :] = (update * prior + (1.0 - update) * fresh).astype(BF16)

    def to_lead(t):
        return remote(pt.at[t], po.at[s], out_s.at[t], out_r, section=t)

    def level4(t):
        coarse = s3[t + 1, 1:5].astype(F32)[:, 8:40, :].astype(BF16).reshape(128, 256)
        lift = nt(coarse, lm[...]).astype(BF16)
        lifted = jnp.dot(up[...], lift, preferred_element_type=F32).reshape(4, 64, 128)
        p = s4[t].astype(F32)
        for i in range(8):
            j4[i, :, 0:96] = lifted[i // 2, :, 0:96]
        j4[:, :, 96:128] = p[:, :, 96:128]
        j4[:, :, 128:192] = p[:, :, 0:64]
        u = taps(j4, 0, 8, 8, 56)
        sums = sum(nt(u[a : a + 6].reshape(288, 768), gates4(a)) for a in range(3))
        reset = jax.nn.sigmoid(sums[:, :128]).reshape(6, 48, 128)
        update = jax.nn.sigmoid(sums[:, 128:]).reshape(6, 48, 128)[1:5, 8:40, :]
        gated = reset * p[1:7, 8:56, :]
        j4[1:7, 8:56, 96:128] = gated[:, :, 96:128]
        j4[1:7, 8:56, 128:192] = gated[:, :, 0:64]
        v = taps(j4, 1, 7, 16, 48)
        fresh = sum(nt(v[a : a + 4].reshape(128, 768), cand4(a)) for a in range(3))
        fresh = jnp.maximum(fresh, 0.0).reshape(4, 32, 128)
        prior = p[2:6, 16:48, :]
        state = (update * prior + (1.0 - update) * fresh).astype(BF16)
        if t < LEADS - 1:
            s4[t + 1, 2:6, 16:48, :] = state
            send_4(t + 1)
        pt[t] = nt(ro[...], state.reshape(128, 128))

        @pl.when(s == t)
        def _():
            po[t] = pt[t]

        @pl.when(s != t)
        def _():
            to_lead(t).start()

    level3(0)
    send_3(1)
    for chunk in CH4:
        plane_pass(chunk, order(chunk))
    for t in range(LEADS):
        wait_bytes(view_3, n3_r.at[t + 1])
        if t + 1 < LEADS:
            level3(t + 1)
            send_3(t + 2)
        if t == 0:
            for chunk in CH4:
                wait_bytes(shared_view(chunk), f_r.at[chunk])
        else:
            wait_bytes(view_4, n4_r.at[t])
        level4(t)

    wait_bytes(po.at[0:3], out_r)
    o_ref[...] = po[...]

    raw3.wait_send()
    raw4.wait_send()
    wait_bytes(view_a, xa_s)
    wait_bytes(view_x, xn_s)
    for t in range(LEADS + 1):
        wait_bytes(view_3, n3_s.at[t])
    for t in range(LEADS):
        wait_bytes(view_4, n4_s.at[t])
    for chunk in range(len(CHUNKS)):
        level, slot, n = CHUNKS[chunk]
        s1 = s13 if level == 3 else s14
        @pl.when(alone)
        def _(s1=s1, slot=slot, n=n, chunk=chunk):
            wait_bytes(s1.at[0:3, slot : slot + n], col_s.at[chunk])
        @pl.when(jnp.logical_not(alone))
        def _(s1=s1, slot=slot, n=n, chunk=chunk):
            wait_bytes(s1.at[:, slot : slot + n], col_s.at[chunk])
        for d in order(chunk):
            plane_copy(chunk, d, owner_of(chunk, 0)).wait_send()
        wait_bytes(shared_view(chunk), f_s.at[chunk])
    for t in range(LEADS):
        @pl.when(s != t)
        def _(t=t):
            to_lead(t).wait_send()


def local(coarse_inputs, init_level3, init_level4, weight_level3, weight_level4, lift_map, readout):
    n = len(CHUNKS)
    dma = pltpu.SemaphoreType.DMA
    fields = pl.pallas_call(
        kernel,
        out_shape=jax.ShapeDtypeStruct((4, 16, 128), F32),
        in_specs=[pl.BlockSpec(memory_space=pl.ANY)] * 7,
        out_specs=pl.BlockSpec(memory_space=pltpu.VMEM),
        scratch_shapes=[
            pltpu.VMEM((2, 16, 192), BF16),
            pltpu.VMEM((4, 32, 96), BF16),
            pltpu.VMEM((96, 192), BF16),
            pltpu.VMEM((16, 96), BF16),
            pltpu.VMEM((9, 36, 384), BF16),
            pltpu.VMEM((9, 18, 192), BF16),
            pltpu.VMEM((9, 36, 384), BF16),
            pltpu.VMEM((9, 18, 192), BF16),
            pltpu.VMEM((K3, WIN3, 128), BF16),
            pltpu.VMEM((K4, WIN4, 128), BF16),
            pltpu.VMEM((4, 1 + X3, WIN3, 128), BF16),
            pltpu.VMEM((4, 1 + X4, WIN4, 128), BF16),
            pltpu.VMEM((2, K3, H3R, 128), BF16),
            pltpu.VMEM((2, K4, H4R, 128), BF16),
            pltpu.VMEM((2, 4, 6, 48, 192), BF16),
            pltpu.VMEM((10, 6, 48, 256), BF16),
            pltpu.VMEM((8, 8, 64, 128), BF16),
            pltpu.VMEM((6, 48, 384), F32),
            pltpu.VMEM((8, 64, 256), F32),
            pltpu.VMEM((272, 256), F32),
            pltpu.VMEM((128, 256), BF16),
            pltpu.VMEM((16, 128), BF16),
            pltpu.VMEM((256, 128), BF16),
            pltpu.VMEM((4, 16, 128), F32),
            pltpu.VMEM((4, 16, 128), F32),
            dma((7,)), dma((2,)), dma((2,)), dma((n,)), dma((n,)),
            dma((n, NS)), dma((n, NS)), dma((n, NW)), dma((n, NW)), dma((n,)), dma((n,)),
            dma, dma, dma, dma, dma((5,)), dma((5,)), dma((4,)), dma((4,)), dma((4,)), dma,
        ],
        compiler_params=pltpu.CompilerParams(
            collective_id=0, has_side_effects=True, vmem_limit_bytes=64 << 20
        ),
        name="nowcast",
    )(
        coarse_inputs[0].transpose(0, 2, 3, 1),
        init_level3.transpose(1, 2, 0),
        init_level4.transpose(1, 2, 0),
        weight_level3.transpose(1, 0, 2),
        weight_level4.transpose(1, 0, 2),
        lift_map,
        readout,
    )
    return fields.reshape(1, 4, 16, 4, 32)


def solution(mesh):
    return jax.shard_map(
        local,
        mesh=mesh,
        in_specs=(
            P("section", None, None, "ha", "wa"),
            P(None, "ha", "wa"),
            P(None, "ha", "wa"),
            P("ha", None, None),
            P("ha", None, None),
            P(),
            P(),
        ),
        out_specs=P("section", None, None, "ha", "wa"),
        check_vma=False,
    )
```

```python
import jax
import jax.numpy as jnp
from jax import lax
from jax.experimental import pallas as pl
from jax.experimental.pallas import tpu as pltpu
from jax.sharding import PartitionSpec as P

MESH = pl.DeviceIdType.MESH
BF16 = jnp.bfloat16
F32 = jnp.float32

NS, NH, NW = 4, 16, 8
LEADS = 4

X3, X4 = 4, 2
C3, C4 = 3, 2
K3, K4 = 8 + NS * X3 + C3, 8 + NS * X4 + C4
H3R, H4R = 288, 144
WIN3, WIN4 = 80, 48

CHUNKS = [(3, 0, 1), (3, 1, 1), (3, 2, 1), (3, 3, 2), (4, 0, 1), (4, 1, 2), (3, 5, 3), (4, 3, 2)]
CH3, CH4 = (0, 1, 2, 3, 6), (4, 5, 7)

NEIGHBOURS = [(-1, -1), (-1, 1), (1, -1), (1, 1), (0, -1), (0, 1), (-1, 0), (1, 0)]
X_ORDER = (1, 3, 2)
Z_ORDER = (1, 7, 2, 6, 3, 5, 4)


def nt(a, b):
    return lax.dot_general(a, b, (((1,), (1,)), ((), ())), preferred_element_type=F32)


def kernel(
    x_ref, i3_ref, i4_ref, w3_ref, w4_ref, lm_ref, ro_ref, o_ref,
    i3v, i4v, lmv, rov, own3, own4, sis3, sis4, cw3, cw4, s13, s14, wb3, wb4,
    xc, xe, xh, s3c, s3e, s3h, s4c, s4e, s4h, jx, j3, j4, p4, xg, xk, tmp, lm, ro, up, pt, po,
    load_sem, raw_s, raw_r, col_s, col_r, x_s, x_r, z_s, z_r, f_s, f_r,
    xa_s, xa_r, xn_s, xn_r, n3_s, n3_r, n4_s, n4_r, out_s, out_r,
):
    s = lax.axis_index("section")
    h = lax.axis_index("ha")
    w = lax.axis_index("wa")
    core = lax.rem(h, 2)
    y = h // 2
    sister = h + 1 - 2 * core
    half = y // 4

    def remote(src, dst, send, recv, **where):
        return pltpu.make_async_remote_copy(
            src_ref=src, dst_ref=dst, send_sem=send, recv_sem=recv, device_id=where, device_id_type=MESH
        )

    def wait_bytes(view, sem):
        pltpu.make_async_copy(view, view, sem).wait()

    for ref, n in ((xc, 1), (xh, 1), (s3c, 5), (s3h, 5), (s4c, 3), (s4h, 3)):
        ref[0:n] = jnp.zeros((n,) + ref.shape[1:], BF16)
    loads = [
        pltpu.make_async_copy(src, dst, load_sem.at[k])
        for k, (src, dst) in enumerate([
            (w3_ref, own3), (w4_ref, own4), (x_ref.at[s], xc.at[0, s, 2:4]),
            (i3_ref, i3v), (i4_ref, i4v), (lm_ref, lmv), (ro_ref, rov),
        ])
    ]
    for load in loads:
        load.start()

    def shifted(rows, count, offset):
        r = lax.broadcasted_iota(jnp.int32, (rows, count), 0)
        c = lax.broadcasted_iota(jnp.int32, (rows, count), 1)
        return jnp.where(r == c + offset, 1.0, 0.0).astype(BF16)

    low = lax.broadcasted_iota(jnp.int32, (1, 128), 1) < 64

    def place3(shard, which, add):
        put = shifted(WIN3, 36, 8 * lax.rem(y, 2) + 36 * which)
        for tap in range(9):
            rows = jnp.dot(put, shard[tap], preferred_element_type=F32)
            v1, v2 = rows[:, 128:256], rows[:, 256:384]
            for k, v in enumerate((rows[:, :128], jnp.where(low, v2, v1), jnp.where(low, v1, v2))):
                v = v.astype(BF16)
                cw3[3 * tap + k] = cw3[3 * tap + k] + v if add else v

    def place4(shard, which, add):
        put = shifted(WIN4, 18, 4 * lax.rem(y, 4) + 18 * which)
        for tap in range(9):
            rows = jnp.dot(put, shard[tap], preferred_element_type=F32)
            tmp[0:WIN4, 0:64] = rows[:, 128:192]
            tmp[0:WIN4, 64:128] = jnp.zeros((WIN4, 64), F32)
            for k, v in enumerate((rows[:, :128], tmp[0:WIN4, 0:128])):
                v = v.astype(BF16)
                cw4[2 * tap + k] = cw4[2 * tap + k] + v if add else v

    barrier = pltpu.get_barrier_semaphore()
    alone = (half == core) & (lax.rem(y, 2) == core)
    count = 0
    greet = [{"ha": sister}, {"ha": lax.rem(h + 2 * core + NH - 1, NH)}]
    greet += [{"wa": lax.rem(w + d, NW)} for d in range(1, NW)]
    greet += [{"section": lax.rem(s + d, NS)} for d in range(1, NS)]
    greet += [
        {"ha": lax.rem(h + dy, NH), "wa": lax.rem(w + dx, NW)} for dy in (1, NH - 1) for dx in (1, NW - 1)
    ]
    for where in greet:
        pl.semaphore_signal(barrier, inc=1, device_id=where, device_id_type=MESH)
    for i in range(4):
        source = 2 * (4 * core + i) + lax.rem(y, 2)
        @pl.when(source != h)
        def _(source=source):
            pl.semaphore_signal(barrier, inc=1, device_id={"ha": source}, device_id_type=MESH)
    loads[0].wait()
    place3(own3, core, False)
    loads[1].wait()
    place4(own4, core, False)
    pl.semaphore_wait(barrier, len(greet) + 4 - alone.astype(jnp.int32))

    raw3 = remote(w3_ref, sis3, raw_s.at[0], raw_r.at[0], ha=sister)
    raw4 = remote(w4_ref, sis4, raw_s.at[1], raw_r.at[1], ha=sister)
    raw3.start()
    raw4.start()
    for d in range(1, NS):
        m = lax.rem(s + d, NS)
        remote(x_ref.at[m], xc.at[0, s, 2:4], xa_s, xa_r, section=m).start()

    raw3.wait_recv()
    place3(sis3, 1 - core, True)

    def first_block(chunk, z, x):
        level, slot, n = CHUNKS[chunk]
        per = X3 if level == 3 else X4
        if slot == 0:
            return z
        return 8 + x * per + slot - 1 if slot <= per else 8 + (NS - 1) * per + slot - 1

    def column_parts(chunk):
        level, slot, n = CHUNKS[chunk]
        cw, s1 = (cw3, s13) if level == 3 else (cw4, s14)
        first = first_block(chunk, w, s)
        return cw.at[pl.ds(first, n)], s1.at[lax.rem(y, 4), slot : slot + n], s1.at[:, slot : slot + n]

    def column_start(chunk):
        src, dst, _ = column_parts(chunk)
        for i in range(4):
            target = 2 * (2 * i + core) + half
            @pl.when(target != h)
            def _(target=target):
                remote(src, dst, col_s.at[chunk], col_r.at[chunk], ha=target).start()
        @pl.when(alone)
        def _():
            pltpu.make_async_copy(src, dst, col_r.at[chunk]).start()

    def column_wait(chunk):
        wait_bytes(column_parts(chunk)[2], col_r.at[chunk])

    for chunk in range(4):
        column_start(chunk)
    raw4.wait_recv()
    place4(sis4, 1 - core, True)
    for chunk in range(4, 8):
        column_start(chunk)

    def edges(e, t, tile, rows):
        lanes = tile.shape[-1]
        e[t, 0] = tile[:, 0:8, :].reshape(rows * 8, lanes).astype(BF16)
        e[t, 1] = tile[:, tile.shape[1] - 8 :, :].reshape(rows * 8, lanes).astype(BF16)

    def keep3(t, tile):
        s3c[t, 2:4] = tile.astype(BF16)
        edges(s3e, t, tile, 2)

    def keep4(t, tile):
        s4c[t, 4:8] = tile.astype(BF16)
        edges(s4e, t, tile, 4)

    for load in loads[2:]:
        load.wait()
    tmp[...] = jnp.zeros_like(tmp)
    tmp[0:32, 0:192] = i3v[...].reshape(32, 192).astype(F32)
    tmp[32:128, 0:192] = lmv[...].astype(F32)
    tmp[128:256, 0:96] = i4v[...].reshape(128, 96).astype(F32)
    tmp[256:272, 0:96] = rov[...].astype(F32)
    first = pltpu.roll(tmp[0:128, 0:128], 64, 1).astype(BF16)
    second = pltpu.roll(tmp[0:128, 128:256], 64, 1).astype(BF16)
    tmp[0:32, 0:128] = pltpu.roll(tmp[0:32, 0:128], 64, 1)
    tmp[0:32, 128:256] = pltpu.roll(tmp[0:32, 128:256], 64, 1)
    keep3(0, tmp[0:32, 0:256].reshape(2, 16, 256))
    lm[0:96, 0:128] = first[32:128]
    lm[0:96, 128:256] = second[32:128]
    lm[96:128, :] = jnp.zeros((32, 256), BF16)
    third = pltpu.roll(tmp[128:272, 0:128], 96, 1)
    keep4(0, third[0:128].reshape(4, 32, 128))
    ro[...] = third[128:144].astype(BF16)
    fine = lax.broadcasted_iota(jnp.int32, (384, 192), 0)
    cell = lax.broadcasted_iota(jnp.int32, (384, 192), 1)
    up[...] = jnp.where((fine // 64) * 32 + lax.rem(fine, 64) // 2 == cell, 1.0, 0.0).astype(BF16)
    j4[:, :, 192:256] = jnp.zeros((12, 64, 64), F32)

    def away(dy, dx):
        oy = 1 - (h + NH - 1) // NH if dy < 0 else (h + 1) // NH if dy > 0 else 0
        ox = 1 - (w + NW - 1) // NW if dx < 0 else (w + 1) // NW if dx > 0 else 0
        return oy + ox - oy * ox

    def neighbour(dy, dx):
        where = {}
        if dy:
            where["ha"] = lax.rem(h + dy + NH, NH)
        if dx:
            where["wa"] = lax.rem(w + dx + NW, NW)
        return where

    def send_tiles(c, e, halo, t, steps, rows, send, recv):
        for dy, dx in NEIGHBOURS:
            to = t + steps * away(dy, dx)
            if dx == 0:
                src, dst = c.at[t, rows : 2 * rows], c.at[to, rows * (1 - dy) : rows * (2 - dy)]
            else:
                src, dst = e.at[t, (dx + 1) // 2], halo.at[to, (1 - dx) // 2, 1 - dy]
            remote(src, dst, send, recv, **neighbour(dy, dx)).start()

    def send_3(t):
        send_tiles(s3c, s3e, s3h, t, 5, 2, n3_s.at[t], n3_r.at[t])

    def send_4(t):
        send_tiles(s4c, s4e, s4h, t, 3, 4, n4_s.at[t], n4_r.at[t])

    view_3 = s3c.at[0:2, 0:5]
    view_4 = s4c.at[0:2, 0:7]
    view_x = xc.at[0:2, :, 0:5]
    view_a = xc.at[0, 0:3, 2:4]

    send_3(0)
    wait_bytes(view_a, xa_r)
    for lead in range(LEADS):
        edges(xe.at[lead], 0, xc[0, lead, 2:4].astype(F32), 2)
    for dy, dx in NEIGHBOURS:
        if dx == 0:
            src, dst = xc.at[0, :, 2:4], xc.at[away(dy, dx), :, 2 - 2 * dy : 4 - 2 * dy]
        else:
            src, dst = xe.at[:, 0, (dx + 1) // 2], xh.at[away(dy, dx), (1 - dx) // 2, 1 - dy]
        remote(src, dst, xn_s, xn_r, **neighbour(dy, dx)).start()
    send_4(0)

    def merged3(slot):
        out = []
        for g in (0, 2):
            a, b = s13[g, slot], s13[g + 1, slot]
            out += [a[0:64], a[64:80] + b[0:16], b[16:80]]
        return jnp.concatenate(out, 0)

    def merged4(slot):
        a, b, c, d = (s14[i, slot] for i in range(4))
        return jnp.concatenate(
            [a[0:32], a[32:48] + b[0:16], b[16:32], b[32:48] + c[0:16], c[16:32], c[32:48] + d[0:16], d[16:48]], 0
        )

    def piece(chunk, c, owner):
        level, slot, n = CHUNKS[chunk]
        return (wb3 if level == 3 else wb4).at[c, pl.ds(first_block(chunk, owner, owner), n)]

    def along_wa(chunk):
        return CHUNKS[chunk][1] == 0

    def plane_copy(chunk, d, owner):
        part = piece(chunk, core, owner)
        if along_wa(chunk):
            return remote(part, part, z_s.at[chunk, d], z_r.at[chunk, d], wa=lax.rem(w + d, NW))
        return remote(part, part, x_s.at[chunk, d], x_r.at[chunk, d], section=lax.rem(s + d, NS))

    def owner_of(chunk, d):
        return lax.rem(w + NW - d, NW) if along_wa(chunk) else lax.rem(s + NS - d, NS)

    def order(chunk):
        level, slot, n = CHUNKS[chunk]
        return Z_ORDER if slot == 0 else X_ORDER if slot <= (X3 if level == 3 else X4) else ()

    def share(chunk, d):
        part = piece(chunk, core, owner_of(chunk, d))
        remote(part, part, f_s.at[chunk], f_r.at[chunk], ha=sister).start()

    def shared_view(chunk):
        level, slot, n = CHUNKS[chunk]
        return (wb3 if level == 3 else wb4).at[0, 0 : (1 + len(order(chunk))) * n]

    def plane_start(chunk):
        level, slot, n = CHUNKS[chunk]
        column_wait(chunk)
        wb, merged = (wb3, merged3) if level == 3 else (wb4, merged4)
        for k in range(n):
            kb = first_block(chunk, w, s) + k
            wb[pl.ds(core, 1), pl.ds(kb, 1)] = merged(slot + k)[None, None]
        for d in order(chunk):
            plane_copy(chunk, d, owner_of(chunk, 0)).start()
        share(chunk, 0)

    def plane_pass(chunk, ds):
        for d in ds:
            plane_copy(chunk, d, owner_of(chunk, d)).wait_recv()
            share(chunk, d)

    for chunk in (0, 1, 2, 3):
        plane_start(chunk)
    plane_pass(1, X_ORDER)
    plane_pass(0, Z_ORDER[:4])
    plane_pass(2, X_ORDER)
    plane_pass(0, Z_ORDER[4:6])
    plane_start(4)
    plane_pass(3, X_ORDER[:2])
    plane_start(5)
    plane_start(6)
    plane_pass(0, Z_ORDER[6:])
    plane_pass(3, X_ORDER[2:])
    wait_bytes(view_3, n3_r.at[0])
    wait_bytes(view_x, xn_r)
    wait_bytes(view_4, n4_r.at[0])
    for chunk in CH3:
        wait_bytes(shared_view(chunk), f_r.at[chunk])

    def wide(halo, centre, rows):
        sides = [halo[k].astype(F32).reshape(rows, 8, centre.shape[-1]) for k in range(2)]
        return jnp.concatenate([sides[0], centre.astype(F32), sides[1]], 1)

    def blocks3(a, kinds):
        return [3 * (3 * a + b) + kind for b in range(3) for kind in kinds]

    def gates3(a, kinds):
        blocks = []
        for kb in blocks3(a, kinds):
            lo, hi = wb3.at[0, kb], wb3.at[1, kb]
            blocks.append(jnp.concatenate([
                lo[64:128, :], lo[0:64, :], lo[128:192, :], lo[128:192, :],
                lo[256:288, :], hi[0:32, :], lo[192:256, :], hi[32:96, :], hi[32:96, :],
            ], 0))
        return jnp.concatenate(blocks, 1)

    def cand3(a, kinds):
        zero = jnp.zeros((64, 128), BF16)
        blocks = []
        for kb in blocks3(a, kinds):
            hi = wb3.at[1, kb]
            blocks.append(jnp.concatenate([hi[160:224, :], hi[96:160, :], zero, hi[224:288, :]], 0))
        return jnp.concatenate(blocks, 1)

    def gates4(a):
        blocks = []
        for kb in range(6 * a, 6 * a + 6):
            lo, hi = wb4.at[0, kb], wb4.at[1, kb]
            blocks.append(jnp.concatenate([
                lo[32:96, :], lo[0:32, :], lo[0:32, :],
                lo[128:144, :], hi[0:48, :], lo[96:128, :], lo[96:128, :],
            ], 0))
        return jnp.concatenate(blocks, 1)

    def cand4(a):
        zero = jnp.zeros((32, 128), BF16)
        blocks = []
        for kb in range(6 * a, 6 * a + 6):
            hi = wb4.at[1, kb]
            blocks.append(jnp.concatenate([hi[80:144, :], zero, hi[48:80, :]], 0))
        return jnp.concatenate(blocks, 1)

    def conv(ref, r0, rows, c0, cols, weights):
        u = jnp.concatenate(
            [ref[r0 - 1 : r0 + rows + 1, c0 + b - 1 : c0 + b - 1 + cols, :].astype(BF16) for b in range(3)], 2
        )
        return sum(nt(u[a : a + rows].reshape(rows * cols, u.shape[2]), weights(a)) for a in range(3))

    def input_sums(t):
        jx[:, 8:40, :] = wide(xh.at[0, :, :, t], xc[0, t], 6)[:, :, 0:128]
        xg[t] = conv(jx, 1, 4, 8, 32, lambda a: gates3(a, (0,)))
        xk[t] = conv(jx, 2, 2, 16, 16, lambda a: cand3(a, (0,)))

    def level3(t):
        p = wide(s3h.at[t], s3c[t], 6)
        j3[:, 8:40, 0:128] = p[:, :, 0:128]
        j3[:, 8:40, 128:192] = wide(xh.at[0, :, :, t], xc[0, t], 6)[:, :, 128:192]
        j3[:, 8:40, 192:256] = p[:, :, 192:256]
        sums = xg[t] + conv(j3, 1, 4, 8, 32, lambda a: gates3(a, (1, 2)))
        reset = jax.nn.sigmoid(sums[:, :256]).reshape(4, 32, 256)
        update = jax.nn.sigmoid(sums[:, 256:]).reshape(4, 32, 256)[1:3, 8:24, :]
        gated = reset * p[1:5]
        j3[1:5, 8:40, 0:128] = gated[:, :, 0:128]
        j3[1:5, 8:40, 192:256] = gated[:, :, 192:256]
        fresh = xk[t] + conv(j3, 2, 2, 16, 16, lambda a: cand3(a, (1, 2)))
        fresh = jnp.maximum(fresh, 0.0).reshape(2, 16, 256)
        prior = p[2:4, 8:24, :]
        keep3(t + 1, update * prior + (1.0 - update) * fresh)
        send_3(t + 1)

    def to_lead(t):
        return remote(pt.at[t], po.at[s], out_s.at[t], out_r, section=t)

    def lift(t):
        coarse = wide(s3h.at[t + 1], s3c[t + 1], 6).astype(BF16).reshape(192, 256)
        lifted = nt(coarse, lm[...]).astype(BF16)
        lifted = jnp.dot(up[...], lifted, preferred_element_type=F32).reshape(6, 64, 128)
        for i in range(12):
            j4[i, :, 0:96] = lifted[i // 2, :, 0:96]

    def level4(t):
        border = 2 if t == LEADS - 2 else 0
        g0, g1 = 3 - border, 9 + border
        p = p4[...] if t == LEADS - 1 else wide(s4h.at[t], s4c[t], 12)
        j4[:, 8:56, 96:128] = p[:, :, 96:128]
        j4[:, 8:56, 128:192] = p[:, :, 0:64]
        sums = conv(j4, g0, g1 - g0, 8, 48, gates4)
        reset = jax.nn.sigmoid(sums[:, :128]).reshape(g1 - g0, 48, 128)
        update = jax.nn.sigmoid(sums[:, 128:]).reshape(g1 - g0, 48, 128)
        gated = reset * p[g0:g1]
        j4[g0:g1, 8:56, 96:128] = gated[:, :, 96:128]
        j4[g0:g1, 8:56, 128:192] = gated[:, :, 0:64]
        c0, cols = (8, 48) if border else (16, 32)
        rows = g1 - g0 - 2
        fresh = conv(j4, g0 + 1, rows, c0, cols, cand4)
        fresh = jnp.maximum(fresh, 0.0).reshape(rows, cols, 128)
        update, prior = update[1 : rows + 1, c0 - 8 : c0 - 8 + cols], p[g0 + 1 : g1 - 1, c0 - 8 : c0 - 8 + cols]
        state = update * prior + (1.0 - update) * fresh
        if border:
            row = lax.broadcasted_iota(jnp.int32, state.shape, 0) + (4 * h + g0 + 1 - 4)
            col = lax.broadcasted_iota(jnp.int32, state.shape, 1) + (32 * w + c0 - 16)
            inside = (row >= 0) & (row < 4 * NH) & (col >= 0) & (col < 32 * NW)
            p4[g0 + 1 : g1 - 1] = jnp.where(inside, state, 0.0).astype(BF16).astype(F32)
            state = state[border : border + 4, 8:40]
        elif t < LEADS - 2:
            keep4(t + 1, state)
            send_4(t + 1)
        pt[t] = nt(ro[...], state.astype(BF16).reshape(128, 128))

        @pl.when(s == t)
        def _():
            po[t] = pt[t]

        @pl.when(s != t)
        def _():
            to_lead(t).start()

    input_sums(0)
    level3(0)
    plane_start(7)
    for t in range(1, LEADS):
        input_sums(t)
    plane_pass(5, X_ORDER)
    for t in range(LEADS):
        wait_bytes(view_3, n3_r.at[t + 1])
        if t + 1 < LEADS:
            level3(t + 1)
        if t == 0:
            plane_pass(4, Z_ORDER)
        lift(t)
        if t == 0:
            for chunk in CH4:
                wait_bytes(shared_view(chunk), f_r.at[chunk])
        if 0 < t < LEADS - 1:
            wait_bytes(view_4, n4_r.at[t])
        level4(t)

    wait_bytes(po.at[0:3], out_r)
    o_ref[...] = po[...]

    raw3.wait_send()
    raw4.wait_send()
    wait_bytes(view_a, xa_s)
    wait_bytes(view_x, xn_s)
    for t in range(LEADS + 1):
        wait_bytes(view_3, n3_s.at[t])
    for t in range(LEADS - 1):
        wait_bytes(view_4, n4_s.at[t])
    for chunk in range(len(CHUNKS)):
        level, slot, n = CHUNKS[chunk]
        s1 = s13 if level == 3 else s14
        @pl.when(alone)
        def _(s1=s1, slot=slot, n=n, chunk=chunk):
            wait_bytes(s1.at[0:3, slot : slot + n], col_s.at[chunk])
        @pl.when(jnp.logical_not(alone))
        def _(s1=s1, slot=slot, n=n, chunk=chunk):
            wait_bytes(s1.at[:, slot : slot + n], col_s.at[chunk])
        for d in order(chunk):
            plane_copy(chunk, d, owner_of(chunk, 0)).wait_send()
        wait_bytes(shared_view(chunk), f_s.at[chunk])
    for t in range(LEADS):
        @pl.when(s != t)
        def _(t=t):
            to_lead(t).wait_send()


def local(coarse_inputs, init_level3, init_level4, weight_level3, weight_level4, lift_map, readout):
    n = len(CHUNKS)
    dma = pltpu.SemaphoreType.DMA
    fields = pl.pallas_call(
        kernel,
        out_shape=jax.ShapeDtypeStruct((4, 16, 128), F32),
        in_specs=[pl.BlockSpec(memory_space=pl.ANY)] * 7,
        out_specs=pl.BlockSpec(memory_space=pltpu.VMEM),
        scratch_shapes=[
            pltpu.VMEM((2, 16, 192), BF16),
            pltpu.VMEM((4, 32, 96), BF16),
            pltpu.VMEM((96, 192), BF16),
            pltpu.VMEM((16, 96), BF16),
            pltpu.VMEM((9, 36, 384), BF16),
            pltpu.VMEM((9, 18, 192), BF16),
            pltpu.VMEM((9, 36, 384), BF16),
            pltpu.VMEM((9, 18, 192), BF16),
            pltpu.VMEM((K3, WIN3, 128), BF16),
            pltpu.VMEM((K4, WIN4, 128), BF16),
            pltpu.VMEM((4, 1 + X3 + C3, WIN3, 128), BF16),
            pltpu.VMEM((4, 1 + X4 + C4, WIN4, 128), BF16),
            pltpu.VMEM((2, K3, H3R, 128), BF16),
            pltpu.VMEM((2, K4, H4R, 128), BF16),
            pltpu.VMEM((2, 4, 6, 16, 192), BF16),
            pltpu.VMEM((4, 1, 2, 16, 192), BF16),
            pltpu.VMEM((2, 2, 3, 4, 16, 192), BF16),
            pltpu.VMEM((10, 6, 16, 256), BF16),
            pltpu.VMEM((5, 2, 16, 256), BF16),
            pltpu.VMEM((10, 2, 3, 16, 256), BF16),
            pltpu.VMEM((6, 12, 32, 128), BF16),
            pltpu.VMEM((3, 2, 32, 128), BF16),
            pltpu.VMEM((6, 2, 3, 32, 128), BF16),
            pltpu.VMEM((6, 48, 128), F32),
            pltpu.VMEM((6, 48, 256), F32),
            pltpu.VMEM((12, 64, 256), F32),
            pltpu.VMEM((12, 48, 128), F32),
            pltpu.VMEM((4, 128, 512), F32),
            pltpu.VMEM((4, 32, 256), F32),
            pltpu.VMEM((272, 256), F32),
            pltpu.VMEM((128, 256), BF16),
            pltpu.VMEM((16, 128), BF16),
            pltpu.VMEM((384, 192), BF16),
            pltpu.VMEM((4, 16, 128), F32),
            pltpu.VMEM((4, 16, 128), F32),
            dma((7,)), dma((2,)), dma((2,)), dma((n,)), dma((n,)),
            dma((n, NS)), dma((n, NS)), dma((n, NW)), dma((n, NW)), dma((n,)), dma((n,)),
            dma, dma, dma, dma, dma((5,)), dma((5,)), dma((3,)), dma((3,)), dma((4,)), dma,
        ],
        compiler_params=pltpu.CompilerParams(
            collective_id=0, has_side_effects=True, vmem_limit_bytes=64 << 20
        ),
        name="nowcast",
    )(
        coarse_inputs[0].transpose(0, 2, 3, 1),
        init_level3.transpose(1, 2, 0),
        init_level4.transpose(1, 2, 0),
        weight_level3.transpose(1, 0, 2),
        weight_level4.transpose(1, 0, 2),
        lift_map,
        readout,
    )
    return fields.reshape(1, 4, 16, 4, 32)


def solution(mesh):
    return jax.shard_map(
        local,
        mesh=mesh,
        in_specs=(
            P("section", None, None, "ha", "wa"),
            P(None, "ha", "wa"),
            P(None, "ha", "wa"),
            P("ha", None, None),
            P("ha", None, None),
            P(),
            P(),
        ),
        out_specs=P("section", None, None, "ha", "wa"),
        check_vma=False,
    )
```

```python
import jax
import jax.numpy as jnp
from jax import lax
from jax.experimental import pallas as pl
from jax.experimental.pallas import tpu as pltpu
from jax.sharding import PartitionSpec as P

MESH = pl.DeviceIdType.MESH
BF16 = jnp.bfloat16
F32 = jnp.float32

NS, NH, NW = 4, 16, 8
LEADS = 4

X3, X4 = 4, 2
C3, C4 = 3, 2
K3, K4 = 8 + NS * X3 + C3, 8 + NS * X4 + C4
H3R, H4R = 288, 144
WIN3, WIN4 = 80, 48

CHUNKS = [(3, 0, 1), (3, 1, 1), (3, 2, 1), (3, 3, 1), (3, 4, 1), (4, 0, 1), (3, 5, 3), (4, 1, 2), (4, 3, 2)]
CH3, CH4 = (0, 1, 2, 3, 4, 6), (5, 7, 8)

NEIGHBOURS = [(-1, -1), (-1, 1), (1, -1), (1, 1), (0, -1), (0, 1), (-1, 0), (1, 0)]

Z_HOPS = [(1, 1, 0), (7, -1, 0), (2, 2, 0), (6, -2, 0), (3, 1, 0), (5, -1, 0), (4, 2, 1), (4, -2, 2)]
Z_RELAY = {2: (4, 6), 3: (5, 7)}
X_HOPS = [(1, 1, 0), (3, -1, 0), (2, 2, 0)]
X_RELAY = {}
XR_HOPS = [(1, 1, 0), (3, -1, 0), (2, 1, 1), (2, -1, 2)]
XR_RELAY = {0: (2,), 1: (3,)}
RELAYED = (1, 2)


def nt(a, b):
    return lax.dot_general(a, b, (((1,), (1,)), ((), ())), preferred_element_type=F32)


def kernel(
    x_ref, i3_ref, i4_ref, w3_ref, w4_ref, lm_ref, ro_ref, o_ref,
    i3v, i4v, lmv, rov, own3, own4, sis3, sis4, cw3, cw4, s13, s14, wb3, wb4,
    xa, xi, xc, xe, xh, s3i, s3w, s4c, s4e, s4h, s4w, jx, j3, j4, p4, xg, xk, tmp, lm, ro, up, pt, po,
    load_sem, raw_s, raw_r, col_s, col_r, x_s, x_r, z_s, z_r, f_s, f_r,
    xa_s, xa_r, x0_s, x0_r, xn_s, xn_r, n3_s, n3_r, n4_s, n4_r, out_s, out_r,
):
    s = lax.axis_index("section")
    h = lax.axis_index("ha")
    w = lax.axis_index("wa")
    core = lax.rem(h, 2)
    y = h // 2
    sister = h + 1 - 2 * core
    half = y // 4

    def remote(src, dst, send, recv, **where):
        return pltpu.make_async_remote_copy(
            src_ref=src, dst_ref=dst, send_sem=send, recv_sem=recv, device_id=where, device_id_type=MESH
        )

    def wait_bytes(view, sem):
        pltpu.make_async_copy(view, view, sem).wait()

    for ref, n in ((xi, 1), (xc, 1), (xh, 1), (s3i, 1), (s3w, 4), (s4c, 1), (s4h, 1), (s4w, 2)):
        ref[0:n] = jnp.zeros((n,) + ref.shape[1:], BF16)
    j3[...] = jnp.zeros_like(j3)
    j4[...] = jnp.zeros_like(j4)
    loads = [
        pltpu.make_async_copy(src, dst, load_sem.at[k])
        for k, (src, dst) in enumerate([
            (w3_ref, own3), (w4_ref, own4), (x_ref.at[s], xa.at[s]),
            (i3_ref, i3v), (i4_ref, i4v), (lm_ref, lmv), (ro_ref, rov),
        ])
    ]
    for load in loads:
        load.start()

    def shifted(rows, count, offset):
        r = lax.broadcasted_iota(jnp.int32, (rows, count), 0)
        c = lax.broadcasted_iota(jnp.int32, (rows, count), 1)
        return jnp.where(r == c + offset, 1.0, 0.0).astype(BF16)

    low = lax.broadcasted_iota(jnp.int32, (1, 128), 1) < 64

    def place3(shard, which, add):
        put = shifted(WIN3, 36, 8 * lax.rem(y, 2) + 36 * which)
        for tap in range(9):
            rows = jnp.dot(put, shard[tap], preferred_element_type=F32)
            v1, v2 = rows[:, 128:256], rows[:, 256:384]
            for k, v in enumerate((rows[:, :128], jnp.where(low, v2, v1), jnp.where(low, v1, v2))):
                v = v.astype(BF16)
                cw3[9 * k + tap] = cw3[9 * k + tap] + v if add else v

    def place4(shard, which, add):
        put = shifted(WIN4, 18, 4 * lax.rem(y, 4) + 18 * which)
        for tap in range(9):
            rows = jnp.dot(put, shard[tap], preferred_element_type=F32)
            tmp[0:WIN4, 0:64] = rows[:, 128:192]
            tmp[0:WIN4, 64:128] = jnp.zeros((WIN4, 64), F32)
            for k, v in enumerate((rows[:, :128], tmp[0:WIN4, 0:128])):
                v = v.astype(BF16)
                cw4[2 * tap + k] = cw4[2 * tap + k] + v if add else v

    barrier = pltpu.get_barrier_semaphore()
    alone = (half == core) & (lax.rem(y, 2) == core)
    count = 0
    greet = [{"ha": sister}, {"ha": lax.rem(h + 2 * core + NH - 1, NH)}]
    greet += [{"wa": lax.rem(w + d, NW)} for d in (1, 2, NW - 2, NW - 1)]
    greet += [{"section": lax.rem(s + d, NS)} for d in range(1, NS)]
    greet += [
        {"ha": lax.rem(h + dy, NH), "wa": lax.rem(w + dx, NW)} for dy in (1, NH - 1) for dx in (1, NW - 1)
    ]
    for where in greet:
        pl.semaphore_signal(barrier, inc=1, device_id=where, device_id_type=MESH)
    for i in range(4):
        source = 2 * (4 * core + i) + lax.rem(y, 2)
        @pl.when(source != h)
        def _(source=source):
            pl.semaphore_signal(barrier, inc=1, device_id={"ha": source}, device_id_type=MESH)
    loads[0].wait()
    place3(own3, core, False)
    loads[1].wait()
    place4(own4, core, False)
    pl.semaphore_wait(barrier, len(greet) + 4 - alone.astype(jnp.int32))

    raw3 = remote(w3_ref, sis3, raw_s.at[0], raw_r.at[0], ha=sister)
    raw4 = remote(w4_ref, sis4, raw_s.at[1], raw_r.at[1], ha=sister)
    raw3.start()
    raw4.start()
    for d in range(1, NS):
        m = lax.rem(s + d, NS)
        remote(x_ref.at[m], xa.at[s], xa_s, xa_r, section=m).start()

    raw3.wait_recv()
    place3(sis3, 1 - core, True)

    def first_block(chunk, z, x):
        level, slot, n = CHUNKS[chunk]
        per = X3 if level == 3 else X4
        if slot == 0:
            return z
        return 8 + x * per + slot - 1 if slot <= per else 8 + (NS - 1) * per + slot - 1

    def column_parts(chunk):
        level, slot, n = CHUNKS[chunk]
        cw, s1 = (cw3, s13) if level == 3 else (cw4, s14)
        first = first_block(chunk, w, s)
        return cw.at[pl.ds(first, n)], s1.at[lax.rem(y, 4), slot : slot + n], s1.at[:, slot : slot + n]

    def column_start(chunk):
        src, dst, _ = column_parts(chunk)
        for i in range(4):
            target = 2 * (2 * i + core) + half
            @pl.when(target != h)
            def _(target=target):
                remote(src, dst, col_s.at[chunk], col_r.at[chunk], ha=target).start()
        @pl.when(alone)
        def _():
            pltpu.make_async_copy(src, dst, col_r.at[chunk]).start()

    def column_wait(chunk):
        wait_bytes(column_parts(chunk)[2], col_r.at[chunk])

    for chunk in range(5):
        column_start(chunk)
    raw4.wait_recv()
    place4(sis4, 1 - core, True)
    for load in loads[2:]:
        load.wait()
    tmp[...] = jnp.zeros_like(tmp)
    tmp[0:32, 0:192] = i3v[...].reshape(32, 192).astype(F32)
    tmp[32:128, 0:192] = lmv[...].astype(F32)
    tmp[128:256, 0:96] = i4v[...].reshape(128, 96).astype(F32)
    tmp[256:272, 0:96] = rov[...].astype(F32)
    first = pltpu.roll(tmp[0:128, 0:128], 64, 1).astype(BF16)
    second = pltpu.roll(tmp[0:128, 128:256], 64, 1).astype(BF16)
    tmp[0:32, 0:128] = pltpu.roll(tmp[0:32, 0:128], 64, 1)
    tmp[0:32, 128:256] = pltpu.roll(tmp[0:32, 128:256], 64, 1)
    s3i[0, 2:4, 16:32, :] = tmp[0:32, 0:256].reshape(2, 16, 256).astype(BF16)
    lm[0:96, 0:128] = first[32:128]
    lm[0:96, 128:256] = second[32:128]
    lm[96:128, :] = jnp.zeros((32, 256), BF16)
    third = pltpu.roll(tmp[128:272, 0:128], 96, 1)
    s4c[0, 4:8] = third[0:128].reshape(4, 32, 128).astype(BF16)
    for k in range(2):
        s4e[k] = third[0:128].reshape(4, 32, 128)[:, 24 * k : 24 * k + 8, :].reshape(32, 128).astype(BF16)
    ro[...] = third[128:144].astype(BF16)
    fine = lax.broadcasted_iota(jnp.int32, (384, 192), 0)
    cell = lax.broadcasted_iota(jnp.int32, (384, 192), 1)
    up[...] = jnp.where((fine // 64) * 32 + lax.rem(fine, 64) // 2 == cell, 1.0, 0.0).astype(BF16)

    def away(dy, dx):
        oy = 1 - (h + NH - 1) // NH if dy < 0 else (h + 1) // NH if dy > 0 else 0
        ox = 1 - (w + NW - 1) // NW if dx < 0 else (w + 1) // NW if dx > 0 else 0
        return oy + ox - oy * ox

    def neighbour(dy, dx):
        where = {}
        if dy:
            where["ha"] = lax.rem(h + dy + NH, NH)
        if dx:
            where["wa"] = lax.rem(w + dx + NW, NW)
        return where

    def send_rows(ref, t, steps, rows, send, recv):
        for dy in (-1, 1):
            to = t + steps * away(dy, 0)
            remote(
                ref.at[t, rows : 2 * rows], ref.at[to, rows * (1 - dy) : rows * (2 - dy)], send, recv, **neighbour(dy, 0)
            ).start()

    def send_3(t):
        send_rows(s3w, t, 4, 2, n3_s.at[t], n3_r.at[t])

    def send_4(t):
        send_rows(s4w, t, 2, 4, n4_s.at[t], n4_r.at[t])

    view_3 = s3w.at[0, 0:4]
    view_4 = s4w.at[0, 0:8]
    view_a = xa.at[0:3]
    view_s3 = s3i.at[0:2, 0:4, 0:32]
    view_x0 = xi.at[0:2, 0:4, 0:32]
    view_x = xc.at[0:2, 0:3, 0:5]
    view_s4 = s4c.at[0:2, 0:7]

    def send_whole(src, dst, send, recv):
        for dy, dx in NEIGHBOURS:
            remote(
                src, dst.at[away(dy, dx), 2 - 2 * dy : 4 - 2 * dy, 16 - 16 * dx : 32 - 16 * dx], send, recv,
                **neighbour(dy, dx),
            ).start()

    def send_borders():
        send_whole(s3i.at[0, 2:4, 16:32], s3i, n3_s.at[4], n3_r.at[4])
        wait_bytes(view_a, xa_r)
        xi[0, 2:4, 16:32, :] = xa[0]
        send_whole(xa.at[0], xi, x0_s, x0_r)
        for lead in range(1, LEADS):
            xc[0, lead - 1, 2:4] = xa[lead]
            tile = xa[lead].astype(F32)
            for k in range(2):
                xe[lead - 1, k] = tile[:, 8 * k : 8 * k + 8, :].reshape(16, 192).astype(BF16)
        for dy, dx in NEIGHBOURS:
            to = away(dy, dx)
            if dx == 0:
                one = xa.at[1:4], xc.at[to, :, 2 - 2 * dy : 4 - 2 * dy]
                two = s4c.at[0, 4:8], s4c.at[to, 4 - 4 * dy : 8 - 4 * dy]
            else:
                one = xe.at[:, (dx + 1) // 2], xh.at[to, (1 - dx) // 2, 1 - dy]
                two = s4e.at[(dx + 1) // 2], s4h.at[to, (1 - dx) // 2, 1 - dy]
            remote(*one, xn_s, xn_r, **neighbour(dy, dx)).start()
            remote(*two, n4_s.at[2], n4_r.at[2], **neighbour(dy, dx)).start()

    def wait_borders():
        wait_bytes(view_s3, n3_r.at[4])
        wait_bytes(view_x0, x0_r)
        wait_bytes(view_x, xn_r)
        wait_bytes(view_s4, n4_r.at[2])

    def merged3(slot):
        out = []
        for g in (0, 2):
            a, b = s13[g, slot], s13[g + 1, slot]
            out += [a[0:64], a[64:80] + b[0:16], b[16:80]]
        return jnp.concatenate(out, 0)

    def merged4(slot):
        a, b, c, d = (s14[i, slot] for i in range(4))
        return jnp.concatenate(
            [a[0:32], a[32:48] + b[0:16], b[16:32], b[32:48] + c[0:16], c[16:32], c[32:48] + d[0:16], d[16:48]], 0
        )

    def hops(chunk):
        level, slot, n = CHUNKS[chunk]
        if slot == 0:
            return Z_HOPS, Z_RELAY
        if slot <= (X3 if level == 3 else X4):
            return (XR_HOPS, XR_RELAY) if chunk in RELAYED else (X_HOPS, X_RELAY)
        return [], {}

    def piece(chunk, owner, part):
        level, slot, n = CHUNKS[chunk]
        wb, rows, cut = (wb3, H3R, 144) if level == 3 else (wb4, H4R, 80)
        lo, hi = ((0, rows), (0, cut), (cut, rows))[part]
        return wb.at[core, pl.ds(first_block(chunk, owner, owner), n), lo:hi]

    def along(chunk):
        return (w, NW, "wa", z_s, z_r) if CHUNKS[chunk][1] == 0 else (s, NS, "section", x_s, x_r)

    def hop(chunk, k):
        d, step, part = hops(chunk)[0][k]
        me, size, axis, send, recv = along(chunk)
        view = piece(chunk, lax.rem(me + step - d + 2 * size, size), part)
        return remote(view, view, send.at[chunk, k], recv.at[chunk, k], **{axis: lax.rem(me + step + size, size)})

    def received(chunk, k):
        d, step, part = hops(chunk)[0][k]
        me, size, axis, send, recv = along(chunk)
        return piece(chunk, lax.rem(me - d + size, size), part), recv.at[chunk, k]

    def share(chunk, view):
        remote(view, view, f_s.at[chunk], f_r.at[chunk], ha=sister).start()

    def shared_view(chunk):
        level, slot, n = CHUNKS[chunk]
        owners = 8 if slot == 0 else NS if slot <= (X3 if level == 3 else X4) else 1
        return (wb3 if level == 3 else wb4).at[0, 0 : owners * n]

    def plane_start(chunk):
        level, slot, n = CHUNKS[chunk]
        column_wait(chunk)
        wb, merged = (wb3, merged3) if level == 3 else (wb4, merged4)
        first = first_block(chunk, w, s)
        for k in range(n):
            wb[pl.ds(core, 1), pl.ds(first + k, 1)] = merged(slot + k)[None, None]
        relayed = [k for ks in hops(chunk)[1].values() for k in ks]
        for k in range(len(hops(chunk)[0])):
            if k not in relayed:
                hop(chunk, k).start()
        share(chunk, piece(chunk, w if slot == 0 else s, 0))

    def plane_pass(chunk, *ks):
        for k in ks:
            view, sem = received(chunk, k)
            wait_bytes(view, sem)
            for j in hops(chunk)[1].get(k, ()):
                hop(chunk, j).start()
            share(chunk, view)

    send_borders()
    for chunk in range(5, len(CHUNKS)):
        column_start(chunk)
    plane_start(0)
    plane_start(1)
    plane_start(2)
    plane_pass(0, 0, 1)
    plane_pass(1, 0, 1)
    plane_start(3)
    plane_pass(0, 2, 3)
    plane_start(4)
    plane_pass(2, 0, 1)
    plane_pass(1, 2, 3)
    plane_pass(0, 4, 5, 6, 7)
    plane_start(5)
    plane_pass(2, 2, 3)
    plane_pass(3, 0, 1, 2)
    wait_borders()

    def wide(halo, centre, rows):
        sides = [halo[k].astype(F32).reshape(rows, 8, centre.shape[-1]) for k in range(2)]
        return jnp.concatenate([sides[0], centre.astype(F32), sides[1]], 1)

    def blocks3(a, kinds):
        return [9 * kind + 3 * a + b for b in range(3) for kind in kinds]

    def gates3(a, kinds):
        blocks = []
        for kb in blocks3(a, kinds):
            lo, hi = wb3.at[0, kb], wb3.at[1, kb]
            blocks.append(jnp.concatenate([
                lo[64:128, :], lo[0:64, :], lo[128:192, :], lo[128:192, :],
                lo[256:288, :], hi[0:32, :], lo[192:256, :], hi[32:96, :], hi[32:96, :],
            ], 0))
        return jnp.concatenate(blocks, 1)

    def cand3(a, kinds):
        zero = jnp.zeros((64, 128), BF16)
        blocks = []
        for kb in blocks3(a, kinds):
            hi = wb3.at[1, kb]
            blocks.append(jnp.concatenate([hi[160:224, :], hi[96:160, :], zero, hi[224:288, :]], 0))
        return jnp.concatenate(blocks, 1)

    def gates4(a):
        blocks = []
        for kb in range(6 * a, 6 * a + 6):
            lo, hi = wb4.at[0, kb], wb4.at[1, kb]
            blocks.append(jnp.concatenate([
                lo[32:96, :], lo[0:32, :], lo[0:32, :],
                lo[128:144, :], hi[0:48, :], lo[96:128, :], lo[96:128, :],
            ], 0))
        return jnp.concatenate(blocks, 1)

    def cand4(a):
        zero = jnp.zeros((32, 128), BF16)
        blocks = []
        for kb in range(6 * a, 6 * a + 6):
            hi = wb4.at[1, kb]
            blocks.append(jnp.concatenate([hi[80:144, :], zero, hi[48:80, :]], 0))
        return jnp.concatenate(blocks, 1)

    def conv(ref, r0, rows, c0, cols, weights):
        u = jnp.concatenate(
            [ref[r0 - 1 : r0 + rows + 1, c0 + b - 1 : c0 + b - 1 + cols, :].astype(BF16) for b in range(3)], 2
        )
        return sum(nt(u[a : a + rows].reshape(rows * cols, u.shape[2]), weights(a)) for a in range(3))

    def inputs(t):
        return xi[0].astype(F32) if t == 0 else wide(xh.at[0, :, :, t - 1], xc[0, t - 1], 6)

    def input_sums(t):
        c0, c1 = (0, 48) if t == 0 else (8, 40)
        jx[:, c0:c1, :] = inputs(t)[:, :, 0:128]
        xg[t] = conv(jx, 1, 4, 8, 32, lambda a: gates3(a, (0,)))
        xk[t] = conv(jx, 2, 2, 8, 32, lambda a: cand3(a, (0,)))

    def level3(t):
        c0, c1 = (0, 48) if t == 0 else (8, 40)
        p = s3i[0].astype(F32) if t == 0 else s3w[t - 1].astype(F32)
        j3[:, c0:c1, 0:128] = p[:, :, 0:128]
        j3[:, c0:c1, 128:192] = inputs(t)[:, :, 128:192]
        j3[:, c0:c1, 192:256] = p[:, :, 192:256]
        p = p[:, 8 - c0 : 40 - c0, :]
        sums = xg[t] + conv(j3, 1, 4, 8, 32, lambda a: gates3(a, (1, 2)))
        reset = jax.nn.sigmoid(sums[:, :256]).reshape(4, 32, 256)
        update = jax.nn.sigmoid(sums[:, 256:]).reshape(4, 32, 256)[1:3]
        gated = reset * p[1:5]
        j3[1:5, 8:40, 0:128] = gated[:, :, 0:128]
        j3[1:5, 8:40, 192:256] = gated[:, :, 192:256]
        fresh = xk[t] + conv(j3, 2, 2, 8, 32, lambda a: cand3(a, (1, 2)))
        fresh = jnp.maximum(fresh, 0.0).reshape(2, 32, 256)
        state = update * p[2:4] + (1.0 - update) * fresh
        col = lax.broadcasted_iota(jnp.int32, state.shape, 1) + (16 * w - 8)
        s3w[t, 2:4] = jnp.where((col >= 0) & (col < 16 * NW), state, 0.0).astype(BF16)
        send_3(t)

    def to_lead(t):
        return remote(pt.at[t], po.at[s], out_s.at[t], out_r, section=t)

    def lift(t):
        lifted = nt(s3w[t].reshape(192, 256), lm[...]).astype(BF16)
        lifted = jnp.dot(up[...], lifted, preferred_element_type=F32).reshape(6, 64, 128)
        for i in range(12):
            j4[i, :, 0:96] = lifted[i // 2, :, 0:96]

    def level4(t):
        border = 2 if t == LEADS - 2 else 0
        g0, g1 = 3 - border, 9 + border
        if t == 0:
            p = wide(s4h.at[0], s4c[0], 12)
        else:
            p = p4[...] if t == LEADS - 1 else s4w[t - 1].astype(F32)
        j4[:, 8:56, 96:128] = p[:, :, 96:128]
        j4[:, 8:56, 128:192] = p[:, :, 0:64]
        sums = conv(j4, g0, g1 - g0, 8, 48, gates4)
        reset = jax.nn.sigmoid(sums[:, :128]).reshape(g1 - g0, 48, 128)
        update = jax.nn.sigmoid(sums[:, 128:]).reshape(g1 - g0, 48, 128)
        gated = reset * p[g0:g1]
        j4[g0:g1, 8:56, 96:128] = gated[:, :, 96:128]
        j4[g0:g1, 8:56, 128:192] = gated[:, :, 0:64]
        c0, cols = (16, 32) if t == LEADS - 1 else (8, 48)
        rows = g1 - g0 - 2
        fresh = conv(j4, g0 + 1, rows, c0, cols, cand4)
        fresh = jnp.maximum(fresh, 0.0).reshape(rows, cols, 128)
        update, prior = update[1 : rows + 1, c0 - 8 : c0 - 8 + cols], p[g0 + 1 : g1 - 1, c0 - 8 : c0 - 8 + cols]
        state = update * prior + (1.0 - update) * fresh
        if t < LEADS - 1:
            row = lax.broadcasted_iota(jnp.int32, state.shape, 0) + (4 * h + g0 + 1 - 4)
            col = lax.broadcasted_iota(jnp.int32, state.shape, 1) + (32 * w - 8)
            inside = (row >= 0) & (row < 4 * NH) & (col >= 0) & (col < 32 * NW)
            state = jnp.where(inside, state, 0.0).astype(BF16)
            if border:
                p4[g0 + 1 : g1 - 1] = state.astype(F32)
            else:
                s4w[t, 4:8] = state
                send_4(t)
            state = state.astype(F32)[border : border + 4, 8:40]
        pt[t] = nt(ro[...], state.astype(BF16).reshape(128, 128))

        @pl.when(s == t)
        def _():
            po[t] = pt[t]

        @pl.when(s != t)
        def _():
            to_lead(t).start()

    for chunk in (0, 1):
        wait_bytes(shared_view(chunk), f_r.at[chunk])
    input_sums(0)
    plane_pass(4, 0, 1, 2)
    plane_start(6)
    plane_start(7)
    for chunk in CH3[2:]:
        wait_bytes(shared_view(chunk), f_r.at[chunk])
    level3(0)
    plane_start(8)
    plane_pass(5, 0, 1, 2, 3)
    for t in range(1, LEADS):
        input_sums(t)
    for t in range(LEADS):
        wait_bytes(view_3, n3_r.at[t])
        if t + 1 < LEADS:
            level3(t + 1)
        if t == 0:
            plane_pass(7, 0, 1, 2)
            plane_pass(5, 4, 5, 6, 7)
        lift(t)
        if t == 0:
            for chunk in CH4:
                wait_bytes(shared_view(chunk), f_r.at[chunk])
        elif t < LEADS - 1:
            wait_bytes(view_4, n4_r.at[t - 1])
        level4(t)

    wait_bytes(po.at[0:3], out_r)
    o_ref[...] = po[...]

    raw3.wait_send()
    raw4.wait_send()
    wait_bytes(view_a, xa_s)
    wait_bytes(view_s3, n3_s.at[4])
    wait_bytes(view_x0, x0_s)
    wait_bytes(view_x, xn_s)
    wait_bytes(view_s4, n4_s.at[2])
    for t in range(LEADS):
        wait_bytes(view_3, n3_s.at[t])
    for t in range(LEADS - 2):
        wait_bytes(view_4, n4_s.at[t])
    for chunk in range(len(CHUNKS)):
        level, slot, n = CHUNKS[chunk]
        s1 = s13 if level == 3 else s14
        @pl.when(alone)
        def _(s1=s1, slot=slot, n=n, chunk=chunk):
            wait_bytes(s1.at[0:3, slot : slot + n], col_s.at[chunk])
        @pl.when(jnp.logical_not(alone))
        def _(s1=s1, slot=slot, n=n, chunk=chunk):
            wait_bytes(s1.at[:, slot : slot + n], col_s.at[chunk])
        for k in range(len(hops(chunk)[0])):
            hop(chunk, k).wait_send()
        wait_bytes(shared_view(chunk), f_s.at[chunk])
    for t in range(LEADS):
        @pl.when(s != t)
        def _(t=t):
            to_lead(t).wait_send()


def local(coarse_inputs, init_level3, init_level4, weight_level3, weight_level4, lift_map, readout):
    n = len(CHUNKS)
    dma = pltpu.SemaphoreType.DMA
    fields = pl.pallas_call(
        kernel,
        out_shape=jax.ShapeDtypeStruct((4, 16, 128), F32),
        in_specs=[pl.BlockSpec(memory_space=pl.ANY)] * 7,
        out_specs=pl.BlockSpec(memory_space=pltpu.VMEM),
        scratch_shapes=[
            pltpu.VMEM((2, 16, 192), BF16),
            pltpu.VMEM((4, 32, 96), BF16),
            pltpu.VMEM((96, 192), BF16),
            pltpu.VMEM((16, 96), BF16),
            pltpu.VMEM((9, 36, 384), BF16),
            pltpu.VMEM((9, 18, 192), BF16),
            pltpu.VMEM((9, 36, 384), BF16),
            pltpu.VMEM((9, 18, 192), BF16),
            pltpu.VMEM((K3, WIN3, 128), BF16),
            pltpu.VMEM((K4, WIN4, 128), BF16),
            pltpu.VMEM((4, 1 + X3 + C3, WIN3, 128), BF16),
            pltpu.VMEM((4, 1 + X4 + C4, WIN4, 128), BF16),
            pltpu.VMEM((2, K3, H3R, 128), BF16),
            pltpu.VMEM((2, K4, H4R, 128), BF16),
            pltpu.VMEM((4, 2, 16, 192), BF16),
            pltpu.VMEM((2, 6, 48, 192), BF16),
            pltpu.VMEM((2, 3, 6, 16, 192), BF16),
            pltpu.VMEM((3, 2, 16, 192), BF16),
            pltpu.VMEM((2, 2, 3, 3, 16, 192), BF16),
            pltpu.VMEM((2, 6, 48, 256), BF16),
            pltpu.VMEM((8, 6, 32, 256), BF16),
            pltpu.VMEM((2, 12, 32, 128), BF16),
            pltpu.VMEM((2, 32, 128), BF16),
            pltpu.VMEM((2, 2, 3, 32, 128), BF16),
            pltpu.VMEM((4, 12, 48, 128), BF16),
            pltpu.VMEM((6, 48, 128), F32),
            pltpu.VMEM((6, 48, 256), F32),
            pltpu.VMEM((12, 64, 256), F32),
            pltpu.VMEM((12, 48, 128), F32),
            pltpu.VMEM((4, 128, 512), F32),
            pltpu.VMEM((4, 64, 256), F32),
            pltpu.VMEM((272, 256), F32),
            pltpu.VMEM((128, 256), BF16),
            pltpu.VMEM((16, 128), BF16),
            pltpu.VMEM((384, 192), BF16),
            pltpu.VMEM((4, 16, 128), F32),
            pltpu.VMEM((4, 16, 128), F32),
            dma((7,)), dma((2,)), dma((2,)), dma((n,)), dma((n,)),
            dma((n, NS)), dma((n, NS)), dma((n, NW)), dma((n, NW)), dma((n,)), dma((n,)),
            dma, dma, dma, dma, dma, dma, dma((5,)), dma((5,)), dma((3,)), dma((3,)), dma((4,)), dma,
        ],
        compiler_params=pltpu.CompilerParams(
            collective_id=0, has_side_effects=True, vmem_limit_bytes=64 << 20
        ),
        name="nowcast",
    )(
        coarse_inputs[0].transpose(0, 2, 3, 1),
        init_level3.transpose(1, 2, 0),
        init_level4.transpose(1, 2, 0),
        weight_level3.transpose(1, 0, 2),
        weight_level4.transpose(1, 0, 2),
        lift_map,
        readout,
    )
    return fields.reshape(1, 4, 16, 4, 32)


def solution(mesh):
    return jax.shard_map(
        local,
        mesh=mesh,
        in_specs=(
            P("section", None, None, "ha", "wa"),
            P(None, "ha", "wa"),
            P(None, "ha", "wa"),
            P("ha", None, None),
            P("ha", None, None),
            P(),
            P(),
        ),
        out_specs=P("section", None, None, "ha", "wa"),
        check_vma=False,
    )
```

```python
import jax
import jax.numpy as jnp
from jax import lax
from jax.experimental import pallas as pl
from jax.experimental.pallas import tpu as pltpu
from jax.sharding import PartitionSpec as P

MESH = pl.DeviceIdType.MESH
BF16 = jnp.bfloat16
F32 = jnp.float32

NS, NH, NW = 4, 16, 8
LEADS = 4

X3, X4 = 4, 2
C3, C4 = 3, 2
K3, K4 = 8 + NS * X3 + C3, 8 + NS * X4 + C4
H3R, H4R = 288, 144
WIN3, WIN4 = 80, 48

CHUNKS = [(3, 0, 1), (3, 1, 1), (3, 2, 1), (3, 3, 1), (3, 4, 1), (4, 0, 1), (3, 5, 3), (4, 1, 2), (4, 3, 2)]
CH3, CH4 = (0, 1, 2, 3, 4, 6), (5, 7, 8)

NEIGHBOURS = [(-1, -1), (-1, 1), (1, -1), (1, 1), (0, -1), (0, 1), (-1, 0), (1, 0)]

Z_HOPS = [(1, 1, 0), (7, -1, 0), (2, 2, 0), (6, -2, 0), (3, 1, 0), (5, -1, 0), (4, 2, 1), (4, -2, 2)]
Z_RELAY = {2: (4, 6), 3: (5, 7)}
ZD_HOPS = [(1, 1, 0), (7, -1, 0), (2, 2, 0), (6, -2, 0), (3, 3, 0), (5, -3, 0), (4, 4, 0)]
X_HOPS = [(1, 1, 0), (3, -1, 0), (2, 2, 0)]
X_RELAY = {}
XR_HOPS = [(1, 1, 0), (3, -1, 0), (2, 1, 1), (2, -1, 2)]
XR_RELAY = {0: (2,), 1: (3,)}
RELAYED = (1, 2)
Z_CHUNKS = [k for k, (level, slot, n) in enumerate(CHUNKS) if slot == 0]
X_CHUNKS = [k for k, (level, slot, n) in enumerate(CHUNKS) if 0 < slot <= (X3 if level == 3 else X4)]


def nt(a, b):
    return lax.dot_general(a, b, (((1,), (1,)), ((), ())), preferred_element_type=F32)


def kernel(
    x_ref, i3_ref, i4_ref, w3_ref, w4_ref, lm_ref, ro_ref, o_ref,
    i3v, i4v, lmv, rov, own3, own4, sis3, sis4, cw3, cw4, s13, s14, wb3, wb4,
    xa, xi, xc, xe, xh, s3i, s3w, s4c, s4e, s4h, s4w, xw, pw, jx, j3, j4, p4, xg, xk, tmp, lm, ro, up, pt, po,
    load_sem, raw_s, raw_r, col_s, col_r, plane_s, x_r, z_r, f_s, f_r,
    xa_s, xa_r, x0_s, x0_r, xn_s, xn_r, n3_s, n3_r, n4_s, n4_r, out_s, out_r,
):
    s = lax.axis_index("section")
    h = lax.axis_index("ha")
    w = lax.axis_index("wa")
    core = lax.rem(h, 2)
    y = h // 2
    sister = h + 1 - 2 * core
    half = y // 4

    def remote(src, dst, send, recv, **where):
        return pltpu.make_async_remote_copy(
            src_ref=src, dst_ref=dst, send_sem=send, recv_sem=recv, device_id=where, device_id_type=MESH
        )

    def wait_bytes(view, sem):
        pltpu.make_async_copy(view, view, sem).wait()

    for ref, n in ((xi, 1), (xc, 1), (xh, 1), (s3i, 1), (s4c, 1), (s4h, 1)):
        ref[0:n] = jnp.zeros((n,) + ref.shape[1:], BF16)
    for ref, n, rows in ((s3w, 4, 2), (s4w, 3, 4)):
        for first in (0, 2 * rows):
            ref[0:n, first : first + rows] = jnp.zeros((n, rows) + ref.shape[2:], BF16)
    loads = [
        pltpu.make_async_copy(src, dst, load_sem.at[k])
        for k, (src, dst) in enumerate([
            (w3_ref, own3), (w4_ref, own4), (x_ref.at[s], xa.at[s]),
            (i3_ref, i3v), (i4_ref, i4v), (lm_ref, lmv), (ro_ref, rov),
        ])
    ]
    for load in loads:
        load.start()

    def shifted(rows, count, offset):
        r = lax.broadcasted_iota(jnp.int32, (rows, count), 0)
        c = lax.broadcasted_iota(jnp.int32, (rows, count), 1)
        return jnp.where(r == c + offset, 1.0, 0.0).astype(BF16)

    low = lax.broadcasted_iota(jnp.int32, (1, 128), 1) < 64

    def place3(shard, which, add):
        put = shifted(WIN3, 36, 8 * lax.rem(y, 2) + 36 * which)
        for tap in range(9):
            rows = jnp.dot(put, shard[tap], preferred_element_type=F32)
            v1, v2 = rows[:, 128:256], rows[:, 256:384]
            for k, v in enumerate((rows[:, :128], jnp.where(low, v2, v1), jnp.where(low, v1, v2))):
                v = v.astype(BF16)
                cw3[9 * k + tap] = cw3[9 * k + tap] + v if add else v

    def place4(shard, which, add):
        put = shifted(WIN4, 18, 4 * lax.rem(y, 4) + 18 * which)
        for tap in range(9):
            rows = jnp.dot(put, shard[tap], preferred_element_type=F32)
            tmp[0:WIN4, 0:64] = rows[:, 128:192]
            tmp[0:WIN4, 64:128] = jnp.zeros((WIN4, 64), F32)
            for k, v in enumerate((rows[:, :128], tmp[0:WIN4, 0:128])):
                v = v.astype(BF16)
                cw4[2 * tap + k] = cw4[2 * tap + k] + v if add else v

    barrier = pltpu.get_barrier_semaphore()
    alone = (half == core) & (lax.rem(y, 2) == core)
    count = 0
    greet = [
        {"ha": lax.rem(h + dy, NH), "wa": lax.rem(w + dx, NW)} for dy in (1, NH - 1) for dx in (1, NW - 1)
    ]
    greet += [{"wa": lax.rem(w + d, NW)} for d in (4, 3, 5, 2, 6, 1, 7)]
    greet += [{"section": lax.rem(s + d, NS)} for d in (2, 1, 3)]
    greet += [{"ha": lax.rem(h + 2 * core + NH - 1, NH)}, {"ha": sister}]
    for where in greet:
        pl.semaphore_signal(barrier, inc=1, device_id=where, device_id_type=MESH)
    for i in range(4):
        source = 2 * (4 * core + i) + lax.rem(y, 2)
        @pl.when(source != h)
        def _(source=source):
            pl.semaphore_signal(barrier, inc=1, device_id={"ha": source}, device_id_type=MESH)
    for ref in (j3, j4, xw):
        ref[...] = jnp.zeros_like(ref)
    loads[0].wait()
    place3(own3, core, False)
    loads[1].wait()
    place4(own4, core, False)
    pl.semaphore_wait(barrier, len(greet) + 4 - alone.astype(jnp.int32))

    raw3 = remote(w3_ref, sis3, raw_s.at[0], raw_r.at[0], ha=sister)
    raw4 = remote(w4_ref, sis4, raw_s.at[1], raw_r.at[1], ha=sister)
    raw3.start()
    raw4.start()
    for d in range(1, NS):
        m = lax.rem(s + d, NS)
        remote(x_ref.at[m], xa.at[s], xa_s, xa_r, section=m).start()

    raw3.wait_recv()
    place3(sis3, 1 - core, True)

    def first_block(chunk, z, x):
        level, slot, n = CHUNKS[chunk]
        per = X3 if level == 3 else X4
        if slot == 0:
            return z
        return 8 + x * per + slot - 1 if slot <= per else 8 + (NS - 1) * per + slot - 1

    def column_parts(chunk):
        level, slot, n = CHUNKS[chunk]
        cw, s1 = (cw3, s13) if level == 3 else (cw4, s14)
        first = first_block(chunk, w, s)
        return cw.at[pl.ds(first, n)], s1.at[lax.rem(y, 4), slot : slot + n], s1.at[:, slot : slot + n]

    def column_start(chunk):
        src, dst, _ = column_parts(chunk)
        for i in range(4):
            target = 2 * (2 * i + core) + half
            @pl.when(target != h)
            def _(target=target):
                remote(src, dst, col_s.at[CHUNKS[chunk][0] - 3], col_r.at[chunk], ha=target).start()
        @pl.when(alone)
        def _():
            pltpu.make_async_copy(src, dst, col_r.at[chunk]).start()

    def column_wait(chunk):
        wait_bytes(column_parts(chunk)[2], col_r.at[chunk])

    for chunk in range(5):
        column_start(chunk)
    raw4.wait_recv()
    place4(sis4, 1 - core, True)
    for load in loads[2:]:
        load.wait()
    tmp[...] = jnp.zeros_like(tmp)
    tmp[0:32, 0:192] = i3v[...].reshape(32, 192).astype(F32)
    tmp[32:128, 0:192] = lmv[...].astype(F32)
    tmp[128:256, 0:96] = i4v[...].reshape(128, 96).astype(F32)
    tmp[256:272, 0:96] = rov[...].astype(F32)
    first = pltpu.roll(tmp[0:128, 0:128], 64, 1).astype(BF16)
    second = pltpu.roll(tmp[0:128, 128:256], 64, 1).astype(BF16)
    tmp[0:32, 0:128] = pltpu.roll(tmp[0:32, 0:128], 64, 1)
    tmp[0:32, 128:256] = pltpu.roll(tmp[0:32, 128:256], 64, 1)
    s3i[0, 2:4, 16:32, :] = tmp[0:32, 0:256].reshape(2, 16, 256).astype(BF16)
    lm[0:96, 0:128] = first[32:128]
    lm[0:96, 128:256] = second[32:128]
    lm[96:128, :] = jnp.zeros((32, 256), BF16)
    third = pltpu.roll(tmp[128:272, 0:128], 96, 1)
    s4c[0, 4:8] = third[0:128].reshape(4, 32, 128).astype(BF16)
    for k in range(2):
        s4e[k] = third[0:128].reshape(4, 32, 128)[:, 24 * k : 24 * k + 8, :].reshape(32, 128).astype(BF16)
    ro[...] = third[128:144].astype(BF16)
    fine = lax.broadcasted_iota(jnp.int32, (384, 192), 0)
    cell = lax.broadcasted_iota(jnp.int32, (384, 192), 1)
    up[...] = jnp.where((fine // 64) * 32 + lax.rem(fine, 64) // 2 == cell, 1.0, 0.0).astype(BF16)

    def wide(halo, centre, rows):
        sides = [halo[k].astype(F32).reshape(rows, 8, centre.shape[-1]) for k in range(2)]
        return jnp.concatenate([sides[0], centre.astype(F32), sides[1]], 1)

    def away(dy, dx):
        oy = 1 - (h + NH - 1) // NH if dy < 0 else (h + 1) // NH if dy > 0 else 0
        ox = 1 - (w + NW - 1) // NW if dx < 0 else (w + 1) // NW if dx > 0 else 0
        return oy + ox - oy * ox

    def neighbour(dy, dx):
        where = {}
        if dy:
            where["ha"] = lax.rem(h + dy + NH, NH)
        if dx:
            where["wa"] = lax.rem(w + dx + NW, NW)
        return where

    def send_rows(ref, t, steps, rows, send, recv):
        for dy in (-1, 1):
            to = t + steps * away(dy, 0)
            remote(
                ref.at[t, rows : 2 * rows], ref.at[to, rows * (1 - dy) : rows * (2 - dy)], send, recv, **neighbour(dy, 0)
            ).start()

    def send_3(t):
        send_rows(s3w, t, 4, 2, n3_s.at[0], n3_r.at[t])

    def send_4(t):
        send_rows(s4w, t, 3, 4, n4_s.at[1], n4_r.at[t])

    view_3 = s3w.at[0, 0:4]
    view_4 = s4w.at[0, 0:8]
    view_a = xa.at[0:3]
    view_s3 = s3i.at[0:2, 0:4, 0:32]
    view_x0 = xi.at[0:2, 0:4, 0:32]
    view_x = xc.at[0:2, 0:3, 0:5]
    view_s4 = s4c.at[0:2, 0:7]

    def send_whole(src, dst, send, recv):
        for dy, dx in NEIGHBOURS:
            remote(
                src, dst.at[away(dy, dx), 2 - 2 * dy : 4 - 2 * dy, 16 - 16 * dx : 32 - 16 * dx], send, recv,
                **neighbour(dy, dx),
            ).start()

    def send_borders():
        send_whole(s3i.at[0, 2:4, 16:32], s3i, n3_s.at[1], n3_r.at[4])
        wait_bytes(view_a, xa_r)
        xi[0, 2:4, 16:32, :] = xa[0]
        send_whole(xa.at[0], xi, x0_s, x0_r)
        for lead in range(1, LEADS):
            xc[0, lead - 1, 2:4] = xa[lead]
            tile = xa[lead].astype(F32)
            for k in range(2):
                xe[lead - 1, k] = tile[:, 8 * k : 8 * k + 8, :].reshape(16, 192).astype(BF16)
        for dy, dx in NEIGHBOURS:
            to = away(dy, dx)
            if dx == 0:
                one = xa.at[1:4], xc.at[to, :, 2 - 2 * dy : 4 - 2 * dy]
                two = s4c.at[0, 4:8], s4c.at[to, 4 - 4 * dy : 8 - 4 * dy]
            else:
                one = xe.at[:, (dx + 1) // 2], xh.at[to, (1 - dx) // 2, 1 - dy]
                two = s4e.at[(dx + 1) // 2], s4h.at[to, (1 - dx) // 2, 1 - dy]
            remote(*one, xn_s, xn_r, **neighbour(dy, dx)).start()
            remote(*two, n4_s.at[0], n4_r.at[0], **neighbour(dy, dx)).start()

    def wait_borders():
        wait_bytes(view_s3, n3_r.at[4])
        wait_bytes(view_x0, x0_r)
        wait_bytes(view_x, xn_r)
        wait_bytes(view_s4, n4_r.at[0])
        s4w[0] = wide(s4h.at[0], s4c[0], 12).astype(BF16)
        pw[...] = s3i[0].astype(F32)
        xw[0] = xi[0].astype(F32)
        for lead in range(1, LEADS):
            xw[lead, :, 8:40, :] = wide(xh.at[0, :, :, lead - 1], xc[0, lead - 1], 6)

    def merged3(slot):
        out = []
        for g in (0, 2):
            a, b = s13[g, slot], s13[g + 1, slot]
            out += [a[0:64], a[64:80] + b[0:16], b[16:80]]
        return jnp.concatenate(out, 0)

    def merged4(slot):
        a, b, c, d = (s14[i, slot] for i in range(4))
        return jnp.concatenate(
            [a[0:32], a[32:48] + b[0:16], b[16:32], b[32:48] + c[0:16], c[16:32], c[32:48] + d[0:16], d[16:48]], 0
        )

    def hops(chunk):
        level, slot, n = CHUNKS[chunk]
        if slot == 0:
            return (Z_HOPS, Z_RELAY) if level == 3 else (ZD_HOPS, {})
        if slot <= (X3 if level == 3 else X4):
            return (XR_HOPS, XR_RELAY) if chunk in RELAYED else (X_HOPS, X_RELAY)
        return [], {}

    def piece(chunk, owner, part):
        level, slot, n = CHUNKS[chunk]
        wb, rows, cut = (wb3, H3R, 144) if level == 3 else (wb4, H4R, 80)
        lo, hi = ((0, rows), (0, cut), (cut, rows))[part]
        return wb.at[core, pl.ds(first_block(chunk, owner, owner), n), lo:hi]

    def along(chunk):
        if chunk in Z_CHUNKS:
            return w, NW, "wa", z_r.at[Z_CHUNKS.index(chunk)]
        return s, NS, "section", x_r.at[X_CHUNKS.index(chunk)]

    def hop(chunk, k):
        d, step, part = hops(chunk)[0][k]
        me, size, axis, recv = along(chunk)
        view = piece(chunk, lax.rem(me + step - d + 2 * size, size), part)
        to = lax.rem(me + step + size, size)
        return remote(view, view, plane_s.at[CHUNKS[chunk][0] - 3], recv.at[k], **{axis: to})

    def received(chunk, k):
        d, step, part = hops(chunk)[0][k]
        me, size, axis, recv = along(chunk)
        return piece(chunk, lax.rem(me - d + size, size), part), recv.at[k]

    def share(chunk, view):
        remote(view, view, f_s.at[CHUNKS[chunk][0] - 3], f_r.at[chunk], ha=sister).start()

    def shared_view(chunk):
        level, slot, n = CHUNKS[chunk]
        owners = 8 if slot == 0 else NS if slot <= (X3 if level == 3 else X4) else 1
        return (wb3 if level == 3 else wb4).at[0, 0 : owners * n]

    def plane_start(chunk):
        level, slot, n = CHUNKS[chunk]
        column_wait(chunk)
        wb, merged = (wb3, merged3) if level == 3 else (wb4, merged4)
        first = first_block(chunk, w, s)
        for k in range(n):
            wb[pl.ds(core, 1), pl.ds(first + k, 1)] = merged(slot + k)[None, None]
        relayed = [k for ks in hops(chunk)[1].values() for k in ks]
        for k in range(len(hops(chunk)[0])):
            if k not in relayed:
                hop(chunk, k).start()
        share(chunk, piece(chunk, w if slot == 0 else s, 0))

    def plane_pass(chunk, *ks):
        for k in ks:
            view, sem = received(chunk, k)
            wait_bytes(view, sem)
            for j in hops(chunk)[1].get(k, ()):
                hop(chunk, j).start()
            share(chunk, view)

    send_borders()
    for chunk in range(5, len(CHUNKS)):
        column_start(chunk)
    plane_start(0)
    plane_start(1)
    plane_start(2)
    plane_pass(0, 0, 1)
    plane_pass(1, 0, 1)
    plane_start(3)
    plane_pass(0, 2, 3)
    plane_start(4)
    plane_pass(2, 0, 1)
    plane_pass(1, 2, 3)
    plane_pass(0, 4, 5, 6, 7)
    plane_start(5)
    plane_pass(2, 2, 3)
    plane_pass(3, 0, 1, 2)
    wait_borders()

    def blocks3(a, kinds):
        return [9 * kind + 3 * a + b for b in range(3) for kind in kinds]

    def gates3(a, kinds):
        blocks = []
        for kb in blocks3(a, kinds):
            lo, hi = wb3.at[0, kb], wb3.at[1, kb]
            blocks.append(jnp.concatenate([
                lo[64:128, :], lo[0:64, :], lo[128:192, :], lo[128:192, :],
                lo[256:288, :], hi[0:32, :], lo[192:256, :], hi[32:96, :], hi[32:96, :],
            ], 0))
        return jnp.concatenate(blocks, 1)

    def cand3(a, kinds):
        zero = jnp.zeros((64, 128), BF16)
        blocks = []
        for kb in blocks3(a, kinds):
            hi = wb3.at[1, kb]
            blocks.append(jnp.concatenate([hi[160:224, :], hi[96:160, :], zero, hi[224:288, :]], 0))
        return jnp.concatenate(blocks, 1)

    def gates4(a):
        blocks = []
        for kb in range(6 * a, 6 * a + 6):
            lo, hi = wb4.at[0, kb], wb4.at[1, kb]
            blocks.append(jnp.concatenate([
                lo[32:96, :], lo[0:32, :], lo[0:32, :],
                lo[128:144, :], hi[0:48, :], lo[96:128, :], lo[96:128, :],
            ], 0))
        return jnp.concatenate(blocks, 1)

    def cand4(a):
        zero = jnp.zeros((32, 128), BF16)
        blocks = []
        for kb in range(6 * a, 6 * a + 6):
            hi = wb4.at[1, kb]
            blocks.append(jnp.concatenate([hi[80:144, :], zero, hi[48:80, :]], 0))
        return jnp.concatenate(blocks, 1)

    def conv(ref, r0, rows, c0, cols, weights):
        u = jnp.concatenate(
            [ref[r0 - 1 : r0 + rows + 1, c0 + b - 1 : c0 + b - 1 + cols, :].astype(BF16) for b in range(3)], 2
        )
        return sum(nt(u[a : a + rows].reshape(rows * cols, u.shape[2]), weights(a)) for a in range(3))

    def input_sums(t):
        jx[...] = xw[t, :, :, 0:128]
        xg[t] = conv(jx, 1, 4, 8, 32, lambda a: gates3(a, (0,)))
        xk[t] = conv(jx, 2, 2, 8, 32, lambda a: cand3(a, (0,)))

    def level3(t):
        p = pw[...]
        j3[:, :, 0:128] = p[:, :, 0:128]
        j3[:, :, 128:192] = xw[t, :, :, 128:192]
        j3[:, :, 192:256] = p[:, :, 192:256]
        p = p[:, 8:40, :]
        sums = xg[t] + conv(j3, 1, 4, 8, 32, lambda a: gates3(a, (1, 2)))
        reset = jax.nn.sigmoid(sums[:, :256]).reshape(4, 32, 256)
        update = jax.nn.sigmoid(sums[:, 256:]).reshape(4, 32, 256)[1:3]
        gated = reset * p[1:5]
        j3[1:5, 8:40, 0:128] = gated[:, :, 0:128]
        j3[1:5, 8:40, 192:256] = gated[:, :, 192:256]
        fresh = xk[t] + conv(j3, 2, 2, 8, 32, lambda a: cand3(a, (1, 2)))
        fresh = jnp.maximum(fresh, 0.0).reshape(2, 32, 256)
        state = update * p[2:4] + (1.0 - update) * fresh
        col = lax.broadcasted_iota(jnp.int32, state.shape, 1) + (16 * w - 8)
        s3w[t, 2:4] = jnp.where((col >= 0) & (col < 16 * NW), state, 0.0).astype(BF16)
        send_3(t)

    def to_lead(t):
        return remote(pt.at[t], po.at[s], out_s, out_r, section=t)

    def lift(t):
        lifted = nt(s3w[t].reshape(192, 256), lm[...]).astype(BF16)
        lifted = jnp.dot(up[...], lifted, preferred_element_type=F32).reshape(6, 64, 128)
        for i in range(12):
            j4[i, :, 0:96] = lifted[i // 2, :, 0:96]

    def level4(t, border=0, last=False):
        g0, g1 = 3 - border, 9 + border
        p = p4[...] if last else s4w[t].astype(F32)
        j4[:, 8:56, 96:128] = p[:, :, 96:128]
        j4[:, 8:56, 128:192] = p[:, :, 0:64]
        sums = conv(j4, g0, g1 - g0, 8, 48, gates4)
        reset = jax.nn.sigmoid(sums[:, :128]).reshape(g1 - g0, 48, 128)
        update = jax.nn.sigmoid(sums[:, 128:]).reshape(g1 - g0, 48, 128)
        gated = reset * p[g0:g1]
        j4[g0:g1, 8:56, 96:128] = gated[:, :, 96:128]
        j4[g0:g1, 8:56, 128:192] = gated[:, :, 0:64]
        c0, cols = (16, 32) if last else (8, 48)
        rows = g1 - g0 - 2
        fresh = conv(j4, g0 + 1, rows, c0, cols, cand4)
        fresh = jnp.maximum(fresh, 0.0).reshape(rows, cols, 128)
        update, prior = update[1 : rows + 1, c0 - 8 : c0 - 8 + cols], p[g0 + 1 : g1 - 1, c0 - 8 : c0 - 8 + cols]
        state = update * prior + (1.0 - update) * fresh
        if not last:
            row = lax.broadcasted_iota(jnp.int32, state.shape, 0) + (4 * h + g0 + 1 - 4)
            col = lax.broadcasted_iota(jnp.int32, state.shape, 1) + (32 * w - 8)
            inside = (row >= 0) & (row < 4 * NH) & (col >= 0) & (col < 32 * NW)
            state = jnp.where(inside, state, 0.0).astype(BF16)
            if border:
                p4[g0 + 1 : g1 - 1] = state.astype(F32)
            else:
                s4w[t + 1, 4:8] = state
                send_4(t + 1)
            state = state.astype(F32)[border : border + 4, 8:40]
        pt[t] = nt(ro[...], state.astype(BF16).reshape(128, 128))

        @pl.when(s == t)
        def _():
            po[t] = pt[t]

        @pl.when(s != t)
        def _():
            to_lead(t).start()

    for chunk in (0, 1):
        wait_bytes(shared_view(chunk), f_r.at[chunk])
    input_sums(0)
    plane_pass(4, 0, 1, 2)
    plane_start(6)
    plane_start(7)
    for chunk in CH3[2:]:
        wait_bytes(shared_view(chunk), f_r.at[chunk])

    @pl.loop(0, LEADS)
    def _(t):
        @pl.when(t > 0)
        def _():
            wait_bytes(view_3, n3_r.at[t - 1])
            pw[:, 8:40, :] = s3w[t - 1].astype(F32)

        level3(t)

        @pl.when(t == 0)
        def _():
            plane_start(8)
            pl.loop(1, LEADS)(input_sums)
            plane_pass(5, 0, 1, 2, 3, 4, 5, 6)
            plane_pass(7, 0, 1, 2)

        @pl.when(t > 0)
        def _():
            lift(t - 1)

        @pl.when(t == 1)
        def _():
            for chunk in CH4:
                wait_bytes(shared_view(chunk), f_r.at[chunk])

        @pl.when(t > 1)
        def _():
            wait_bytes(view_4, n4_r.at[t - 1])

        @pl.when((t > 0) & (t < LEADS - 1))
        def _():
            level4(t - 1)

        @pl.when(t == LEADS - 1)
        def _():
            level4(t - 1, border=2)

    wait_bytes(view_3, n3_r.at[LEADS - 1])
    lift(LEADS - 1)
    level4(LEADS - 1, last=True)

    wait_bytes(po.at[0:3], out_r)
    o_ref[...] = po[...]

    raw3.wait_send()
    raw4.wait_send()
    wait_bytes(view_a, xa_s)
    wait_bytes(view_s3, n3_s.at[1])
    wait_bytes(view_x0, x0_s)
    wait_bytes(view_x, xn_s)
    wait_bytes(view_s4, n4_s.at[0])
    wait_bytes(s3w.at[0:4, 0:4], n3_s.at[0])
    wait_bytes(s4w.at[0:2, 0:8], n4_s.at[1])
    for k, (wb, s1, per) in enumerate(((wb3, s13, X3), (wb4, s14, X4))):
        wait_bytes(wb.at[0, 0 : 7 + 3 * per], plane_s.at[k])
        wait_bytes(wb.at[0], f_s.at[k])
        @pl.when(alone)
        def _(s1=s1, k=k):
            wait_bytes(s1.at[0:3], col_s.at[k])
        @pl.when(jnp.logical_not(alone))
        def _(s1=s1, k=k):
            wait_bytes(s1, col_s.at[k])
    wait_bytes(pt.at[0:3], out_s)


def local(coarse_inputs, init_level3, init_level4, weight_level3, weight_level4, lift_map, readout):
    n = len(CHUNKS)
    dma = pltpu.SemaphoreType.DMA
    fields = pl.pallas_call(
        kernel,
        out_shape=jax.ShapeDtypeStruct((4, 16, 128), F32),
        in_specs=[pl.BlockSpec(memory_space=pl.ANY)] * 7,
        out_specs=pl.BlockSpec(memory_space=pltpu.VMEM),
        scratch_shapes=[
            pltpu.VMEM((2, 16, 192), BF16),
            pltpu.VMEM((4, 32, 96), BF16),
            pltpu.VMEM((96, 192), BF16),
            pltpu.VMEM((16, 96), BF16),
            pltpu.VMEM((9, 36, 384), BF16),
            pltpu.VMEM((9, 18, 192), BF16),
            pltpu.VMEM((9, 36, 384), BF16),
            pltpu.VMEM((9, 18, 192), BF16),
            pltpu.VMEM((K3, WIN3, 128), BF16),
            pltpu.VMEM((K4, WIN4, 128), BF16),
            pltpu.VMEM((4, 1 + X3 + C3, WIN3, 128), BF16),
            pltpu.VMEM((4, 1 + X4 + C4, WIN4, 128), BF16),
            pltpu.VMEM((2, K3, H3R, 128), BF16),
            pltpu.VMEM((2, K4, H4R, 128), BF16),
            pltpu.VMEM((4, 2, 16, 192), BF16),
            pltpu.VMEM((2, 6, 48, 192), BF16),
            pltpu.VMEM((2, 3, 6, 16, 192), BF16),
            pltpu.VMEM((3, 2, 16, 192), BF16),
            pltpu.VMEM((2, 2, 3, 3, 16, 192), BF16),
            pltpu.VMEM((2, 6, 48, 256), BF16),
            pltpu.VMEM((8, 6, 32, 256), BF16),
            pltpu.VMEM((2, 12, 32, 128), BF16),
            pltpu.VMEM((2, 32, 128), BF16),
            pltpu.VMEM((2, 2, 3, 32, 128), BF16),
            pltpu.VMEM((6, 12, 48, 128), BF16),
            pltpu.VMEM((4, 6, 48, 192), F32),
            pltpu.VMEM((6, 48, 256), F32),
            pltpu.VMEM((6, 48, 128), F32),
            pltpu.VMEM((6, 48, 256), F32),
            pltpu.VMEM((12, 64, 256), F32),
            pltpu.VMEM((12, 48, 128), F32),
            pltpu.VMEM((4, 128, 512), F32),
            pltpu.VMEM((4, 64, 256), F32),
            pltpu.VMEM((272, 256), F32),
            pltpu.VMEM((128, 256), BF16),
            pltpu.VMEM((16, 128), BF16),
            pltpu.VMEM((384, 192), BF16),
            pltpu.VMEM((4, 16, 128), F32),
            pltpu.VMEM((4, 16, 128), F32),
            dma((7,)), dma((2,)), dma((2,)), dma((2,)), dma((n,)),
            dma((2,)), dma((len(X_CHUNKS), NS)), dma((len(Z_CHUNKS), NW)), dma((2,)), dma((n,)),
            dma, dma, dma, dma, dma, dma, dma((2,)), dma((5,)), dma((2,)), dma((3,)), dma, dma,
        ],
        compiler_params=pltpu.CompilerParams(
            collective_id=0, has_side_effects=True, vmem_limit_bytes=64 << 20
        ),
        name="nowcast",
    )(
        coarse_inputs[0].transpose(0, 2, 3, 1),
        init_level3.transpose(1, 2, 0),
        init_level4.transpose(1, 2, 0),
        weight_level3.transpose(1, 0, 2),
        weight_level4.transpose(1, 0, 2),
        lift_map,
        readout,
    )
    return fields.reshape(1, 4, 16, 4, 32)


def solution(mesh):
    return jax.shard_map(
        local,
        mesh=mesh,
        in_specs=(
            P("section", None, None, "ha", "wa"),
            P(None, "ha", "wa"),
            P(None, "ha", "wa"),
            P("ha", None, None),
            P("ha", None, None),
            P(),
            P(),
        ),
        out_specs=P("section", None, None, "ha", "wa"),
        check_vma=False,
    )
```

```python
import jax
import jax.numpy as jnp
from jax import lax
from jax.experimental import pallas as pl
from jax.experimental.pallas import tpu as pltpu
from jax.sharding import PartitionSpec as P

MESH = pl.DeviceIdType.MESH
BF16 = jnp.bfloat16
F32 = jnp.float32

NS, NH, NW = 4, 16, 8
LEADS = 4

X3, X4 = 4, 2
C3, C4 = 3, 2
K3, K4 = 8 + NS * X3 + C3, 8 + NS * X4 + C4
H3R, H4R = 288, 144
WIN3, WIN4 = 80, 48

CHUNKS = [(3, 0, 1), (3, 1, 1), (3, 2, 1), (3, 3, 1), (3, 4, 1), (4, 0, 1), (3, 5, 3), (4, 1, 2), (4, 3, 2)]
CH3, CH4 = (0, 1, 2, 3, 4, 6), (5, 7, 8)

NEIGHBOURS = [(-1, -1), (-1, 1), (1, -1), (1, 1), (0, -1), (0, 1), (-1, 0), (1, 0)]

Z_HOPS = [(1, 1, 0), (7, -1, 0), (2, 2, 0), (6, -2, 0), (3, 1, 0), (5, -1, 0), (4, 2, 1), (4, -2, 2)]
Z_RELAY = {2: (4, 6), 3: (5, 7)}
ZD_HOPS = [(1, 1, 0), (7, -1, 0), (2, 2, 0), (6, -2, 0), (3, 3, 0), (5, -3, 0), (4, 4, 0)]
X_HOPS = [(1, 1, 0), (3, -1, 0), (2, 2, 0)]
X_RELAY = {}
XR_HOPS = [(1, 1, 0), (3, -1, 0), (2, 1, 1), (2, -1, 2)]
XR_RELAY = {0: (2,), 1: (3,)}
RELAYED = (1, 2)
Z_CHUNKS = [k for k, (level, slot, n) in enumerate(CHUNKS) if slot == 0]
X_CHUNKS = [k for k, (level, slot, n) in enumerate(CHUNKS) if 0 < slot <= (X3 if level == 3 else X4)]


def nt(a, b):
    return lax.dot_general(a, b, (((1,), (1,)), ((), ())), preferred_element_type=F32)


def kernel(
    x_ref, i3_ref, i4_ref, w3_ref, w4_ref, lm_ref, ro_ref, o_ref,
    i3v, i4v, lmv, rov, own3, own4, sis3, sis4, cw3, cw4, early, s1e, s13, s14, wb3, wb4,
    xa, xi, xc, xe, xh, s3i, s3w, s4c, s4e, s4h, s4w, xw, pw, jx, j3, j4, p4, xg, xk, tmp, lm, ro, up, pt, po,
    load_sem, raw_s, raw_r, col_s, col_r, plane_s, x_r, z_r, f_s, f_r,
    xa_s, xa_r, x0_s, x0_r, xn_s, xn_r, n3_s, n3_r, n4_s, n4_r, out_s, out_r,
):
    s = lax.axis_index("section")
    h = lax.axis_index("ha")
    w = lax.axis_index("wa")
    core = lax.rem(h, 2)
    y = h // 2
    sister = h + 1 - 2 * core
    half = y // 4

    def remote(src, dst, send, recv, **where):
        return pltpu.make_async_remote_copy(
            src_ref=src, dst_ref=dst, send_sem=send, recv_sem=recv, device_id=where, device_id_type=MESH
        )

    def wait_bytes(view, sem):
        pltpu.make_async_copy(view, view, sem).wait()

    for ref, n in ((xi, 1), (xc, 1), (xh, 1), (s3i, 1), (s4c, 1), (s4h, 1)):
        ref[0:n] = jnp.zeros((n,) + ref.shape[1:], BF16)
    for ref, n, rows in ((s3w, 4, 2), (s4w, 3, 4)):
        for first in (0, 2 * rows):
            ref[0:n, first : first + rows] = jnp.zeros((n, rows) + ref.shape[2:], BF16)
    loads = [
        pltpu.make_async_copy(src, dst, load_sem.at[k])
        for k, (src, dst) in enumerate([
            (w3_ref, own3), (w4_ref, own4), (x_ref.at[s], xa.at[s]),
            (i3_ref, i3v), (i4_ref, i4v), (lm_ref, lmv), (ro_ref, rov),
        ])
    ]
    for load in loads:
        load.start()

    def shifted(rows, count, offset):
        r = lax.broadcasted_iota(jnp.int32, (rows, count), 0)
        c = lax.broadcasted_iota(jnp.int32, (rows, count), 1)
        return jnp.where(r == c + offset, 1.0, 0.0).astype(BF16)

    low = lax.broadcasted_iota(jnp.int32, (1, 128), 1) < 64

    def place3(shard, which, add):
        put = shifted(WIN3, 36, 8 * lax.rem(y, 2) + 36 * which)
        for tap in range(9):
            rows = jnp.dot(put, shard[tap], preferred_element_type=F32)
            v1, v2 = rows[:, 128:256], rows[:, 256:384]
            for k, v in enumerate((rows[:, :128], jnp.where(low, v2, v1), jnp.where(low, v1, v2))):
                v = v.astype(BF16)
                cw3[9 * k + tap] = cw3[9 * k + tap] + v if add else v

    def place4(shard, which, add):
        put = shifted(WIN4, 18, 4 * lax.rem(y, 4) + 18 * which)
        for tap in range(9):
            rows = jnp.dot(put, shard[tap], preferred_element_type=F32)
            tmp[0:WIN4, 0:64] = rows[:, 128:192]
            tmp[0:WIN4, 64:128] = jnp.zeros((WIN4, 64), F32)
            for k, v in enumerate((rows[:, :128], tmp[0:WIN4, 0:128])):
                v = v.astype(BF16)
                cw4[2 * tap + k] = cw4[2 * tap + k] + v if add else v

    barrier = pltpu.get_barrier_semaphore()
    alone = (half == core) & (lax.rem(y, 2) == core)
    count = 0
    greet = [
        {"ha": lax.rem(h + dy, NH), "wa": lax.rem(w + dx, NW)} for dy in (1, NH - 1) for dx in (1, NW - 1)
    ]
    greet += [{"wa": lax.rem(w + d, NW)} for d in (4, 3, 5, 2, 6, 1, 7)]
    greet += [{"section": lax.rem(s + d, NS)} for d in (2, 1, 3)]
    greet += [{"ha": lax.rem(h + 2 * core + NH - 1, NH)}, {"ha": sister}]
    for where in greet:
        pl.semaphore_signal(barrier, inc=1, device_id=where, device_id_type=MESH)
    for i in range(8):
        source = 8 * core + i
        @pl.when(source != h)
        def _(source=source):
            pl.semaphore_signal(barrier, inc=1, device_id={"ha": source}, device_id_type=MESH)
    for ref in (j3, j4, xw):
        ref[...] = jnp.zeros_like(ref)
    loads[0].wait()
    place3(own3, core, False)
    for j, block in enumerate((w, 8 + X3 * s)):
        early[j] = cw3[block, pl.ds(pl.multiple_of(32 * core, 16), 48), :]
    loads[1].wait()
    place4(own4, core, False)
    pl.semaphore_wait(barrier, len(greet) + 8 - (half == core).astype(jnp.int32))

    raw3 = remote(w3_ref, sis3, raw_s.at[0], raw_r.at[0], ha=sister)
    raw4 = remote(w4_ref, sis4, raw_s.at[1], raw_r.at[1], ha=sister)
    raw3.start()
    raw4.start()

    for j in range(2):
        landing = s1e.at[j, lax.rem(h, 8)]
        for i in range(8):
            target = 2 * i + half
            @pl.when(target != h)
            def _(target=target, j=j, landing=landing):
                remote(early.at[j], landing, col_s.at[2], col_r.at[j], ha=target).start()
        @pl.when(half == core)
        def _(j=j, landing=landing):
            pltpu.make_async_copy(early.at[j], landing, col_r.at[j]).start()
    for d in range(1, NS):
        m = lax.rem(s + d, NS)
        remote(x_ref.at[m], xa.at[s], xa_s, xa_r, section=m).start()

    raw3.wait_recv()
    place3(sis3, 1 - core, True)

    def first_block(chunk, z, x):
        level, slot, n = CHUNKS[chunk]
        per = X3 if level == 3 else X4
        if slot == 0:
            return z
        return 8 + x * per + slot - 1 if slot <= per else 8 + (NS - 1) * per + slot - 1

    def column_parts(chunk):
        level, slot, n = CHUNKS[chunk]
        cw, s1 = (cw3, s13) if level == 3 else (cw4, s14)
        first = first_block(chunk, w, s)
        return cw.at[pl.ds(first, n)], s1.at[lax.rem(y, 4), slot : slot + n], s1.at[:, slot : slot + n]

    def column_start(chunk):
        src, dst, _ = column_parts(chunk)
        for i in range(4):
            target = 2 * (2 * i + core) + half
            @pl.when(target != h)
            def _(target=target):
                remote(src, dst, col_s.at[CHUNKS[chunk][0] - 3], col_r.at[chunk], ha=target).start()
        @pl.when(alone)
        def _():
            pltpu.make_async_copy(src, dst, col_r.at[chunk]).start()

    def column_wait(chunk):
        if chunk < 2:
            wait_bytes(s1e.at[chunk], col_r.at[chunk])
            return
        wait_bytes(column_parts(chunk)[2], col_r.at[chunk])

    for chunk in range(2, 5):
        column_start(chunk)
    raw4.wait_recv()
    place4(sis4, 1 - core, True)
    column_start(5)
    for load in loads[2:]:
        load.wait()
    tmp[...] = jnp.zeros_like(tmp)
    tmp[0:32, 0:192] = i3v[...].reshape(32, 192).astype(F32)
    tmp[32:128, 0:192] = lmv[...].astype(F32)
    tmp[128:256, 0:96] = i4v[...].reshape(128, 96).astype(F32)
    tmp[256:272, 0:96] = rov[...].astype(F32)
    first = pltpu.roll(tmp[0:128, 0:128], 64, 1).astype(BF16)
    second = pltpu.roll(tmp[0:128, 128:256], 64, 1).astype(BF16)
    tmp[0:32, 0:128] = pltpu.roll(tmp[0:32, 0:128], 64, 1)
    tmp[0:32, 128:256] = pltpu.roll(tmp[0:32, 128:256], 64, 1)
    s3i[0, 2:4, 16:32, :] = tmp[0:32, 0:256].reshape(2, 16, 256).astype(BF16)
    lm[0:96, 0:128] = first[32:128]
    lm[0:96, 128:256] = second[32:128]
    lm[96:128, :] = jnp.zeros((32, 256), BF16)
    third = pltpu.roll(tmp[128:272, 0:128], 96, 1)
    s4c[0, 4:8] = third[0:128].reshape(4, 32, 128).astype(BF16)
    for k in range(2):
        s4e[k] = third[0:128].reshape(4, 32, 128)[:, 24 * k : 24 * k + 8, :].reshape(32, 128).astype(BF16)
    ro[...] = third[128:144].astype(BF16)
    fine = lax.broadcasted_iota(jnp.int32, (384, 192), 0)
    cell = lax.broadcasted_iota(jnp.int32, (384, 192), 1)
    up[...] = jnp.where((fine // 64) * 32 + lax.rem(fine, 64) // 2 == cell, 1.0, 0.0).astype(BF16)

    def wide(halo, centre, rows):
        sides = [halo[k].astype(F32).reshape(rows, 8, centre.shape[-1]) for k in range(2)]
        return jnp.concatenate([sides[0], centre.astype(F32), sides[1]], 1)

    def away(dy, dx):
        oy = 1 - (h + NH - 1) // NH if dy < 0 else (h + 1) // NH if dy > 0 else 0
        ox = 1 - (w + NW - 1) // NW if dx < 0 else (w + 1) // NW if dx > 0 else 0
        return oy + ox - oy * ox

    def neighbour(dy, dx):
        where = {}
        if dy:
            where["ha"] = lax.rem(h + dy + NH, NH)
        if dx:
            where["wa"] = lax.rem(w + dx + NW, NW)
        return where

    def send_rows(ref, t, steps, rows, send, recv):
        for dy in (-1, 1):
            to = t + steps * away(dy, 0)
            remote(
                ref.at[t, rows : 2 * rows], ref.at[to, rows * (1 - dy) : rows * (2 - dy)], send, recv, **neighbour(dy, 0)
            ).start()

    def send_3(t):
        send_rows(s3w, t, 4, 2, n3_s.at[0], n3_r.at[t])

    def send_4(t):
        send_rows(s4w, t, 3, 4, n4_s.at[1], n4_r.at[t])

    view_3 = s3w.at[0, 0:4]
    view_4 = s4w.at[0, 0:8]
    view_a = xa.at[0:3]
    view_s3 = s3i.at[0:2, 0:4, 0:32]
    view_x0 = xi.at[0:2, 0:4, 0:32]
    view_x = xc.at[0:2, 0:3, 0:5]
    view_s4 = s4c.at[0:2, 0:7]

    def send_whole(src, dst, send, recv):
        for dy, dx in NEIGHBOURS:
            remote(
                src, dst.at[away(dy, dx), 2 - 2 * dy : 4 - 2 * dy, 16 - 16 * dx : 32 - 16 * dx], send, recv,
                **neighbour(dy, dx),
            ).start()

    def send_borders():
        send_whole(s3i.at[0, 2:4, 16:32], s3i, n3_s.at[1], n3_r.at[4])
        wait_bytes(view_a, xa_r)
        xi[0, 2:4, 16:32, :] = xa[0]
        send_whole(xa.at[0], xi, x0_s, x0_r)
        for lead in range(1, LEADS):
            xc[0, lead - 1, 2:4] = xa[lead]
            tile = xa[lead].astype(F32)
            for k in range(2):
                xe[lead - 1, k] = tile[:, 8 * k : 8 * k + 8, :].reshape(16, 192).astype(BF16)
        for dy, dx in NEIGHBOURS:
            to = away(dy, dx)
            if dx == 0:
                one = xa.at[1:4], xc.at[to, :, 2 - 2 * dy : 4 - 2 * dy]
                two = s4c.at[0, 4:8], s4c.at[to, 4 - 4 * dy : 8 - 4 * dy]
            else:
                one = xe.at[:, (dx + 1) // 2], xh.at[to, (1 - dx) // 2, 1 - dy]
                two = s4e.at[(dx + 1) // 2], s4h.at[to, (1 - dx) // 2, 1 - dy]
            remote(*one, xn_s, xn_r, **neighbour(dy, dx)).start()
            remote(*two, n4_s.at[0], n4_r.at[0], **neighbour(dy, dx)).start()

    def wait_borders():
        wait_bytes(view_s3, n3_r.at[4])
        wait_bytes(view_x0, x0_r)
        wait_bytes(view_x, xn_r)
        wait_bytes(view_s4, n4_r.at[0])
        s4w[0] = wide(s4h.at[0], s4c[0], 12).astype(BF16)
        pw[...] = s3i[0].astype(F32)
        xw[0] = xi[0].astype(F32)
        for lead in range(1, LEADS):
            xw[lead, :, 8:40, :] = wide(xh.at[0, :, :, lead - 1], xc[0, lead - 1], 6)

    def window3(i, slot):
        if slot > 1:
            return s13[i, slot]
        a, b = s1e[slot, 2 * i], s1e[slot, 2 * i + 1]
        return jnp.concatenate([a[0:32], a[32:48] + b[0:16], b[16:48]], 0)

    def merged3(slot):
        out = []
        for g in (0, 2):
            a, b = window3(g, slot), window3(g + 1, slot)
            out += [a[0:64], a[64:80] + b[0:16], b[16:80]]
        return jnp.concatenate(out, 0)

    def merged4(slot):
        a, b, c, d = (s14[i, slot] for i in range(4))
        return jnp.concatenate(
            [a[0:32], a[32:48] + b[0:16], b[16:32], b[32:48] + c[0:16], c[16:32], c[32:48] + d[0:16], d[16:48]], 0
        )

    def hops(chunk):
        level, slot, n = CHUNKS[chunk]
        if slot == 0:
            return (Z_HOPS, Z_RELAY) if level == 3 else (ZD_HOPS, {})
        if slot <= (X3 if level == 3 else X4):
            return (XR_HOPS, XR_RELAY) if chunk in RELAYED else (X_HOPS, X_RELAY)
        return [], {}

    def piece(chunk, owner, part):
        level, slot, n = CHUNKS[chunk]
        wb, rows, cut = (wb3, H3R, 144) if level == 3 else (wb4, H4R, 80)
        lo, hi = ((0, rows), (0, cut), (cut, rows))[part]
        return wb.at[core, pl.ds(first_block(chunk, owner, owner), n), lo:hi]

    def along(chunk):
        if chunk in Z_CHUNKS:
            return w, NW, "wa", z_r.at[Z_CHUNKS.index(chunk)]
        return s, NS, "section", x_r.at[X_CHUNKS.index(chunk)]

    def hop(chunk, k):
        d, step, part = hops(chunk)[0][k]
        me, size, axis, recv = along(chunk)
        view = piece(chunk, lax.rem(me + step - d + 2 * size, size), part)
        to = lax.rem(me + step + size, size)
        return remote(view, view, plane_s.at[CHUNKS[chunk][0] - 3], recv.at[k], **{axis: to})

    def received(chunk, k):
        d, step, part = hops(chunk)[0][k]
        me, size, axis, recv = along(chunk)
        return piece(chunk, lax.rem(me - d + size, size), part), recv.at[k]

    def share(chunk, view):
        remote(view, view, f_s.at[CHUNKS[chunk][0] - 3], f_r.at[chunk], ha=sister).start()

    def shared_view(chunk):
        level, slot, n = CHUNKS[chunk]
        owners = 8 if slot == 0 else NS if slot <= (X3 if level == 3 else X4) else 1
        return (wb3 if level == 3 else wb4).at[0, 0 : owners * n]

    def plane_start(chunk):
        level, slot, n = CHUNKS[chunk]
        column_wait(chunk)
        wb, merged = (wb3, merged3) if level == 3 else (wb4, merged4)
        first = first_block(chunk, w, s)
        for k in range(n):
            wb[pl.ds(core, 1), pl.ds(first + k, 1)] = merged(slot + k)[None, None]
        relayed = [k for ks in hops(chunk)[1].values() for k in ks]
        for k in range(len(hops(chunk)[0])):
            if k not in relayed:
                hop(chunk, k).start()
        share(chunk, piece(chunk, w if slot == 0 else s, 0))

    def plane_pass(chunk, *ks):
        for k in ks:
            view, sem = received(chunk, k)
            wait_bytes(view, sem)
            for j in hops(chunk)[1].get(k, ()):
                hop(chunk, j).start()
            share(chunk, view)

    send_borders()
    column_start(6)
    plane_start(0)
    plane_start(1)
    plane_start(2)
    column_start(7)
    column_start(8)
    plane_pass(0, 0, 1)
    plane_pass(1, 0, 1)
    plane_start(3)
    plane_pass(0, 2, 3)
    plane_start(4)
    plane_pass(2, 0, 1)
    plane_pass(1, 2, 3)
    plane_pass(0, 4, 5, 6, 7)
    plane_start(5)
    plane_pass(2, 2, 3)
    plane_pass(3, 0, 1, 2)
    wait_borders()

    def blocks3(a, kinds):
        return [9 * kind + 3 * a + b for b in range(3) for kind in kinds]

    def gates3(a, kinds):
        blocks = []
        for kb in blocks3(a, kinds):
            lo, hi = wb3.at[0, kb], wb3.at[1, kb]
            blocks.append(jnp.concatenate([
                lo[64:128, :], lo[0:64, :], lo[128:192, :], lo[128:192, :],
                lo[256:288, :], hi[0:32, :], lo[192:256, :], hi[32:96, :], hi[32:96, :],
            ], 0))
        return jnp.concatenate(blocks, 1)

    def cand3(a, kinds):
        zero = jnp.zeros((64, 128), BF16)
        blocks = []
        for kb in blocks3(a, kinds):
            hi = wb3.at[1, kb]
            blocks.append(jnp.concatenate([hi[160:224, :], hi[96:160, :], zero, hi[224:288, :]], 0))
        return jnp.concatenate(blocks, 1)

    def gates4(a):
        blocks = []
        for kb in range(6 * a, 6 * a + 6):
            lo, hi = wb4.at[0, kb], wb4.at[1, kb]
            blocks.append(jnp.concatenate([
                lo[32:96, :], lo[0:32, :], lo[0:32, :],
                lo[128:144, :], hi[0:48, :], lo[96:128, :], lo[96:128, :],
            ], 0))
        return jnp.concatenate(blocks, 1)

    def cand4(a):
        zero = jnp.zeros((32, 128), BF16)
        blocks = []
        for kb in range(6 * a, 6 * a + 6):
            hi = wb4.at[1, kb]
            blocks.append(jnp.concatenate([hi[80:144, :], zero, hi[48:80, :]], 0))
        return jnp.concatenate(blocks, 1)

    def conv(ref, r0, rows, c0, cols, weights):
        u = jnp.concatenate(
            [ref[r0 - 1 : r0 + rows + 1, c0 + b - 1 : c0 + b - 1 + cols, :].astype(BF16) for b in range(3)], 2
        )
        return sum(nt(u[a : a + rows].reshape(rows * cols, u.shape[2]), weights(a)) for a in range(3))

    def input_sums(t):
        jx[...] = xw[t, :, :, 0:128]
        xg[t] = conv(jx, 1, 4, 8, 32, lambda a: gates3(a, (0,)))
        xk[t] = conv(jx, 2, 2, 8, 32, lambda a: cand3(a, (0,)))

    def level3(t):
        p = pw[...]
        j3[:, :, 0:128] = p[:, :, 0:128]
        j3[:, :, 128:192] = xw[t, :, :, 128:192]
        j3[:, :, 192:256] = p[:, :, 192:256]
        p = p[:, 8:40, :]
        sums = xg[t] + conv(j3, 1, 4, 8, 32, lambda a: gates3(a, (1, 2)))
        reset = jax.nn.sigmoid(sums[:, :256]).reshape(4, 32, 256)
        update = jax.nn.sigmoid(sums[:, 256:]).reshape(4, 32, 256)[1:3]
        gated = reset * p[1:5]
        j3[1:5, 8:40, 0:128] = gated[:, :, 0:128]
        j3[1:5, 8:40, 192:256] = gated[:, :, 192:256]
        fresh = xk[t] + conv(j3, 2, 2, 8, 32, lambda a: cand3(a, (1, 2)))
        fresh = jnp.maximum(fresh, 0.0).reshape(2, 32, 256)
        state = update * p[2:4] + (1.0 - update) * fresh
        col = lax.broadcasted_iota(jnp.int32, state.shape, 1) + (16 * w - 8)
        s3w[t, 2:4] = jnp.where((col >= 0) & (col < 16 * NW), state, 0.0).astype(BF16)
        send_3(t)

    def to_lead(t):
        return remote(pt.at[t], po.at[s], out_s, out_r, section=t)

    def lift(t):
        lifted = nt(s3w[t].reshape(192, 256), lm[...]).astype(BF16)
        lifted = jnp.dot(up[...], lifted, preferred_element_type=F32).reshape(6, 64, 128)
        for i in range(12):
            j4[i, :, 0:96] = lifted[i // 2, :, 0:96]

    def level4(t, border=0, last=False):
        g0, g1 = 3 - border, 9 + border
        p = p4[...] if last else s4w[t].astype(F32)
        j4[:, 8:56, 96:128] = p[:, :, 96:128]
        j4[:, 8:56, 128:192] = p[:, :, 0:64]
        sums = conv(j4, g0, g1 - g0, 8, 48, gates4)
        reset = jax.nn.sigmoid(sums[:, :128]).reshape(g1 - g0, 48, 128)
        update = jax.nn.sigmoid(sums[:, 128:]).reshape(g1 - g0, 48, 128)
        gated = reset * p[g0:g1]
        j4[g0:g1, 8:56, 96:128] = gated[:, :, 96:128]
        j4[g0:g1, 8:56, 128:192] = gated[:, :, 0:64]
        c0, cols = (16, 32) if last else (8, 48)
        rows = g1 - g0 - 2
        fresh = conv(j4, g0 + 1, rows, c0, cols, cand4)
        fresh = jnp.maximum(fresh, 0.0).reshape(rows, cols, 128)
        update, prior = update[1 : rows + 1, c0 - 8 : c0 - 8 + cols], p[g0 + 1 : g1 - 1, c0 - 8 : c0 - 8 + cols]
        state = update * prior + (1.0 - update) * fresh
        if not last:
            row = lax.broadcasted_iota(jnp.int32, state.shape, 0) + (4 * h + g0 + 1 - 4)
            col = lax.broadcasted_iota(jnp.int32, state.shape, 1) + (32 * w - 8)
            inside = (row >= 0) & (row < 4 * NH) & (col >= 0) & (col < 32 * NW)
            state = jnp.where(inside, state, 0.0).astype(BF16)
            if border:
                p4[g0 + 1 : g1 - 1] = state.astype(F32)
            else:
                s4w[t + 1, 4:8] = state
                send_4(t + 1)
            state = state.astype(F32)[border : border + 4, 8:40]
        pt[t] = nt(ro[...], state.astype(BF16).reshape(128, 128))

        @pl.when(s == t)
        def _():
            po[t] = pt[t]

        @pl.when(s != t)
        def _():
            to_lead(t).start()

    for chunk in (0, 1):
        wait_bytes(shared_view(chunk), f_r.at[chunk])
    input_sums(0)
    plane_pass(4, 0, 1, 2)
    plane_start(6)
    plane_start(7)
    for chunk in CH3[2:]:
        wait_bytes(shared_view(chunk), f_r.at[chunk])

    @pl.loop(0, LEADS)
    def _(t):
        @pl.when(t > 0)
        def _():
            wait_bytes(view_3, n3_r.at[t - 1])
            pw[:, 8:40, :] = s3w[t - 1].astype(F32)

        level3(t)

        @pl.when(t == 0)
        def _():
            plane_start(8)
            pl.loop(1, LEADS)(input_sums)
            plane_pass(5, 0, 1, 2, 3, 4, 5, 6)
            plane_pass(7, 0, 1, 2)

        @pl.when(t > 0)
        def _():
            lift(t - 1)

        @pl.when(t == 1)
        def _():
            for chunk in CH4:
                wait_bytes(shared_view(chunk), f_r.at[chunk])

        @pl.when(t > 1)
        def _():
            wait_bytes(view_4, n4_r.at[t - 1])

        @pl.when((t > 0) & (t < LEADS - 1))
        def _():
            level4(t - 1)

        @pl.when(t == LEADS - 1)
        def _():
            level4(t - 1, border=2)

    wait_bytes(view_3, n3_r.at[LEADS - 1])
    lift(LEADS - 1)
    level4(LEADS - 1, last=True)

    wait_bytes(po.at[0:3], out_r)
    o_ref[...] = po[...]

    raw3.wait_send()
    raw4.wait_send()
    wait_bytes(view_a, xa_s)
    wait_bytes(view_s3, n3_s.at[1])
    wait_bytes(view_x0, x0_s)
    wait_bytes(view_x, xn_s)
    wait_bytes(view_s4, n4_s.at[0])
    wait_bytes(s3w.at[0:4, 0:4], n3_s.at[0])
    wait_bytes(s4w.at[0:2, 0:8], n4_s.at[1])
    @pl.when(half == core)
    def _():
        wait_bytes(s1e.at[:, 0:7], col_s.at[2])

    @pl.when(half != core)
    def _():
        wait_bytes(s1e, col_s.at[2])

    for k, (wb, s1, per) in enumerate(((wb3, s13.at[:, 2:], X3), (wb4, s14, X4))):
        wait_bytes(wb.at[0, 0 : 7 + 3 * per], plane_s.at[k])
        wait_bytes(wb.at[0], f_s.at[k])
        @pl.when(alone)
        def _(s1=s1, k=k):
            wait_bytes(s1.at[0:3], col_s.at[k])
        @pl.when(jnp.logical_not(alone))
        def _(s1=s1, k=k):
            wait_bytes(s1, col_s.at[k])
    wait_bytes(pt.at[0:3], out_s)


def local(coarse_inputs, init_level3, init_level4, weight_level3, weight_level4, lift_map, readout):
    n = len(CHUNKS)
    dma = pltpu.SemaphoreType.DMA
    fields = pl.pallas_call(
        kernel,
        out_shape=jax.ShapeDtypeStruct((4, 16, 128), F32),
        in_specs=[pl.BlockSpec(memory_space=pl.ANY)] * 7,
        out_specs=pl.BlockSpec(memory_space=pltpu.VMEM),
        scratch_shapes=[
            pltpu.VMEM((2, 16, 192), BF16),
            pltpu.VMEM((4, 32, 96), BF16),
            pltpu.VMEM((96, 192), BF16),
            pltpu.VMEM((16, 96), BF16),
            pltpu.VMEM((9, 36, 384), BF16),
            pltpu.VMEM((9, 18, 192), BF16),
            pltpu.VMEM((9, 36, 384), BF16),
            pltpu.VMEM((9, 18, 192), BF16),
            pltpu.VMEM((K3, WIN3, 128), BF16),
            pltpu.VMEM((K4, WIN4, 128), BF16),
            pltpu.VMEM((2, 48, 128), BF16),
            pltpu.VMEM((2, 8, 48, 128), BF16),
            pltpu.VMEM((4, 1 + X3 + C3, WIN3, 128), BF16),
            pltpu.VMEM((4, 1 + X4 + C4, WIN4, 128), BF16),
            pltpu.VMEM((2, K3, H3R, 128), BF16),
            pltpu.VMEM((2, K4, H4R, 128), BF16),
            pltpu.VMEM((4, 2, 16, 192), BF16),
            pltpu.VMEM((2, 6, 48, 192), BF16),
            pltpu.VMEM((2, 3, 6, 16, 192), BF16),
            pltpu.VMEM((3, 2, 16, 192), BF16),
            pltpu.VMEM((2, 2, 3, 3, 16, 192), BF16),
            pltpu.VMEM((2, 6, 48, 256), BF16),
            pltpu.VMEM((8, 6, 32, 256), BF16),
            pltpu.VMEM((2, 12, 32, 128), BF16),
            pltpu.VMEM((2, 32, 128), BF16),
            pltpu.VMEM((2, 2, 3, 32, 128), BF16),
            pltpu.VMEM((6, 12, 48, 128), BF16),
            pltpu.VMEM((4, 6, 48, 192), F32),
            pltpu.VMEM((6, 48, 256), F32),
            pltpu.VMEM((6, 48, 128), F32),
            pltpu.VMEM((6, 48, 256), F32),
            pltpu.VMEM((12, 64, 256), F32),
            pltpu.VMEM((12, 48, 128), F32),
            pltpu.VMEM((4, 128, 512), F32),
            pltpu.VMEM((4, 64, 256), F32),
            pltpu.VMEM((272, 256), F32),
            pltpu.VMEM((128, 256), BF16),
            pltpu.VMEM((16, 128), BF16),
            pltpu.VMEM((384, 192), BF16),
            pltpu.VMEM((4, 16, 128), F32),
            pltpu.VMEM((4, 16, 128), F32),
            dma((7,)), dma((2,)), dma((2,)), dma((3,)), dma((n,)),
            dma((2,)), dma((len(X_CHUNKS), NS)), dma((len(Z_CHUNKS), NW)), dma((2,)), dma((n,)),
            dma, dma, dma, dma, dma, dma, dma((2,)), dma((5,)), dma((2,)), dma((3,)), dma, dma,
        ],
        compiler_params=pltpu.CompilerParams(
            collective_id=0, has_side_effects=True, vmem_limit_bytes=64 << 20
        ),
        name="nowcast",
    )(
        coarse_inputs[0].transpose(0, 2, 3, 1),
        init_level3.transpose(1, 2, 0),
        init_level4.transpose(1, 2, 0),
        weight_level3.transpose(1, 0, 2),
        weight_level4.transpose(1, 0, 2),
        lift_map,
        readout,
    )
    return fields.reshape(1, 4, 16, 4, 32)


def solution(mesh):
    return jax.shard_map(
        local,
        mesh=mesh,
        in_specs=(
            P("section", None, None, "ha", "wa"),
            P(None, "ha", "wa"),
            P(None, "ha", "wa"),
            P("ha", None, None),
            P("ha", None, None),
            P(),
            P(),
        ),
        out_specs=P("section", None, None, "ha", "wa"),
        check_vma=False,
    )
```

```python
import jax
import jax.numpy as jnp
from jax import lax
from jax.experimental import pallas as pl
from jax.experimental.pallas import tpu as pltpu
from jax.sharding import PartitionSpec as P

MESH = pl.DeviceIdType.MESH
BF16 = jnp.bfloat16
F32 = jnp.float32

NS, NH, NW = 4, 16, 8
LEADS = 4

X3, X4 = 4, 2
C3, C4 = 3, 2
K3, K4 = 8 + NS * X3 + C3, 8 + NS * X4 + C4
H3R, H4R = 288, 144
WIN3, WIN4 = 80, 48

CHUNKS = [(3, 0, 1), (3, 1, 1), (3, 2, 1), (3, 3, 1), (3, 4, 1), (4, 0, 1), (3, 5, 3), (4, 1, 2), (4, 3, 2)]
CH3, CH4 = (0, 1, 2, 3, 4, 6), (5, 7, 8)

NEIGHBOURS = [(-1, -1), (-1, 1), (1, -1), (1, 1), (0, -1), (0, 1), (-1, 0), (1, 0)]

Z_HOPS = [(1, 1, 0), (7, -1, 0), (2, 2, 0), (6, -2, 0), (3, 1, 0), (5, -1, 0), (4, 2, 1), (4, -2, 2)]
Z_RELAY = {2: (4, 6), 3: (5, 7)}
ZD_HOPS = [(1, 1, 0), (7, -1, 0), (2, 2, 0), (6, -2, 0), (3, 3, 0), (5, -3, 0), (4, 4, 0)]
X_HOPS = [(1, 1, 0), (3, -1, 0), (2, 2, 0)]
X_RELAY = {}
XR_HOPS = [(1, 1, 0), (3, -1, 0), (2, 1, 1), (2, -1, 2)]
XR_RELAY = {0: (2,), 1: (3,)}
RELAYED = (1, 2)
Z_CHUNKS = [k for k, (level, slot, n) in enumerate(CHUNKS) if slot == 0]
X_CHUNKS = [k for k, (level, slot, n) in enumerate(CHUNKS) if 0 < slot <= (X3 if level == 3 else X4)]


def nt(a, b):
    return lax.dot_general(a, b, (((1,), (1,)), ((), ())), preferred_element_type=F32)


def kernel(
    x_ref, i3_ref, i4_ref, w3_ref, w4_ref, lm_ref, ro_ref, o_ref,
    i3v, i4v, lmv, rov, own3, own4, sis3, sis4, cw3, cw4, early, s1e, s13, s14, wb3, wb4,
    xa, xi, xc, xe, xh, s3i, s3w, s4c, s4e, s4h, s4w, xw, pw, jx, j3, j4, p4, xg, xk, tmp, lm, ro, up, pt,
    load_sem, raw_s, raw_r, col_s, col_r, plane_s, x_r, z_r, f_s, f_r,
    xa_s, xa_r, x0_s, x0_r, xn_s, xn_r, n3_s, n3_r, n4_s, n4_r, out_s, out_r,
):
    s = lax.axis_index("section")
    h = lax.axis_index("ha")
    w = lax.axis_index("wa")
    core = lax.rem(h, 2)
    y = h // 2
    sister = h + 1 - 2 * core
    half = y // 4

    def remote(src, dst, send, recv, **where):
        return pltpu.make_async_remote_copy(
            src_ref=src, dst_ref=dst, send_sem=send, recv_sem=recv, device_id=where, device_id_type=MESH
        )

    def wait_bytes(view, sem):
        pltpu.make_async_copy(view, view, sem).wait()

    for ref, n in ((xi, 1), (xc, 1), (xh, 1), (s3i, 1), (s4c, 1), (s4h, 1)):
        ref[0:n] = jnp.zeros((n,) + ref.shape[1:], BF16)
    for ref, n, rows in ((s3w, 4, 2), (s4w, 3, 4)):
        for first in (0, 2 * rows):
            ref[0:n, first : first + rows] = jnp.zeros((n, rows) + ref.shape[2:], BF16)
    loads = [
        pltpu.make_async_copy(src, dst, load_sem.at[k])
        for k, (src, dst) in enumerate([
            (w3_ref, own3), (w4_ref, own4), (x_ref.at[s], xa.at[s]),
            (i3_ref, i3v), (i4_ref, i4v), (lm_ref, lmv), (ro_ref, rov),
        ])
    ]
    for load in loads:
        load.start()

    def shifted(rows, count, offset):
        r = lax.broadcasted_iota(jnp.int32, (rows, count), 0)
        c = lax.broadcasted_iota(jnp.int32, (rows, count), 1)
        return jnp.where(r == c + offset, 1.0, 0.0).astype(BF16)

    low = lax.broadcasted_iota(jnp.int32, (1, 128), 1) < 64

    def place3(shard, which, add):
        put = shifted(WIN3, 36, 8 * lax.rem(y, 2) + 36 * which)
        for tap in range(9):
            rows = jnp.dot(put, shard[tap], preferred_element_type=F32)
            v1, v2 = rows[:, 128:256], rows[:, 256:384]
            for k, v in enumerate((rows[:, :128], jnp.where(low, v2, v1), jnp.where(low, v1, v2))):
                v = v.astype(BF16)
                cw3[9 * k + tap] = cw3[9 * k + tap] + v if add else v

    def place4(shard, which, add):
        put = shifted(WIN4, 18, 4 * lax.rem(y, 4) + 18 * which)
        for tap in range(9):
            rows = jnp.dot(put, shard[tap], preferred_element_type=F32)
            tmp[0:WIN4, 0:64] = rows[:, 128:192]
            tmp[0:WIN4, 64:128] = jnp.zeros((WIN4, 64), F32)
            for k, v in enumerate((rows[:, :128], tmp[0:WIN4, 0:128])):
                v = v.astype(BF16)
                cw4[2 * tap + k] = cw4[2 * tap + k] + v if add else v

    barrier = pltpu.get_barrier_semaphore()
    alone = (half == core) & (lax.rem(y, 2) == core)
    count = 0
    greet = [
        {"ha": lax.rem(h + dy, NH), "wa": lax.rem(w + dx, NW)} for dy in (1, NH - 1) for dx in (1, NW - 1)
    ]
    greet += [{"wa": lax.rem(w + d, NW)} for d in (4, 3, 5, 2, 6, 1, 7)]
    greet += [{"section": lax.rem(s + d, NS)} for d in (2, 1, 3)]
    greet += [{"ha": lax.rem(h + 2 * core + NH - 1, NH)}, {"ha": sister}]
    for where in greet:
        pl.semaphore_signal(barrier, inc=1, device_id=where, device_id_type=MESH)
    for i in range(8):
        source = 8 * core + i
        @pl.when(source != h)
        def _(source=source):
            pl.semaphore_signal(barrier, inc=1, device_id={"ha": source}, device_id_type=MESH)
    for ref in (j3, j4, xw):
        ref[...] = jnp.zeros_like(ref)
    loads[0].wait()
    place3(own3, core, False)
    for j, block in enumerate((w, 8 + X3 * s)):
        early[j] = cw3[block, pl.ds(pl.multiple_of(32 * core, 16), 48), :]
    loads[1].wait()
    place4(own4, core, False)
    pl.semaphore_wait(barrier, len(greet) + 8 - (half == core).astype(jnp.int32))

    raw3 = remote(w3_ref, sis3, raw_s.at[0], raw_r.at[0], ha=sister)
    raw4 = remote(w4_ref, sis4, raw_s.at[1], raw_r.at[1], ha=sister)
    raw3.start()
    raw4.start()

    for j in range(2):
        landing = s1e.at[j, lax.rem(h, 8)]
        for i in range(8):
            target = 2 * i + half
            @pl.when(target != h)
            def _(target=target, j=j, landing=landing):
                remote(early.at[j], landing, col_s.at[2], col_r.at[j], ha=target).start()
        @pl.when(half == core)
        def _(j=j, landing=landing):
            pltpu.make_async_copy(early.at[j], landing, col_r.at[j]).start()
    for d in range(1, NS):
        m = lax.rem(s + d, NS)
        remote(x_ref.at[m], xa.at[s], xa_s, xa_r, section=m).start()

    raw3.wait_recv()
    place3(sis3, 1 - core, True)

    def first_block(chunk, z, x):
        level, slot, n = CHUNKS[chunk]
        per = X3 if level == 3 else X4
        if slot == 0:
            return z
        return 8 + x * per + slot - 1 if slot <= per else 8 + (NS - 1) * per + slot - 1

    def column_parts(chunk):
        level, slot, n = CHUNKS[chunk]
        cw, s1 = (cw3, s13) if level == 3 else (cw4, s14)
        first = first_block(chunk, w, s)
        return cw.at[pl.ds(first, n)], s1.at[lax.rem(y, 4), slot : slot + n], s1.at[:, slot : slot + n]

    def column_start(chunk):
        src, dst, _ = column_parts(chunk)
        for i in range(4):
            target = 2 * (2 * i + core) + half
            @pl.when(target != h)
            def _(target=target):
                remote(src, dst, col_s.at[CHUNKS[chunk][0] - 3], col_r.at[chunk], ha=target).start()
        @pl.when(alone)
        def _():
            pltpu.make_async_copy(src, dst, col_r.at[chunk]).start()

    def column_wait(chunk):
        if chunk < 2:
            wait_bytes(s1e.at[chunk], col_r.at[chunk])
            return
        wait_bytes(column_parts(chunk)[2], col_r.at[chunk])

    for chunk in range(2, 5):
        column_start(chunk)
    raw4.wait_recv()
    place4(sis4, 1 - core, True)
    column_start(5)
    for load in loads[2:]:
        load.wait()
    tmp[...] = jnp.zeros_like(tmp)
    tmp[0:32, 0:192] = i3v[...].reshape(32, 192).astype(F32)
    tmp[32:128, 0:192] = lmv[...].astype(F32)
    tmp[128:256, 0:96] = i4v[...].reshape(128, 96).astype(F32)
    tmp[256:272, 0:96] = rov[...].astype(F32)
    first = pltpu.roll(tmp[0:128, 0:128], 64, 1).astype(BF16)
    second = pltpu.roll(tmp[0:128, 128:256], 64, 1).astype(BF16)
    tmp[0:32, 0:128] = pltpu.roll(tmp[0:32, 0:128], 64, 1)
    tmp[0:32, 128:256] = pltpu.roll(tmp[0:32, 128:256], 64, 1)
    s3i[0, 2:4, 16:32, :] = tmp[0:32, 0:256].reshape(2, 16, 256).astype(BF16)
    lm[0:96, 0:128] = first[32:128]
    lm[0:96, 128:256] = second[32:128]
    lm[96:128, :] = jnp.zeros((32, 256), BF16)
    third = pltpu.roll(tmp[128:272, 0:128], 96, 1)
    s4c[0, 4:8] = third[0:128].reshape(4, 32, 128).astype(BF16)
    for k in range(2):
        s4e[k] = third[0:128].reshape(4, 32, 128)[:, 24 * k : 24 * k + 8, :].reshape(32, 128).astype(BF16)
    ro[...] = third[128:144].astype(BF16)
    fine = lax.broadcasted_iota(jnp.int32, (384, 192), 0)
    cell = lax.broadcasted_iota(jnp.int32, (384, 192), 1)
    up[...] = jnp.where((fine // 64) * 32 + lax.rem(fine, 64) // 2 == cell, 1.0, 0.0).astype(BF16)

    def wide(halo, centre, rows):
        sides = [halo[k].astype(F32).reshape(rows, 8, centre.shape[-1]) for k in range(2)]
        return jnp.concatenate([sides[0], centre.astype(F32), sides[1]], 1)

    def away(dy, dx):
        oy = 1 - (h + NH - 1) // NH if dy < 0 else (h + 1) // NH if dy > 0 else 0
        ox = 1 - (w + NW - 1) // NW if dx < 0 else (w + 1) // NW if dx > 0 else 0
        return oy + ox - oy * ox

    def neighbour(dy, dx):
        where = {}
        if dy:
            where["ha"] = lax.rem(h + dy + NH, NH)
        if dx:
            where["wa"] = lax.rem(w + dx + NW, NW)
        return where

    def send_rows(ref, t, steps, rows, send, recv):
        for dy in (-1, 1):
            to = t + steps * away(dy, 0)
            remote(
                ref.at[t, rows : 2 * rows], ref.at[to, rows * (1 - dy) : rows * (2 - dy)], send, recv, **neighbour(dy, 0)
            ).start()

    def send_3(t):
        send_rows(s3w, t, 4, 2, n3_s.at[0], n3_r.at[t])

    def send_4(t):
        send_rows(s4w, t, 3, 4, n4_s.at[1], n4_r.at[t])

    view_3 = s3w.at[0, 0:4]
    view_4 = s4w.at[0, 0:8]
    view_a = xa.at[0:3]
    view_s3 = s3i.at[0:2, 0:4, 0:32]
    view_x0 = xi.at[0:2, 0:4, 0:32]
    view_x = xc.at[0:2, 0:3, 0:5]
    view_s4 = s4c.at[0:2, 0:7]

    def send_whole(src, dst, send, recv):
        for dy, dx in NEIGHBOURS:
            remote(
                src, dst.at[away(dy, dx), 2 - 2 * dy : 4 - 2 * dy, 16 - 16 * dx : 32 - 16 * dx], send, recv,
                **neighbour(dy, dx),
            ).start()

    def send_borders():
        send_whole(s3i.at[0, 2:4, 16:32], s3i, n3_s.at[1], n3_r.at[4])
        wait_bytes(view_a, xa_r)
        xi[0, 2:4, 16:32, :] = xa[0]
        send_whole(xa.at[0], xi, x0_s, x0_r)
        for lead in range(1, LEADS):
            xc[0, lead - 1, 2:4] = xa[lead]
            tile = xa[lead].astype(F32)
            for k in range(2):
                xe[lead - 1, k] = tile[:, 8 * k : 8 * k + 8, :].reshape(16, 192).astype(BF16)
        for dy, dx in NEIGHBOURS:
            to = away(dy, dx)
            if dx == 0:
                one = xa.at[1:4], xc.at[to, :, 2 - 2 * dy : 4 - 2 * dy]
                two = s4c.at[0, 4:8], s4c.at[to, 4 - 4 * dy : 8 - 4 * dy]
            else:
                one = xe.at[:, (dx + 1) // 2], xh.at[to, (1 - dx) // 2, 1 - dy]
                two = s4e.at[(dx + 1) // 2], s4h.at[to, (1 - dx) // 2, 1 - dy]
            remote(*one, xn_s, xn_r, **neighbour(dy, dx)).start()
            remote(*two, n4_s.at[0], n4_r.at[0], **neighbour(dy, dx)).start()

    def wait_borders():
        wait_bytes(view_s3, n3_r.at[4])
        wait_bytes(view_x0, x0_r)
        wait_bytes(view_x, xn_r)
        wait_bytes(view_s4, n4_r.at[0])
        s4w[0] = wide(s4h.at[0], s4c[0], 12).astype(BF16)
        pw[...] = s3i[0].astype(F32)
        xw[0] = xi[0].astype(F32)
        for lead in range(1, LEADS):
            xw[lead, :, 8:40, :] = wide(xh.at[0, :, :, lead - 1], xc[0, lead - 1], 6)

    def window3(i, slot):
        if slot > 1:
            return s13[i, slot]
        a, b = s1e[slot, 2 * i], s1e[slot, 2 * i + 1]
        return jnp.concatenate([a[0:32], a[32:48] + b[0:16], b[16:48]], 0)

    def merged3(slot):
        out = []
        for g in (0, 2):
            a, b = window3(g, slot), window3(g + 1, slot)
            out += [a[0:64], a[64:80] + b[0:16], b[16:80]]
        return jnp.concatenate(out, 0)

    def merged4(slot):
        a, b, c, d = (s14[i, slot] for i in range(4))
        return jnp.concatenate(
            [a[0:32], a[32:48] + b[0:16], b[16:32], b[32:48] + c[0:16], c[16:32], c[32:48] + d[0:16], d[16:48]], 0
        )

    def hops(chunk):
        level, slot, n = CHUNKS[chunk]
        if slot == 0:
            return (Z_HOPS, Z_RELAY) if level == 3 else (ZD_HOPS, {})
        if slot <= (X3 if level == 3 else X4):
            return (XR_HOPS, XR_RELAY) if chunk in RELAYED else (X_HOPS, X_RELAY)
        return [], {}

    def piece(chunk, owner, part):
        level, slot, n = CHUNKS[chunk]
        wb, rows, cut = (wb3, H3R, 144) if level == 3 else (wb4, H4R, 80)
        lo, hi = ((0, rows), (0, cut), (cut, rows))[part]
        return wb.at[core, pl.ds(first_block(chunk, owner, owner), n), lo:hi]

    def along(chunk):
        if chunk in Z_CHUNKS:
            return w, NW, "wa", z_r.at[Z_CHUNKS.index(chunk)]
        return s, NS, "section", x_r.at[X_CHUNKS.index(chunk)]

    def hop(chunk, k):
        d, step, part = hops(chunk)[0][k]
        me, size, axis, recv = along(chunk)
        view = piece(chunk, lax.rem(me + step - d + 2 * size, size), part)
        to = lax.rem(me + step + size, size)
        return remote(view, view, plane_s.at[CHUNKS[chunk][0] - 3], recv.at[k], **{axis: to})

    def received(chunk, k):
        d, step, part = hops(chunk)[0][k]
        me, size, axis, recv = along(chunk)
        return piece(chunk, lax.rem(me - d + size, size), part), recv.at[k]

    def share(chunk, view):
        remote(view, view, f_s.at[CHUNKS[chunk][0] - 3], f_r.at[chunk], ha=sister).start()

    def shared_view(chunk):
        level, slot, n = CHUNKS[chunk]
        owners = 8 if slot == 0 else NS if slot <= (X3 if level == 3 else X4) else 1
        return (wb3 if level == 3 else wb4).at[0, 0 : owners * n]

    def plane_start(chunk):
        level, slot, n = CHUNKS[chunk]
        column_wait(chunk)
        wb, merged = (wb3, merged3) if level == 3 else (wb4, merged4)
        first = first_block(chunk, w, s)
        for k in range(n):
            wb[pl.ds(core, 1), pl.ds(first + k, 1)] = merged(slot + k)[None, None]
        relayed = [k for ks in hops(chunk)[1].values() for k in ks]
        for k in range(len(hops(chunk)[0])):
            if k not in relayed:
                hop(chunk, k).start()
        share(chunk, piece(chunk, w if slot == 0 else s, 0))

    def plane_pass(chunk, *ks):
        for k in ks:
            view, sem = received(chunk, k)
            wait_bytes(view, sem)
            for j in hops(chunk)[1].get(k, ()):
                hop(chunk, j).start()
            share(chunk, view)

    send_borders()
    column_start(6)
    plane_start(0)
    plane_start(1)
    plane_start(2)
    column_start(7)
    column_start(8)
    plane_pass(0, 0, 1)
    plane_pass(1, 0, 1)
    plane_start(3)
    plane_pass(0, 2, 3)
    plane_start(4)
    plane_pass(2, 0, 1)
    plane_pass(1, 2, 3)
    plane_pass(0, 4, 5, 6, 7)
    plane_start(5)
    plane_pass(2, 2, 3)
    plane_pass(3, 0, 1, 2)
    wait_borders()

    def blocks3(a, kinds):
        return [9 * kind + 3 * a + b for b in range(3) for kind in kinds]

    def gates3(a, kinds):
        blocks = []
        for kb in blocks3(a, kinds):
            lo, hi = wb3.at[0, kb], wb3.at[1, kb]
            blocks.append(jnp.concatenate([
                lo[64:128, :], lo[0:64, :], lo[128:192, :], lo[128:192, :],
                lo[256:288, :], hi[0:32, :], lo[192:256, :], hi[32:96, :], hi[32:96, :],
            ], 0))
        return jnp.concatenate(blocks, 1)

    def cand3(a, kinds):
        zero = jnp.zeros((64, 128), BF16)
        blocks = []
        for kb in blocks3(a, kinds):
            hi = wb3.at[1, kb]
            blocks.append(jnp.concatenate([hi[160:224, :], hi[96:160, :], zero, hi[224:288, :]], 0))
        return jnp.concatenate(blocks, 1)

    def gates4(a):
        blocks = []
        for kb in range(6 * a, 6 * a + 6):
            lo, hi = wb4.at[0, kb], wb4.at[1, kb]
            blocks.append(jnp.concatenate([
                lo[32:96, :], lo[0:32, :], lo[0:32, :],
                lo[128:144, :], hi[0:48, :], lo[96:128, :], lo[96:128, :],
            ], 0))
        return jnp.concatenate(blocks, 1)

    def cand4(a):
        zero = jnp.zeros((32, 128), BF16)
        blocks = []
        for kb in range(6 * a, 6 * a + 6):
            hi = wb4.at[1, kb]
            blocks.append(jnp.concatenate([hi[80:144, :], zero, hi[48:80, :]], 0))
        return jnp.concatenate(blocks, 1)

    def conv(ref, r0, rows, c0, cols, weights):
        u = jnp.concatenate(
            [ref[r0 - 1 : r0 + rows + 1, c0 + b - 1 : c0 + b - 1 + cols, :].astype(BF16) for b in range(3)], 2
        )
        return sum(nt(u[a : a + rows].reshape(rows * cols, u.shape[2]), weights(a)) for a in range(3))

    def input_sums(t):
        jx[...] = xw[t, :, :, 0:128]
        xg[t] = conv(jx, 1, 4, 8, 32, lambda a: gates3(a, (0,)))
        xk[t] = conv(jx, 2, 2, 8, 32, lambda a: cand3(a, (0,)))

    def level3(t):
        p = pw[...]
        j3[:, :, 0:128] = p[:, :, 0:128]
        j3[:, :, 128:192] = xw[t, :, :, 128:192]
        j3[:, :, 192:256] = p[:, :, 192:256]
        p = p[:, 8:40, :]
        sums = xg[t] + conv(j3, 1, 4, 8, 32, lambda a: gates3(a, (1, 2)))
        reset = jax.nn.sigmoid(sums[:, :256]).reshape(4, 32, 256)
        update = jax.nn.sigmoid(sums[:, 256:]).reshape(4, 32, 256)[1:3]
        gated = reset * p[1:5]
        j3[1:5, 8:40, 0:128] = gated[:, :, 0:128]
        j3[1:5, 8:40, 192:256] = gated[:, :, 192:256]
        fresh = xk[t] + conv(j3, 2, 2, 8, 32, lambda a: cand3(a, (1, 2)))
        fresh = jnp.maximum(fresh, 0.0).reshape(2, 32, 256)
        state = update * p[2:4] + (1.0 - update) * fresh
        col = lax.broadcasted_iota(jnp.int32, state.shape, 1) + (16 * w - 8)
        s3w[t, 2:4] = jnp.where((col >= 0) & (col < 16 * NW), state, 0.0).astype(BF16)
        send_3(t)

    def to_lead(t):
        return remote(pt.at[t], o_ref.at[s], out_s, out_r, section=t)

    def lift(t):
        lifted = nt(s3w[t].reshape(192, 256), lm[...]).astype(BF16)
        lifted = jnp.dot(up[...], lifted, preferred_element_type=F32).reshape(6, 64, 128)
        for i in range(12):
            j4[i, :, 0:96] = lifted[i // 2, :, 0:96]

    def level4(t, border=0, last=False):
        g0, g1 = 3 - border, 9 + border
        p = p4[...] if last else s4w[t].astype(F32)
        j4[:, 8:56, 96:128] = p[:, :, 96:128]
        j4[:, 8:56, 128:192] = p[:, :, 0:64]
        sums = conv(j4, g0, g1 - g0, 8, 48, gates4)
        reset = jax.nn.sigmoid(sums[:, :128]).reshape(g1 - g0, 48, 128)
        update = jax.nn.sigmoid(sums[:, 128:]).reshape(g1 - g0, 48, 128)
        gated = reset * p[g0:g1]
        j4[g0:g1, 8:56, 96:128] = gated[:, :, 96:128]
        j4[g0:g1, 8:56, 128:192] = gated[:, :, 0:64]
        c0, cols = (16, 32) if last else (8, 48)
        rows = g1 - g0 - 2
        fresh = conv(j4, g0 + 1, rows, c0, cols, cand4)
        fresh = jnp.maximum(fresh, 0.0).reshape(rows, cols, 128)
        update, prior = update[1 : rows + 1, c0 - 8 : c0 - 8 + cols], p[g0 + 1 : g1 - 1, c0 - 8 : c0 - 8 + cols]
        state = update * prior + (1.0 - update) * fresh
        if not last:
            row = lax.broadcasted_iota(jnp.int32, state.shape, 0) + (4 * h + g0 + 1 - 4)
            col = lax.broadcasted_iota(jnp.int32, state.shape, 1) + (32 * w - 8)
            inside = (row >= 0) & (row < 4 * NH) & (col >= 0) & (col < 32 * NW)
            state = jnp.where(inside, state, 0.0).astype(BF16)
            if border:
                p4[g0 + 1 : g1 - 1] = state.astype(F32)
            else:
                s4w[t + 1, 4:8] = state
                send_4(t + 1)
            state = state.astype(F32)[border : border + 4, 8:40]
        pt[t] = nt(ro[...], state.astype(BF16).reshape(128, 128))

        @pl.when(s == t)
        def _():
            pltpu.make_async_copy(pt.at[t], o_ref.at[s], out_r).start()

        @pl.when(s != t)
        def _():
            to_lead(t).start()

    for chunk in (0, 1):
        wait_bytes(shared_view(chunk), f_r.at[chunk])
    input_sums(0)
    plane_pass(4, 0, 1, 2)
    plane_start(6)
    plane_start(7)
    for chunk in CH3[2:]:
        wait_bytes(shared_view(chunk), f_r.at[chunk])

    @pl.loop(0, LEADS)
    def _(t):
        @pl.when(t > 0)
        def _():
            wait_bytes(view_3, n3_r.at[t - 1])
            pw[:, 8:40, :] = s3w[t - 1].astype(F32)

        level3(t)

        @pl.when(t == 0)
        def _():
            plane_start(8)
            pl.loop(1, LEADS)(input_sums)
            plane_pass(5, 0, 1, 2, 3, 4, 5, 6)
            plane_pass(7, 0, 1, 2)

        @pl.when(t > 0)
        def _():
            lift(t - 1)

        @pl.when(t == 1)
        def _():
            for chunk in CH4:
                wait_bytes(shared_view(chunk), f_r.at[chunk])

        @pl.when(t > 1)
        def _():
            wait_bytes(view_4, n4_r.at[t - 1])

        @pl.when((t > 0) & (t < LEADS - 1))
        def _():
            level4(t - 1)

        @pl.when(t == LEADS - 1)
        def _():
            level4(t - 1, border=2)

    wait_bytes(view_3, n3_r.at[LEADS - 1])
    lift(LEADS - 1)
    level4(LEADS - 1, last=True)

    wait_bytes(o_ref, out_r)

    raw3.wait_send()
    raw4.wait_send()
    wait_bytes(view_a, xa_s)
    wait_bytes(view_s3, n3_s.at[1])
    wait_bytes(view_x0, x0_s)
    wait_bytes(view_x, xn_s)
    wait_bytes(view_s4, n4_s.at[0])
    wait_bytes(s3w.at[0:4, 0:4], n3_s.at[0])
    wait_bytes(s4w.at[0:2, 0:8], n4_s.at[1])
    @pl.when(half == core)
    def _():
        wait_bytes(s1e.at[:, 0:7], col_s.at[2])

    @pl.when(half != core)
    def _():
        wait_bytes(s1e, col_s.at[2])

    for k, (wb, s1, per) in enumerate(((wb3, s13.at[:, 2:], X3), (wb4, s14, X4))):
        wait_bytes(wb.at[0, 0 : 7 + 3 * per], plane_s.at[k])
        wait_bytes(wb.at[0], f_s.at[k])
        @pl.when(alone)
        def _(s1=s1, k=k):
            wait_bytes(s1.at[0:3], col_s.at[k])
        @pl.when(jnp.logical_not(alone))
        def _(s1=s1, k=k):
            wait_bytes(s1, col_s.at[k])
    wait_bytes(pt.at[0:3], out_s)


def local(coarse_inputs, init_level3, init_level4, weight_level3, weight_level4, lift_map, readout):
    n = len(CHUNKS)
    dma = pltpu.SemaphoreType.DMA
    fields = pl.pallas_call(
        kernel,
        out_shape=jax.ShapeDtypeStruct((4, 16, 128), F32),
        in_specs=[pl.BlockSpec(memory_space=pl.ANY)] * 7,
        out_specs=pl.BlockSpec(memory_space=pl.ANY),
        scratch_shapes=[
            pltpu.VMEM((2, 16, 192), BF16),
            pltpu.VMEM((4, 32, 96), BF16),
            pltpu.VMEM((96, 192), BF16),
            pltpu.VMEM((16, 96), BF16),
            pltpu.VMEM((9, 36, 384), BF16),
            pltpu.VMEM((9, 18, 192), BF16),
            pltpu.VMEM((9, 36, 384), BF16),
            pltpu.VMEM((9, 18, 192), BF16),
            pltpu.VMEM((K3, WIN3, 128), BF16),
            pltpu.VMEM((K4, WIN4, 128), BF16),
            pltpu.VMEM((2, 48, 128), BF16),
            pltpu.VMEM((2, 8, 48, 128), BF16),
            pltpu.VMEM((4, 1 + X3 + C3, WIN3, 128), BF16),
            pltpu.VMEM((4, 1 + X4 + C4, WIN4, 128), BF16),
            pltpu.VMEM((2, K3, H3R, 128), BF16),
            pltpu.VMEM((2, K4, H4R, 128), BF16),
            pltpu.VMEM((4, 2, 16, 192), BF16),
            pltpu.VMEM((2, 6, 48, 192), BF16),
            pltpu.VMEM((2, 3, 6, 16, 192), BF16),
            pltpu.VMEM((3, 2, 16, 192), BF16),
            pltpu.VMEM((2, 2, 3, 3, 16, 192), BF16),
            pltpu.VMEM((2, 6, 48, 256), BF16),
            pltpu.VMEM((8, 6, 32, 256), BF16),
            pltpu.VMEM((2, 12, 32, 128), BF16),
            pltpu.VMEM((2, 32, 128), BF16),
            pltpu.VMEM((2, 2, 3, 32, 128), BF16),
            pltpu.VMEM((6, 12, 48, 128), BF16),
            pltpu.VMEM((4, 6, 48, 192), F32),
            pltpu.VMEM((6, 48, 256), F32),
            pltpu.VMEM((6, 48, 128), F32),
            pltpu.VMEM((6, 48, 256), F32),
            pltpu.VMEM((12, 64, 256), F32),
            pltpu.VMEM((12, 48, 128), F32),
            pltpu.VMEM((4, 128, 512), F32),
            pltpu.VMEM((4, 64, 256), F32),
            pltpu.VMEM((272, 256), F32),
            pltpu.VMEM((128, 256), BF16),
            pltpu.VMEM((16, 128), BF16),
            pltpu.VMEM((384, 192), BF16),
            pltpu.VMEM((4, 16, 128), F32),
            dma((7,)), dma((2,)), dma((2,)), dma((3,)), dma((n,)),
            dma((2,)), dma((len(X_CHUNKS), NS)), dma((len(Z_CHUNKS), NW)), dma((2,)), dma((n,)),
            dma, dma, dma, dma, dma, dma, dma((2,)), dma((5,)), dma((2,)), dma((3,)), dma, dma,
        ],
        compiler_params=pltpu.CompilerParams(
            collective_id=0, has_side_effects=True, vmem_limit_bytes=64 << 20
        ),
        name="nowcast",
    )(
        coarse_inputs[0].transpose(0, 2, 3, 1),
        init_level3.transpose(1, 2, 0),
        init_level4.transpose(1, 2, 0),
        weight_level3.transpose(1, 0, 2),
        weight_level4.transpose(1, 0, 2),
        lift_map,
        readout,
    )
    return fields.reshape(1, 4, 16, 4, 32)


def solution(mesh):
    return jax.shard_map(
        local,
        mesh=mesh,
        in_specs=(
            P("section", None, None, "ha", "wa"),
            P(None, "ha", "wa"),
            P(None, "ha", "wa"),
            P("ha", None, None),
            P("ha", None, None),
            P(),
            P(),
        ),
        out_specs=P("section", None, None, "ha", "wa"),
        check_vma=False,
    )
```

```python
import jax
import jax.numpy as jnp
from jax import lax
from jax.experimental import pallas as pl
from jax.experimental.pallas import tpu as pltpu
from jax.sharding import PartitionSpec as P

MESH = pl.DeviceIdType.MESH
BF16 = jnp.bfloat16
F32 = jnp.float32

NS, NH, NW = 4, 16, 8
LEADS = 4

X3, X4 = 4, 2
C3, C4 = 3, 2
K3, K4 = 8 + NS * X3 + C3, 8 + NS * X4 + C4
H3R, H4R = 288, 144
WIN3, WIN4 = 80, 48

CHUNKS = [(3, 0, 1), (3, 1, 1), (3, 2, 1), (3, 3, 1), (3, 4, 1), (4, 0, 1), (3, 5, 3), (4, 1, 2), (4, 3, 2)]
CH3, CH4 = (0, 1, 2, 3, 4, 6), (5, 7, 8)

NEIGHBOURS = [(-1, -1), (-1, 1), (1, -1), (1, 1), (0, -1), (0, 1), (-1, 0), (1, 0)]

Z_HOPS = [(1, 1, 0), (7, -1, 0), (2, 2, 0), (6, -2, 0), (3, 1, 0), (5, -1, 0), (4, 2, 1), (4, -2, 2)]
Z_RELAY = {2: (4, 6), 3: (5, 7)}
ZD_HOPS = [(1, 1, 0), (7, -1, 0), (2, 2, 0), (6, -2, 0), (3, 3, 0), (5, -3, 0), (4, 4, 0)]
X_HOPS = [(1, 1, 0), (3, -1, 0), (2, 2, 0)]
X_RELAY = {}
XR_HOPS = [(1, 1, 0), (3, -1, 0), (2, 1, 1), (2, -1, 2)]
XR_RELAY = {0: (2,), 1: (3,)}
RELAYED = (1,)
Z_CHUNKS = [k for k, (level, slot, n) in enumerate(CHUNKS) if slot == 0]
X_CHUNKS = [k for k, (level, slot, n) in enumerate(CHUNKS) if 0 < slot <= (X3 if level == 3 else X4)]


def nt(a, b):
    return lax.dot_general(a, b, (((1,), (1,)), ((), ())), preferred_element_type=F32)


def kernel(
    x_ref, i3_ref, i4_ref, w3_ref, w4_ref, lm_ref, ro_ref, o_ref,
    i3v, i4v, lmv, rov, own3, own4, sis3, sis4, cw3, cw4, early, s1e, s13, s14, wb3, wb4,
    xa, xi, xc, xe, xh, s3i, s3w, s4c, s4e, s4h, s4w, xw, pw, jx, j3, j4, p4, xg, xk, tmp, lm, ro, up, pt,
    load_sem, raw_s, raw_r, col_s, col_r, plane_s, x_r, z_r, f_s, f_r,
    xa_s, xa_r, x0_s, x0_r, xn_s, xn_r, n3_s, n3_r, n4_s, n4_r, out_s, out_r,
):
    s = lax.axis_index("section")
    h = lax.axis_index("ha")
    w = lax.axis_index("wa")
    core = lax.rem(h, 2)
    y = h // 2
    sister = h + 1 - 2 * core
    half = y // 4

    def remote(src, dst, send, recv, **where):
        return pltpu.make_async_remote_copy(
            src_ref=src, dst_ref=dst, send_sem=send, recv_sem=recv, device_id=where, device_id_type=MESH
        )

    def wait_bytes(view, sem):
        pltpu.make_async_copy(view, view, sem).wait()

    for ref, n in ((xi, 1), (xc, 1), (xh, 1), (s3i, 1), (s4c, 1), (s4h, 1)):
        ref[0:n] = jnp.zeros((n,) + ref.shape[1:], BF16)
    for ref, n, rows in ((s3w, 4, 2), (s4w, 3, 4)):
        for first in (0, 2 * rows):
            ref[0:n, first : first + rows] = jnp.zeros((n, rows) + ref.shape[2:], BF16)
    loads = [
        pltpu.make_async_copy(src, dst, load_sem.at[k])
        for k, (src, dst) in enumerate([
            (w3_ref, own3), (w4_ref, own4), (x_ref.at[s], xa.at[s]),
            (i3_ref, i3v), (i4_ref, i4v), (lm_ref, lmv), (ro_ref, rov),
        ])
    ]
    for load in loads:
        load.start()

    def shifted(rows, count, offset):
        r = lax.broadcasted_iota(jnp.int32, (rows, count), 0)
        c = lax.broadcasted_iota(jnp.int32, (rows, count), 1)
        return jnp.where(r == c + offset, 1.0, 0.0).astype(BF16)

    low = lax.broadcasted_iota(jnp.int32, (1, 128), 1) < 64

    def place3(shard, which, add):
        put = shifted(WIN3, 36, 8 * lax.rem(y, 2) + 36 * which)
        for tap in range(9):
            rows = jnp.dot(put, shard[tap], preferred_element_type=F32)
            v1, v2 = rows[:, 128:256], rows[:, 256:384]
            for k, v in enumerate((rows[:, :128], jnp.where(low, v2, v1), jnp.where(low, v1, v2))):
                v = v.astype(BF16)
                cw3[9 * k + tap] = cw3[9 * k + tap] + v if add else v

    def place4(shard, which, add):
        put = shifted(WIN4, 18, 4 * lax.rem(y, 4) + 18 * which)
        for tap in range(9):
            rows = jnp.dot(put, shard[tap], preferred_element_type=F32)
            tmp[0:WIN4, 0:64] = rows[:, 128:192]
            tmp[0:WIN4, 64:128] = jnp.zeros((WIN4, 64), F32)
            for k, v in enumerate((rows[:, :128], tmp[0:WIN4, 0:128])):
                v = v.astype(BF16)
                cw4[2 * tap + k] = cw4[2 * tap + k] + v if add else v

    barrier = pltpu.get_barrier_semaphore()
    alone = (half == core) & (lax.rem(y, 2) == core)
    count = 0
    greet = [
        {"ha": lax.rem(h + dy, NH), "wa": lax.rem(w + dx, NW)} for dy in (1, NH - 1) for dx in (1, NW - 1)
    ]
    greet += [{"wa": lax.rem(w + d, NW)} for d in (4, 3, 5, 2, 6, 1, 7)]
    greet += [{"section": lax.rem(s + d, NS)} for d in (2, 1, 3)]
    greet += [{"ha": lax.rem(h + 2 * core + NH - 1, NH)}, {"ha": sister}]
    for where in greet:
        pl.semaphore_signal(barrier, inc=1, device_id=where, device_id_type=MESH)
    for i in range(8):
        source = 8 * core + i
        @pl.when(source != h)
        def _(source=source):
            pl.semaphore_signal(barrier, inc=1, device_id={"ha": source}, device_id_type=MESH)
    for ref in (j3, j4, xw):
        ref[...] = jnp.zeros_like(ref)
    loads[0].wait()
    place3(own3, core, False)
    for j, block in enumerate((w, 8 + X3 * s)):
        early[j] = cw3[block, pl.ds(pl.multiple_of(32 * core, 16), 48), :]
    loads[1].wait()
    place4(own4, core, False)
    pl.semaphore_wait(barrier, len(greet) + 8 - (half == core).astype(jnp.int32))

    raw3 = remote(w3_ref, sis3, raw_s.at[0], raw_r.at[0], ha=sister)
    raw4 = remote(w4_ref, sis4, raw_s.at[1], raw_r.at[1], ha=sister)
    raw3.start()
    raw4.start()

    for j in range(2):
        landing = s1e.at[j, lax.rem(h, 8)]
        for i in range(8):
            target = 2 * i + half
            @pl.when(target != h)
            def _(target=target, j=j, landing=landing):
                remote(early.at[j], landing, col_s.at[2], col_r.at[j], ha=target).start()
        @pl.when(half == core)
        def _(j=j, landing=landing):
            pltpu.make_async_copy(early.at[j], landing, col_r.at[j]).start()
    for d in range(1, NS):
        m = lax.rem(s + d, NS)
        remote(x_ref.at[m], xa.at[s], xa_s, xa_r, section=m).start()

    raw3.wait_recv()
    place3(sis3, 1 - core, True)

    def first_block(chunk, z, x):
        level, slot, n = CHUNKS[chunk]
        per = X3 if level == 3 else X4
        if slot == 0:
            return z
        return 8 + x * per + slot - 1 if slot <= per else 8 + (NS - 1) * per + slot - 1

    def column_parts(chunk):
        level, slot, n = CHUNKS[chunk]
        cw, s1 = (cw3, s13) if level == 3 else (cw4, s14)
        first = first_block(chunk, w, s)
        return cw.at[pl.ds(first, n)], s1.at[lax.rem(y, 4), slot : slot + n], s1.at[:, slot : slot + n]

    def column_start(chunk):
        src, dst, _ = column_parts(chunk)
        for i in range(4):
            target = 2 * (2 * i + core) + half
            @pl.when(target != h)
            def _(target=target):
                remote(src, dst, col_s.at[CHUNKS[chunk][0] - 3], col_r.at[chunk], ha=target).start()
        @pl.when(alone)
        def _():
            pltpu.make_async_copy(src, dst, col_r.at[chunk]).start()

    def column_wait(chunk):
        if chunk < 2:
            wait_bytes(s1e.at[chunk], col_r.at[chunk])
            return
        wait_bytes(column_parts(chunk)[2], col_r.at[chunk])

    for chunk in range(2, 5):
        column_start(chunk)
    raw4.wait_recv()
    place4(sis4, 1 - core, True)
    column_start(5)
    for load in loads[2:]:
        load.wait()
    tmp[...] = jnp.zeros_like(tmp)
    tmp[0:32, 0:192] = i3v[...].reshape(32, 192).astype(F32)
    tmp[32:128, 0:192] = lmv[...].astype(F32)
    tmp[128:256, 0:96] = i4v[...].reshape(128, 96).astype(F32)
    tmp[256:272, 0:96] = rov[...].astype(F32)
    first = pltpu.roll(tmp[0:128, 0:128], 64, 1).astype(BF16)
    second = pltpu.roll(tmp[0:128, 128:256], 64, 1).astype(BF16)
    tmp[0:32, 0:128] = pltpu.roll(tmp[0:32, 0:128], 64, 1)
    tmp[0:32, 128:256] = pltpu.roll(tmp[0:32, 128:256], 64, 1)
    s3i[0, 2:4, 16:32, :] = tmp[0:32, 0:256].reshape(2, 16, 256).astype(BF16)
    lm[0:96, 0:128] = first[32:128]
    lm[0:96, 128:256] = second[32:128]
    lm[96:128, :] = jnp.zeros((32, 256), BF16)
    third = pltpu.roll(tmp[128:272, 0:128], 96, 1)
    s4c[0, 4:8] = third[0:128].reshape(4, 32, 128).astype(BF16)
    for k in range(2):
        s4e[k] = third[0:128].reshape(4, 32, 128)[:, 24 * k : 24 * k + 8, :].reshape(32, 128).astype(BF16)
    ro[...] = third[128:144].astype(BF16)
    fine = lax.broadcasted_iota(jnp.int32, (384, 192), 0)
    cell = lax.broadcasted_iota(jnp.int32, (384, 192), 1)
    up[...] = jnp.where((fine // 64) * 32 + lax.rem(fine, 64) // 2 == cell, 1.0, 0.0).astype(BF16)

    def wide(halo, centre, rows):
        sides = [halo[k].astype(F32).reshape(rows, 8, centre.shape[-1]) for k in range(2)]
        return jnp.concatenate([sides[0], centre.astype(F32), sides[1]], 1)

    def away(dy, dx):
        oy = 1 - (h + NH - 1) // NH if dy < 0 else (h + 1) // NH if dy > 0 else 0
        ox = 1 - (w + NW - 1) // NW if dx < 0 else (w + 1) // NW if dx > 0 else 0
        return oy + ox - oy * ox

    def neighbour(dy, dx):
        where = {}
        if dy:
            where["ha"] = lax.rem(h + dy + NH, NH)
        if dx:
            where["wa"] = lax.rem(w + dx + NW, NW)
        return where

    def send_rows(ref, t, steps, rows, send, recv):
        for dy in (-1, 1):
            to = t + steps * away(dy, 0)
            remote(
                ref.at[t, rows : 2 * rows], ref.at[to, rows * (1 - dy) : rows * (2 - dy)], send, recv, **neighbour(dy, 0)
            ).start()

    def send_3(t):
        send_rows(s3w, t, 4, 2, n3_s.at[0], n3_r.at[t])

    def send_4(t):
        send_rows(s4w, t, 3, 4, n4_s.at[1], n4_r.at[t])

    view_3 = s3w.at[0, 0:4]
    view_4 = s4w.at[0, 0:8]
    view_a = xa.at[0:3]
    view_s3 = s3i.at[0:2, 0:4, 0:32]
    view_x0 = xi.at[0:2, 0:4, 0:32]
    view_x = xc.at[0:2, 0:3, 0:5]
    view_s4 = s4c.at[0:2, 0:7]

    def send_whole(src, dst, send, recv):
        for dy, dx in NEIGHBOURS:
            remote(
                src, dst.at[away(dy, dx), 2 - 2 * dy : 4 - 2 * dy, 16 - 16 * dx : 32 - 16 * dx], send, recv,
                **neighbour(dy, dx),
            ).start()

    def send_borders():
        send_whole(s3i.at[0, 2:4, 16:32], s3i, n3_s.at[1], n3_r.at[4])
        wait_bytes(view_a, xa_r)
        xi[0, 2:4, 16:32, :] = xa[0]
        send_whole(xa.at[0], xi, x0_s, x0_r)
        for lead in range(1, LEADS):
            xc[0, lead - 1, 2:4] = xa[lead]
            tile = xa[lead].astype(F32)
            for k in range(2):
                xe[lead - 1, k] = tile[:, 8 * k : 8 * k + 8, :].reshape(16, 192).astype(BF16)
        for dy, dx in NEIGHBOURS:
            to = away(dy, dx)
            if dx == 0:
                one = xa.at[1:4], xc.at[to, :, 2 - 2 * dy : 4 - 2 * dy]
                two = s4c.at[0, 4:8], s4c.at[to, 4 - 4 * dy : 8 - 4 * dy]
            else:
                one = xe.at[:, (dx + 1) // 2], xh.at[to, (1 - dx) // 2, 1 - dy]
                two = s4e.at[(dx + 1) // 2], s4h.at[to, (1 - dx) // 2, 1 - dy]
            remote(*one, xn_s, xn_r, **neighbour(dy, dx)).start()
            remote(*two, n4_s.at[0], n4_r.at[0], **neighbour(dy, dx)).start()

    def wait_borders():
        wait_bytes(view_s3, n3_r.at[4])
        wait_bytes(view_x0, x0_r)
        wait_bytes(view_x, xn_r)
        wait_bytes(view_s4, n4_r.at[0])
        s4w[0] = wide(s4h.at[0], s4c[0], 12).astype(BF16)
        pw[...] = s3i[0].astype(F32)
        xw[0] = xi[0].astype(F32)
        for lead in range(1, LEADS):
            xw[lead, :, 8:40, :] = wide(xh.at[0, :, :, lead - 1], xc[0, lead - 1], 6)

    def window3(i, slot):
        if slot > 1:
            return s13[i, slot]
        a, b = s1e[slot, 2 * i], s1e[slot, 2 * i + 1]
        return jnp.concatenate([a[0:32], a[32:48] + b[0:16], b[16:48]], 0)

    def merged3(slot):
        out = []
        for g in (0, 2):
            a, b = window3(g, slot), window3(g + 1, slot)
            out += [a[0:64], a[64:80] + b[0:16], b[16:80]]
        return jnp.concatenate(out, 0)

    def merged4(slot):
        a, b, c, d = (s14[i, slot] for i in range(4))
        return jnp.concatenate(
            [a[0:32], a[32:48] + b[0:16], b[16:32], b[32:48] + c[0:16], c[16:32], c[32:48] + d[0:16], d[16:48]], 0
        )

    def hops(chunk):
        level, slot, n = CHUNKS[chunk]
        if slot == 0:
            return (Z_HOPS, Z_RELAY) if level == 3 else (ZD_HOPS, {})
        if slot <= (X3 if level == 3 else X4):
            return (XR_HOPS, XR_RELAY) if chunk in RELAYED else (X_HOPS, X_RELAY)
        return [], {}

    def piece(chunk, owner, part):
        level, slot, n = CHUNKS[chunk]
        wb, rows, cut = (wb3, H3R, 144) if level == 3 else (wb4, H4R, 80)
        lo, hi = ((0, rows), (0, cut), (cut, rows))[part]
        return wb.at[core, pl.ds(first_block(chunk, owner, owner), n), lo:hi]

    def along(chunk):
        if chunk in Z_CHUNKS:
            return w, NW, "wa", z_r.at[Z_CHUNKS.index(chunk)]
        return s, NS, "section", x_r.at[X_CHUNKS.index(chunk)]

    def hop(chunk, k):
        d, step, part = hops(chunk)[0][k]
        me, size, axis, recv = along(chunk)
        view = piece(chunk, lax.rem(me + step - d + 2 * size, size), part)
        to = lax.rem(me + step + size, size)
        return remote(view, view, plane_s.at[CHUNKS[chunk][0] - 3], recv.at[k], **{axis: to})

    def received(chunk, k):
        d, step, part = hops(chunk)[0][k]
        me, size, axis, recv = along(chunk)
        return piece(chunk, lax.rem(me - d + size, size), part), recv.at[k]

    def share(chunk, view):
        remote(view, view, f_s.at[CHUNKS[chunk][0] - 3], f_r.at[chunk], ha=sister).start()

    def shared_view(chunk):
        level, slot, n = CHUNKS[chunk]
        owners = 8 if slot == 0 else NS if slot <= (X3 if level == 3 else X4) else 1
        return (wb3 if level == 3 else wb4).at[0, 0 : owners * n]

    def plane_start(chunk):
        level, slot, n = CHUNKS[chunk]
        column_wait(chunk)
        wb, merged = (wb3, merged3) if level == 3 else (wb4, merged4)
        first = first_block(chunk, w, s)
        for k in range(n):
            wb[pl.ds(core, 1), pl.ds(first + k, 1)] = merged(slot + k)[None, None]
        relayed = [k for ks in hops(chunk)[1].values() for k in ks]
        for k in range(len(hops(chunk)[0])):
            if k not in relayed:
                hop(chunk, k).start()
        share(chunk, piece(chunk, w if slot == 0 else s, 0))

    def plane_pass(chunk, *ks):
        for k in ks:
            view, sem = received(chunk, k)
            wait_bytes(view, sem)
            for j in hops(chunk)[1].get(k, ()):
                hop(chunk, j).start()
            share(chunk, view)

    send_borders()
    column_start(6)
    plane_start(0)
    plane_start(1)
    plane_start(2)
    column_start(7)
    column_start(8)
    plane_pass(0, 0, 1)
    plane_pass(1, 0, 1)
    plane_start(3)
    plane_pass(0, 2, 3)
    plane_start(4)
    plane_pass(2, 0, 1)
    plane_pass(1, 2, 3)
    plane_pass(0, 4, 5, 6, 7)
    plane_start(5)
    plane_pass(2, 2)
    plane_pass(3, 0, 1, 2)
    wait_borders()

    def blocks3(a, kinds):
        return [9 * kind + 3 * a + b for b in range(3) for kind in kinds]

    def gates3(a, kinds):
        blocks = []
        for kb in blocks3(a, kinds):
            lo, hi = wb3.at[0, kb], wb3.at[1, kb]
            blocks.append(jnp.concatenate([
                lo[64:128, :], lo[0:64, :], lo[128:192, :], lo[128:192, :],
                lo[256:288, :], hi[0:32, :], lo[192:256, :], hi[32:96, :], hi[32:96, :],
            ], 0))
        return jnp.concatenate(blocks, 1)

    def cand3(a, kinds):
        zero = jnp.zeros((64, 128), BF16)
        blocks = []
        for kb in blocks3(a, kinds):
            hi = wb3.at[1, kb]
            blocks.append(jnp.concatenate([hi[160:224, :], hi[96:160, :], zero, hi[224:288, :]], 0))
        return jnp.concatenate(blocks, 1)

    def gates4(a):
        blocks = []
        for kb in range(6 * a, 6 * a + 6):
            lo, hi = wb4.at[0, kb], wb4.at[1, kb]
            blocks.append(jnp.concatenate([
                lo[32:96, :], lo[0:32, :], lo[0:32, :],
                lo[128:144, :], hi[0:48, :], lo[96:128, :], lo[96:128, :],
            ], 0))
        return jnp.concatenate(blocks, 1)

    def cand4(a):
        zero = jnp.zeros((32, 128), BF16)
        blocks = []
        for kb in range(6 * a, 6 * a + 6):
            hi = wb4.at[1, kb]
            blocks.append(jnp.concatenate([hi[80:144, :], zero, hi[48:80, :]], 0))
        return jnp.concatenate(blocks, 1)

    def conv(ref, r0, rows, c0, cols, weights):
        u = jnp.concatenate(
            [ref[r0 - 1 : r0 + rows + 1, c0 + b - 1 : c0 + b - 1 + cols, :].astype(BF16) for b in range(3)], 2
        )
        return sum(nt(u[a : a + rows].reshape(rows * cols, u.shape[2]), weights(a)) for a in range(3))

    def input_sums(t):
        jx[...] = xw[t, :, :, 0:128]
        xg[t] = conv(jx, 1, 4, 8, 32, lambda a: gates3(a, (0,)))
        xk[t] = conv(jx, 2, 2, 8, 32, lambda a: cand3(a, (0,)))

    def level3(t):
        p = pw[...]
        j3[:, :, 0:128] = p[:, :, 0:128]
        j3[:, :, 128:192] = xw[t, :, :, 128:192]
        j3[:, :, 192:256] = p[:, :, 192:256]
        p = p[:, 8:40, :]
        sums = xg[t] + conv(j3, 1, 4, 8, 32, lambda a: gates3(a, (1, 2)))
        reset = jax.nn.sigmoid(sums[:, :256]).reshape(4, 32, 256)
        update = jax.nn.sigmoid(sums[:, 256:]).reshape(4, 32, 256)[1:3]
        gated = reset * p[1:5]
        j3[1:5, 8:40, 0:128] = gated[:, :, 0:128]
        j3[1:5, 8:40, 192:256] = gated[:, :, 192:256]
        fresh = xk[t] + conv(j3, 2, 2, 8, 32, lambda a: cand3(a, (1, 2)))
        fresh = jnp.maximum(fresh, 0.0).reshape(2, 32, 256)
        state = update * p[2:4] + (1.0 - update) * fresh
        col = lax.broadcasted_iota(jnp.int32, state.shape, 1) + (16 * w - 8)
        s3w[t, 2:4] = jnp.where((col >= 0) & (col < 16 * NW), state, 0.0).astype(BF16)
        send_3(t)

    def to_lead(t):
        return remote(pt.at[t], o_ref.at[s], out_s, out_r, section=t)

    def lift(t):
        lifted = nt(s3w[t].reshape(192, 256), lm[...]).astype(BF16)
        lifted = jnp.dot(up[...], lifted, preferred_element_type=F32).reshape(6, 64, 128)
        for i in range(12):
            j4[i, :, 0:96] = lifted[i // 2, :, 0:96]

    def level4(t, border=0, last=False):
        g0, g1 = 3 - border, 9 + border
        p = p4[...] if last else s4w[t].astype(F32)
        j4[:, 8:56, 96:128] = p[:, :, 96:128]
        j4[:, 8:56, 128:192] = p[:, :, 0:64]
        sums = conv(j4, g0, g1 - g0, 8, 48, gates4)
        reset = jax.nn.sigmoid(sums[:, :128]).reshape(g1 - g0, 48, 128)
        update = jax.nn.sigmoid(sums[:, 128:]).reshape(g1 - g0, 48, 128)
        gated = reset * p[g0:g1]
        j4[g0:g1, 8:56, 96:128] = gated[:, :, 96:128]
        j4[g0:g1, 8:56, 128:192] = gated[:, :, 0:64]
        c0, cols = (16, 32) if last else (8, 48)
        rows = g1 - g0 - 2
        fresh = conv(j4, g0 + 1, rows, c0, cols, cand4)
        fresh = jnp.maximum(fresh, 0.0).reshape(rows, cols, 128)
        update, prior = update[1 : rows + 1, c0 - 8 : c0 - 8 + cols], p[g0 + 1 : g1 - 1, c0 - 8 : c0 - 8 + cols]
        state = update * prior + (1.0 - update) * fresh
        if not last:
            row = lax.broadcasted_iota(jnp.int32, state.shape, 0) + (4 * h + g0 + 1 - 4)
            col = lax.broadcasted_iota(jnp.int32, state.shape, 1) + (32 * w - 8)
            inside = (row >= 0) & (row < 4 * NH) & (col >= 0) & (col < 32 * NW)
            state = jnp.where(inside, state, 0.0).astype(BF16)
            if border:
                p4[g0 + 1 : g1 - 1] = state.astype(F32)
            else:
                s4w[t + 1, 4:8] = state
                send_4(t + 1)
            state = state.astype(F32)[border : border + 4, 8:40]
        pt[t] = nt(ro[...], state.astype(BF16).reshape(128, 128))

        @pl.when(s == t)
        def _():
            pltpu.make_async_copy(pt.at[t], o_ref.at[s], out_r).start()

        @pl.when(s != t)
        def _():
            to_lead(t).start()

    for chunk in (0, 1):
        wait_bytes(shared_view(chunk), f_r.at[chunk])
    input_sums(0)
    plane_pass(4, 0, 1, 2)
    plane_start(6)
    plane_start(7)
    for chunk in CH3[2:]:
        wait_bytes(shared_view(chunk), f_r.at[chunk])

    @pl.loop(0, LEADS)
    def _(t):
        @pl.when(t > 0)
        def _():
            wait_bytes(view_3, n3_r.at[t - 1])
            pw[:, 8:40, :] = s3w[t - 1].astype(F32)

        level3(t)

        @pl.when(t == 0)
        def _():
            plane_start(8)
            pl.loop(1, LEADS)(input_sums)
            plane_pass(5, 0, 1, 2, 3, 4, 5, 6)
            plane_pass(7, 0, 1, 2)

        @pl.when(t > 0)
        def _():
            lift(t - 1)

        @pl.when(t == 1)
        def _():
            for chunk in CH4:
                wait_bytes(shared_view(chunk), f_r.at[chunk])

        @pl.when(t > 1)
        def _():
            wait_bytes(view_4, n4_r.at[t - 1])

        @pl.when((t > 0) & (t < LEADS - 1))
        def _():
            level4(t - 1)

        @pl.when(t == LEADS - 1)
        def _():
            level4(t - 1, border=2)

    wait_bytes(view_3, n3_r.at[LEADS - 1])
    lift(LEADS - 1)
    level4(LEADS - 1, last=True)

    wait_bytes(o_ref, out_r)

    raw3.wait_send()
    raw4.wait_send()
    wait_bytes(view_a, xa_s)
    wait_bytes(view_s3, n3_s.at[1])
    wait_bytes(view_x0, x0_s)
    wait_bytes(view_x, xn_s)
    wait_bytes(view_s4, n4_s.at[0])
    wait_bytes(s3w.at[0:4, 0:4], n3_s.at[0])
    wait_bytes(s4w.at[0:2, 0:8], n4_s.at[1])
    @pl.when(half == core)
    def _():
        wait_bytes(s1e.at[:, 0:7], col_s.at[2])

    @pl.when(half != core)
    def _():
        wait_bytes(s1e, col_s.at[2])

    for k, (wb, s1, per) in enumerate(((wb3, s13.at[:, 2:], X3), (wb4, s14, X4))):
        wait_bytes(wb.at[0, 0 : 7 + 3 * per], plane_s.at[k])
        wait_bytes(wb.at[0], f_s.at[k])
        @pl.when(alone)
        def _(s1=s1, k=k):
            wait_bytes(s1.at[0:3], col_s.at[k])
        @pl.when(jnp.logical_not(alone))
        def _(s1=s1, k=k):
            wait_bytes(s1, col_s.at[k])
    wait_bytes(pt.at[0:3], out_s)


def local(coarse_inputs, init_level3, init_level4, weight_level3, weight_level4, lift_map, readout):
    n = len(CHUNKS)
    dma = pltpu.SemaphoreType.DMA
    fields = pl.pallas_call(
        kernel,
        out_shape=jax.ShapeDtypeStruct((4, 16, 128), F32),
        in_specs=[pl.BlockSpec(memory_space=pl.ANY)] * 7,
        out_specs=pl.BlockSpec(memory_space=pl.ANY),
        scratch_shapes=[
            pltpu.VMEM((2, 16, 192), BF16),
            pltpu.VMEM((4, 32, 96), BF16),
            pltpu.VMEM((96, 192), BF16),
            pltpu.VMEM((16, 96), BF16),
            pltpu.VMEM((9, 36, 384), BF16),
            pltpu.VMEM((9, 18, 192), BF16),
            pltpu.VMEM((9, 36, 384), BF16),
            pltpu.VMEM((9, 18, 192), BF16),
            pltpu.VMEM((K3, WIN3, 128), BF16),
            pltpu.VMEM((K4, WIN4, 128), BF16),
            pltpu.VMEM((2, 48, 128), BF16),
            pltpu.VMEM((2, 8, 48, 128), BF16),
            pltpu.VMEM((4, 1 + X3 + C3, WIN3, 128), BF16),
            pltpu.VMEM((4, 1 + X4 + C4, WIN4, 128), BF16),
            pltpu.VMEM((2, K3, H3R, 128), BF16),
            pltpu.VMEM((2, K4, H4R, 128), BF16),
            pltpu.VMEM((4, 2, 16, 192), BF16),
            pltpu.VMEM((2, 6, 48, 192), BF16),
            pltpu.VMEM((2, 3, 6, 16, 192), BF16),
            pltpu.VMEM((3, 2, 16, 192), BF16),
            pltpu.VMEM((2, 2, 3, 3, 16, 192), BF16),
            pltpu.VMEM((2, 6, 48, 256), BF16),
            pltpu.VMEM((8, 6, 32, 256), BF16),
            pltpu.VMEM((2, 12, 32, 128), BF16),
            pltpu.VMEM((2, 32, 128), BF16),
            pltpu.VMEM((2, 2, 3, 32, 128), BF16),
            pltpu.VMEM((6, 12, 48, 128), BF16),
            pltpu.VMEM((4, 6, 48, 192), F32),
            pltpu.VMEM((6, 48, 256), F32),
            pltpu.VMEM((6, 48, 128), F32),
            pltpu.VMEM((6, 48, 256), F32),
            pltpu.VMEM((12, 64, 256), F32),
            pltpu.VMEM((12, 48, 128), F32),
            pltpu.VMEM((4, 128, 512), F32),
            pltpu.VMEM((4, 64, 256), F32),
            pltpu.VMEM((272, 256), F32),
            pltpu.VMEM((128, 256), BF16),
            pltpu.VMEM((16, 128), BF16),
            pltpu.VMEM((384, 192), BF16),
            pltpu.VMEM((4, 16, 128), F32),
            dma((7,)), dma((2,)), dma((2,)), dma((3,)), dma((n,)),
            dma((2,)), dma((len(X_CHUNKS), NS)), dma((len(Z_CHUNKS), NW)), dma((2,)), dma((n,)),
            dma, dma, dma, dma, dma, dma, dma((2,)), dma((5,)), dma((2,)), dma((3,)), dma, dma,
        ],
        compiler_params=pltpu.CompilerParams(
            collective_id=0, has_side_effects=True, vmem_limit_bytes=64 << 20
        ),
        name="nowcast",
    )(
        coarse_inputs[0].transpose(0, 2, 3, 1),
        init_level3.transpose(1, 2, 0),
        init_level4.transpose(1, 2, 0),
        weight_level3.transpose(1, 0, 2),
        weight_level4.transpose(1, 0, 2),
        lift_map,
        readout,
    )
    return fields.reshape(1, 4, 16, 4, 32)


def solution(mesh):
    return jax.shard_map(
        local,
        mesh=mesh,
        in_specs=(
            P("section", None, None, "ha", "wa"),
            P(None, "ha", "wa"),
            P(None, "ha", "wa"),
            P("ha", None, None),
            P("ha", None, None),
            P(),
            P(),
        ),
        out_specs=P("section", None, None, "ha", "wa"),
        check_vma=False,
    )
```
